32 devices in a mesh: ctx: 8 (over z, y), head: 4 (over x, core).
Axes of the slice: x: 2, y: 2, z: 4, core: 2. Of those that a mesh axis runs over, the one named last changes fastest.
Arguments:
- tokens: bfloat16 [2, 2048, 2048], P(None, 'ctx'), may hold values from -6 to 6, as said below
- cotangent: bfloat16 [2, 2048, 2048], P(None, 'ctx'), may hold values from -6 to 6, as said below
- lengths: int32 [2, 2], replicated, may hold values from 1 to 31, as said below
- norm_in: bfloat16 [2048], P('ctx'), may hold values from 0.5 to 1.5
- w_query: bfloat16 [2048, 1024], P('ctx', 'head'), may hold values from -0.125 to 0.125
- w_key: bfloat16 [2048, 1024], P('ctx', 'head'), may hold values from -0.125 to 0.125
- w_value: bfloat16 [2048, 2048], P('ctx', 'head'), may hold values from -0.125 to 0.125
- w_outgate: bfloat16 [2048, 2048], P('ctx', 'head'), may hold values from -0.125 to 0.125
- w_rank: bfloat16 [2048, 16], P('ctx'), may hold values from -0.125 to 0.125
- w_decay: bfloat16 [4, 16, 256], P('head', None, 'ctx'), may hold values from -1.5 to 1.5
- decay_bias: bfloat16 [4, 256], P('head', 'ctx'), may hold values from -3 to 6
- head_gain: bfloat16 [512], P('ctx'), may hold values from 0.5 to 1.5
- w_out: bfloat16 [2048, 2048], P('head', 'ctx'), may hold values from -0.25 to 0.25
- norm_mid: bfloat16 [2048], P('ctx'), may hold values from 0.5 to 1.5
- w_gate: bfloat16 [2048, 5632], P('ctx', 'head'), may hold values from -0.125 to 0.125
- w_up: bfloat16 [2048, 5632], P('ctx', 'head'), may hold values from -0.125 to 0.125
- w_down: bfloat16 [5632, 2048], P('head', 'ctx'), may hold values from -0.15625 to 0.15625
Outputs:
- block_out: bfloat16 [2, 2048, 2048], P(None, 'ctx')
- input_grad: float32 [2, 2048, 2048], P(None, 'ctx')
- grad_norm_in: float32 [2048], P('ctx')
- grad_query: float32 [2048, 1024], P('ctx', 'head')
- grad_key: float32 [2048, 1024], P('ctx', 'head')
- grad_value: float32 [2048, 2048], P('ctx', 'head')
- grad_outgate: float32 [2048, 2048], P('ctx', 'head')
- grad_rank: float32 [2048, 16], P('ctx')
- grad_decay: float32 [4, 16, 256], P('head', None, 'ctx')
- grad_bias: float32 [4, 256], P('head', 'ctx')
- grad_head_gain: float32 [512], P('ctx')
- grad_out: float32 [2048, 2048], P('head', 'ctx')
- grad_norm_mid: float32 [2048], P('ctx')
- grad_gate: float32 [2048, 5632], P('ctx', 'head')
- grad_up: float32 [2048, 5632], P('ctx', 'head')
- grad_down: float32 [5632, 2048], P('head', 'ctx')
The draws below stay inside these ranges and needn't reach their ends.
Inputs may be any that keep to these rules, and one draw needn't show every extreme that they name: Each micro-batch packs its sequences in order from slot 0, each lengths * 64 slots long, all together at most 2048 slots; the slots after the last sequence are padding. In every micro-batch one sequence has slots on the first and on the last index of ctx. `tokens`: independent entries of mean 0 and deviation 1. `cotangent`: independent entries of mean 0 and deviation 1.
All inputs are finite; a program needn't handle non-finite values.
Results may differ from the reference program's by a relative error of at most 0.025.
Values may be sent and summed in bfloat16 or wider, within the bound.
No kernel may reach another device: no remote copies, remote signals or barrier semaphores. Data moves between devices by JAX's collectives and lax.ppermute only.
A program may use at most 192 MiB of HBM per device.

```python
import jax
import jax.numpy as jnp
from jax import lax

D = 2048
HEADS = 4
DK = 256
DV = 512
FF = 5632
RANK = 16
GROUP = 64
SLOT_DEV = 256
MB = 2
SLOTS = 2048


def draw_tokens(key, part):
    key = jax.random.fold_in(key, 23)
    field = jnp.clip(jax.random.normal(key, (MB, SLOTS, D), jnp.float32), -6.0, 6.0)
    return field.astype(jnp.bfloat16)


def draw_cotangent(key, part):
    key = jax.random.fold_in(key, 37)
    field = jnp.clip(jax.random.normal(key, (MB, SLOTS, D), jnp.float32), -6.0, 6.0)
    return field.astype(jnp.bfloat16)


def draw_lengths(key, part):
    base = jax.random.fold_in(key, 11)
    total_key, short_key, order_key, forced_key = jax.random.split(base, 4)
    blocks_all = SLOTS // GROUP
    blocks_dev = SLOT_DEV // GROUP
    batch_ids = jnp.arange(MB, dtype=jnp.int32)
    forced = jax.random.randint(forced_key, (), 0, MB).astype(jnp.int32)
    filled = jax.random.randint(total_key, (MB,), blocks_all - blocks_dev + 2, blocks_all + 1).astype(jnp.int32)
    filled = jnp.where(batch_ids == forced, blocks_all, filled).astype(jnp.int32)
    room = (filled - blocks_all + blocks_dev - 1).astype(jnp.int32)
    short = jax.random.randint(short_key, (MB,), 1, room + 1).astype(jnp.int32)
    short = jnp.where(batch_ids == forced, 1, short).astype(jnp.int32)
    longer = (filled - short).astype(jnp.int32)
    long_first = jax.random.randint(order_key, (MB,), 0, 2).astype(jnp.int32)
    first_col = jnp.where(long_first == 1, longer, short)
    second_col = jnp.where(long_first == 1, short, longer)
    return jnp.stack([first_col, second_col], axis=1).astype(jnp.int32)


def level_of(stream_key, dims, cuts, least, largest):
    factor_of = 1.0
    for dim, parts in cuts:
        steps = jax.random.uniform(jax.random.fold_in(jax.random.fold_in(stream_key, 6), dim), (parts,), jnp.float32, least / len(cuts), largest / len(cuts))
        factor_of = factor_of * jnp.repeat(jnp.exp(steps), dims[dim] // parts).reshape((-1,) + (1,) * (len(dims) - 1 - dim))
    return factor_of


def normal_values(rng, shape, spread, most, shards=(), kind=jnp.bfloat16):
    level = level_of(rng, shape, shards, -0.22, 0.18) if shards else 1.0
    array = jax.random.normal(rng, shape, jnp.float32) * spread * level
    return jnp.minimum(jnp.maximum(array, -most), most).astype(kind)


def setup_inputs(seed: int = 0) -> dict:
    key_of = jax.random.split(jax.random.key(seed), 18)
    return {
        "tokens": draw_tokens(jax.random.fold_in(key_of[17], 71), 0),
        "cotangent": draw_cotangent(jax.random.fold_in(key_of[17], 71), 0),
        "lengths": draw_lengths(jax.random.fold_in(key_of[17], 71), 0),
        "norm_in": jnp.clip(1.0 + 0.1 * jax.random.normal(key_of[3], (D,), jnp.float32), 0.5, 1.5).astype(jnp.bfloat16),
        "w_query": normal_values(key_of[4], (D, HEADS * DK), D ** -0.5, 0.125, ((0, 8), (1, 4))),
        "w_key": normal_values(key_of[5], (D, HEADS * DK), D ** -0.5, 0.125, ((0, 8), (1, 4))),
        "w_value": normal_values(key_of[6], (D, HEADS * DV), D ** -0.5, 0.125, ((0, 8), (1, 4))),
        "w_outgate": normal_values(key_of[7], (D, HEADS * DV), D ** -0.5, 0.125, ((0, 8), (1, 4))),
        "w_rank": normal_values(key_of[8], (D, RANK), D ** -0.5, 0.125, ((0, 8),)),
        "w_decay": normal_values(key_of[9], (HEADS, RANK, DK), RANK ** -0.5, 1.5, ((0, 4), (2, 8))),
        "decay_bias": jnp.clip(-3.0 + 9.0 * jax.random.uniform(key_of[10], (HEADS, DK), jnp.float32) ** level_of(key_of[10], (HEADS, DK), ((0, 4), (1, 8)), -0.2, 0.2), -3.0, 6.0).astype(jnp.bfloat16),
        "head_gain": jnp.clip(1.0 + 0.1 * jax.random.normal(key_of[11], (DV,), jnp.float32), 0.5, 1.5).astype(jnp.bfloat16),
        "w_out": normal_values(key_of[12], (HEADS * DV, D), DV ** -0.5, 0.25, ((0, 4), (1, 8))),
        "norm_mid": jnp.clip(1.0 + 0.1 * jax.random.normal(key_of[13], (D,), jnp.float32), 0.5, 1.5).astype(jnp.bfloat16),
        "w_gate": normal_values(key_of[14], (D, FF), D ** -0.5, 0.125, ((0, 8), (1, 4))),
        "w_up": normal_values(key_of[15], (D, FF), D ** -0.5, 0.125, ((0, 8), (1, 4))),
        "w_down": normal_values(key_of[16], (FF, D), (FF // 4) ** -0.5, 0.15625, ((0, 4), (1, 8))),
    }


EPS = 1e-06
HIGH = lax.Precision.HIGHEST

@jax.custom_vjp
def low(v):
    return lax.optimization_barrier(v.astype(jnp.bfloat16)).astype(jnp.float32)

@jax.custom_vjp
def low_back(v):
    return v

def low_keep(v):
    return (low(v), None)

def low_pass(kept, grad):
    return (grad,)

def back_keep(v):
    return (v, None)

def back_low(kept, grad):
    return (low(grad),)
low.defvjp(low_keep, low_pass)
low_back.defvjp(back_keep, back_low)

def matmul(left, right):
    return jnp.dot(left, right, precision=HIGH, preferred_element_type=jnp.float32)

def rms_norm(value, gain):
    return value * lax.rsqrt(lax.optimization_barrier(jnp.mean(value * value, axis=-1, keepdims=True)) + EPS) * gain

def group_step(carry_state, inputs):
    queries, key_rows, values, decays, resets = inputs
    score_scale = DK ** (-0.5)
    cumulative = jnp.cumsum(decays, axis=1)
    last_cum = cumulative[:, -1, :]
    prior_state = carry_state * (1.0 - resets)
    causal = (jnp.arange(GROUP)[:, None] >= jnp.arange(GROUP)[None, :]).astype(jnp.float32)
    inter_part = jnp.einsum('hcd,hde->hce', queries * jnp.exp(cumulative) * score_scale, prior_state, precision=HIGH)
    pair_decay = jnp.exp(cumulative[:, :, None, :] - cumulative[:, None, :, :])
    scores = jnp.einsum('htd,hsd,htsd->hts', queries, key_rows, pair_decay, precision=HIGH) * (score_scale * causal)
    intra_part = jnp.einsum('hts,hse->hte', scores, values, precision=HIGH)
    carried = key_rows * jnp.exp(last_cum[:, None, :] - cumulative)
    new_state = jnp.exp(last_cum)[:, :, None] * prior_state + jnp.einsum('hsd,hse->hde', carried, values, precision=HIGH)
    return (new_state, inter_part + intra_part)

def layout(lengths_row):
    ends = jnp.cumsum(lengths_row).astype(jnp.int32)
    starts = jnp.concatenate([jnp.zeros((1,), jnp.int32), ends]).astype(jnp.int32)
    group_ids = jnp.arange(SLOTS // GROUP, dtype=jnp.int32)
    resets = jnp.any(group_ids[:, None] == starts[None, :], axis=1).astype(jnp.float32)
    slot_group = jnp.arange(SLOTS, dtype=jnp.int32) // GROUP
    slot_mask = (slot_group < ends[-1]).astype(jnp.float32)
    return (resets, slot_mask)

def forward(inputs, weights, resets):
    norm_in, w_query, w_key, w_value, w_outgate, w_rank, w_decay, decay_bias, head_gain, w_out, norm_mid, w_gate, w_up, w_down = weights
    group_total = SLOTS // GROUP
    normed_in = low(rms_norm(inputs, norm_in))
    queries = low_back(low(matmul(normed_in, w_query)))
    key_rows = low_back(low(matmul(normed_in, w_key)))
    values = low_back(low(matmul(normed_in, w_value)))
    outgate = low_back(low(matmul(normed_in, w_outgate)))
    low_rank = low_back(low(matmul(normed_in, w_rank)))
    logits = low_back(jnp.einsum('tr,hrd->thd', low_rank, w_decay, precision=HIGH) + decay_bias[None])
    decays = jax.nn.log_sigmoid(logits) / 16.0

    def blocks(value, width):
        return value.reshape(group_total, GROUP, HEADS, width).transpose(0, 2, 1, 3)
    sequence_in = (blocks(queries, DK), blocks(key_rows, DK), blocks(values, DV), blocks(decays, DK), resets)
    start_state = jnp.zeros((HEADS, DK, DV), jnp.float32)
    _, mixed_out = lax.scan(jax.checkpoint(group_step), start_state, sequence_in)
    mixed_out = mixed_out.transpose(0, 2, 1, 3).reshape(SLOTS, HEADS, DV)
    gated_out = low(rms_norm(mixed_out, head_gain) * jax.nn.silu(outgate.reshape(SLOTS, HEADS, DV)))
    attention = low_back(matmul(gated_out.reshape(SLOTS, HEADS * DV), w_out))
    residual = inputs + attention
    normed_mid = low(rms_norm(residual, norm_mid))
    gate_proj = low_back(matmul(normed_mid, w_gate))
    up_proj = low_back(matmul(normed_mid, w_up))
    hidden = low(jax.nn.silu(gate_proj) * up_proj)
    return residual + low_back(matmul(hidden, w_down))

def reference(tokens, cotangent, lengths, norm_in, w_query, w_key, w_value, w_outgate, w_rank, w_decay, decay_bias, head_gain, w_out, norm_mid, w_gate, w_up, w_down):
    weights = tuple((weight.astype(jnp.float32) for weight in (norm_in, w_query, w_key, w_value, w_outgate, w_rank, w_decay, decay_bias, head_gain, w_out, norm_mid, w_gate, w_up, w_down)))
    outputs = []
    input_grads = []
    totals = tuple((jnp.zeros(weight.shape, jnp.float32) for weight in weights))
    for batch_index in range(MB):
        resets, slot_mask = layout(lengths[batch_index])
        inputs = tokens[batch_index].astype(jnp.float32)

        def layer_fn(values_in, weights_in):
            return forward(values_in, weights_in, resets)
        layer_out, pullback = jax.vjp(layer_fn, inputs, weights)
        seed_grad = cotangent[batch_index].astype(jnp.float32) * slot_mask[:, None]
        input_grad, weight_grads = pullback(seed_grad)
        outputs.append(layer_out.astype(jnp.bfloat16))
        input_grads.append(input_grad)
        totals = tuple((total + grad_term for total, grad_term in zip(totals, weight_grads)))
    return (jnp.stack(outputs), jnp.stack(input_grads), totals[0], totals[1], totals[2], totals[3], totals[4], totals[5], totals[6], totals[7], totals[8], totals[9], totals[10], totals[11], totals[12], totals[13])
```

```python
import functools

import numpy as np

import jax
import jax.numpy as jnp
from jax import lax
from jax.experimental import pallas as pl
from jax.experimental.pallas import tpu as pltpu
from jax.sharding import Mesh
from jax.sharding import PartitionSpec as P

GROUP = 64
EPS = 1e-06
LEVELS = (32, 16, 8, 4, 2, 1)
f32 = jnp.float32
bf16 = jnp.bfloat16
NZ = 4


def dot(a, b, dims):
    return lax.dot_general(a, b, (dims, ((), ())), preferred_element_type=f32)


def nn(a, b):
    return dot(a, b, ((1,), (0,)))


def nt(a, b):
    return dot(a, b, ((1,), (1,)))


def tn(a, b):
    return dot(a, b, ((0,), (0,)))


def swap(x, axis):
    return lax.ppermute(x, axis, [(0, 1), (1, 0)])


def add_low(a, b):
    return (a.astype(f32) + b.astype(f32)).astype(bf16)


def both_in_order(piece, axis, dim):
    other = swap(piece, axis)
    first = lax.axis_index(axis) == 0
    return jnp.where(
        first, jnp.stack([piece, other], dim), jnp.stack([other, piece], dim)
    )


def silu(v):
    return v * jax.nn.sigmoid(v)


def silu_grad(v):
    sig = jax.nn.sigmoid(v)
    return sig * (1.0 + v * (1.0 - sig))


def inv_rms(v):
    return lax.rsqrt(jnp.mean(v * v, axis=-1, keepdims=True) + EPS)


def norm_back(h, r, gain, grad):
    scaled = gain * grad
    inner = jnp.mean(h * scaled, axis=-1, keepdims=True)
    return r * scaled - h * (r * r * r) * inner


def level_map(rows):
    t = np.arange(rows)[:, None]
    u = np.arange(rows)[None, :]
    out = np.zeros((rows, rows), np.int32)
    for at, half in enumerate(LEVELS):
        hit = (t // (2 * half) == u // (2 * half)) & ((t // half) % 2 == 1) & ((u // half) % 2 == 0)
        out[hit] = at + 1
    out[t == u] = len(LEVELS) + 1
    return out


def lower_map(rows):
    t = np.arange(rows)[:, None]
    u = np.arange(rows)[None, :]
    return ((t // GROUP == u // GROUP) & (t >= u)).astype(np.float32)


def ones_times(ones, value):
    hi = value.astype(bf16)
    rest = value - hi.astype(f32)
    mid = rest.astype(bf16)
    low = (rest - mid.astype(f32)).astype(bf16)
    return nn(ones, hi) + (nn(ones, mid) + nn(ones, low))


def level_decay(cum, half):
    rows, width = cum.shape
    span = max(2 * half, 8)
    parts = cum.reshape(rows // span, span, width)
    if half >= 4:
        mid = parts[:, half - 1 : half, :]
    else:
        at = lax.broadcasted_iota(jnp.int32, parts.shape, 1)
        mid = parts[:, half - 1 : half, :]
        for start in range(2 * half, span, 2 * half):
            mid = jnp.where(at >= start, parts[:, start + half - 1 : start + half, :], mid)
    return jnp.exp(-jnp.abs(parts - mid)).reshape(rows, width)


def block_of(array, at):
    return array[at * GROUP : (at + 1) * GROUP, :]


def scan_forward(qkv_ref, decay_ref, lower_ref, level_ref, open_ref, out_ref, query_ref, state_ref, keep_ref):
    step = pl.program_id(0)
    rows, width = decay_ref.shape
    count = rows // GROUP
    scale = width**-0.5
    queries = qkv_ref[:, :width].astype(f32) * scale
    keys = qkv_ref[:, width : 2 * width].astype(f32)
    values = qkv_ref[:, 2 * width :]
    levels = level_ref[...]
    cum = ones_times(lower_ref[...], decay_ref[...])
    scores = jnp.where(
        levels == len(LEVELS) + 1, nt(queries.astype(bf16), keys.astype(bf16)), 0.0
    )
    for at, half in enumerate(LEVELS):
        decay = level_decay(cum, half)
        part = nt((queries * decay).astype(bf16), (keys * decay).astype(bf16))
        scores = jnp.where(levels == at + 1, part, scores)
    local = nn(scores.astype(bf16), values)
    faded = queries * jnp.exp(cum)
    state = jnp.zeros((values.shape[1], width), f32)
    keep = jnp.ones((1, width), f32)
    for c in range(count):
        is_open = open_ref[step, c]
        state = state * is_open
        keep = keep * is_open
        faded_c = block_of(faded, c)
        cum_c = block_of(cum, c)
        last = cum_c[GROUP - 1 :, :]
        here = block_of(local, c)
        if c:
            here = here + nt(faded_c.astype(bf16), state.astype(bf16))
        out_ref[c * GROUP : (c + 1) * GROUP, :] = here
        query_ref[c * GROUP : (c + 1) * GROUP, :] = (faded_c * keep).astype(bf16)
        carried = (block_of(keys, c) * jnp.exp(last - cum_c)).astype(bf16)
        update = tn(block_of(values, c), carried)
        shrink = jnp.exp(last)
        state = state * shrink + update
        keep = keep * shrink
    state_ref[0] = state.astype(bf16)
    keep_ref[0] = jnp.broadcast_to(keep, keep_ref.shape[1:])


def scan_backward(qkv_ref, decay_ref, logit_ref, grad_ref, enter_ref, leave_ref, lower_ref, upper_ref, level_ref, open_ref, out_ref, logit_out_ref, local_ref, past_ref):
    step = pl.program_id(0)
    rows, width = decay_ref.shape
    count = rows // GROUP
    scale = width**-0.5
    queries = qkv_ref[:, :width].astype(f32) * scale
    keys = qkv_ref[:, width : 2 * width].astype(f32)
    values = qkv_ref[:, 2 * width :]
    grads = grad_ref[...]
    levels = level_ref[...]
    cum = ones_times(lower_ref[...], decay_ref[...])
    pair_grad = nt(grads, values)
    on_diagonal = levels == len(LEVELS) + 1
    own = jnp.sum(jnp.where(on_diagonal, pair_grad, 0.0), axis=1, keepdims=True)
    scores = jnp.where(on_diagonal, nt(queries.astype(bf16), keys.astype(bf16)), 0.0)
    query_grad = jnp.zeros((rows, width), f32)
    key_grad = jnp.zeros((rows, width), f32)
    for at, half in enumerate(LEVELS):
        decay = level_decay(cum, half)
        query_l = (queries * decay).astype(bf16)
        key_l = (keys * decay).astype(bf16)
        hit = levels == at + 1
        scores = jnp.where(hit, nt(query_l, key_l), scores)
        grad_l = jnp.where(hit, pair_grad, 0.0).astype(bf16)
        query_grad = query_grad + nn(grad_l, key_l) * decay
        key_grad = key_grad + tn(grad_l, query_l) * decay
    value_grad = tn(scores.astype(bf16), grads)
    rising = jnp.exp(cum)
    faded = queries * rising
    state = enter_ref[0].astype(f32)
    for c in range(count):
        state = state * open_ref[step, c]
        past_ref[c] = state
        cum_c = block_of(cum, c)
        last = cum_c[GROUP - 1 :, :]
        if c < count - 1:
            carried = (block_of(keys, c) * jnp.exp(last - cum_c)).astype(bf16)
            state = state * jnp.exp(last) + tn(block_of(values, c), carried)
    after = leave_ref[0].astype(f32)
    for c in range(count - 1, -1, -1):
        span = slice(c * GROUP, (c + 1) * GROUP)
        past = past_ref[c]
        cum_c = block_of(cum, c)
        last = cum_c[GROUP - 1 :, :]
        shrink = jnp.exp(last)
        fading = jnp.exp(last - cum_c)
        keys_c = block_of(keys, c)
        queries_c = block_of(queries, c)
        grads_c = block_of(grads, c)
        after_low = after.astype(bf16)
        query_c = block_of(query_grad, c) + nn(grads_c, past.astype(bf16)) * block_of(rising, c)
        key_far = nn(block_of(values, c), after_low) * fading
        key_c = block_of(key_grad, c) + key_far
        value_c = block_of(value_grad, c) + nt((keys_c * fading).astype(bf16), after_low)
        own_c = block_of(own, c)
        out_ref[span, :width] = ((query_c + own_c * keys_c) * scale).astype(bf16)
        out_ref[span, width : 2 * width] = (key_c + own_c * queries_c).astype(bf16)
        out_ref[span, 2 * width :] = value_c.astype(bf16)
        local_ref[span, :] = queries_c * query_c - keys_c * key_c
        at_last = jnp.sum(keys_c * key_far, axis=0, keepdims=True) + shrink * jnp.sum(
            past * after, axis=0, keepdims=True
        )
        logit_out_ref[span, :] = jnp.broadcast_to(at_last, (GROUP, width))
        if c:
            after = (after * shrink + tn(grads_c, block_of(faded, c).astype(bf16))) * open_ref[step, c]
    decay_grad = ones_times(upper_ref[...], local_ref[...]) + logit_out_ref[...]
    logit_out_ref[...] = decay_grad * jax.nn.sigmoid(-logit_ref[...]) * (1.0 / 16.0)


def call_forward(qkv, decays, is_open, micro_count):
    rows = qkv.shape[0] // micro_count
    width = decays.shape[1]
    wide = qkv.shape[1] - 2 * width
    lower = jnp.asarray(lower_map(rows), bf16)
    level = jnp.asarray(level_map(rows))
    whole = lambda m: (0, 0)
    mine = lambda m: (m, 0)
    mine3 = lambda m: (m, 0, 0)
    return pl.pallas_call(
        scan_forward,
        grid=(micro_count,),
        in_specs=[
            pl.BlockSpec((rows, qkv.shape[1]), mine),
            pl.BlockSpec((rows, width), mine),
            pl.BlockSpec((rows, rows), whole),
            pl.BlockSpec((rows, rows), whole),
            pl.BlockSpec(memory_space=pltpu.SMEM),
        ],
        out_specs=[
            pl.BlockSpec((rows, wide), mine),
            pl.BlockSpec((rows, width), mine),
            pl.BlockSpec((1, wide, width), mine3),
            pl.BlockSpec((1, 8, width), mine3),
        ],
        out_shape=[
            jax.ShapeDtypeStruct((micro_count * rows, wide), f32),
            jax.ShapeDtypeStruct((micro_count * rows, width), bf16),
            jax.ShapeDtypeStruct((micro_count, wide, width), bf16),
            jax.ShapeDtypeStruct((micro_count, 8, width), f32),
        ],
        compiler_params=pltpu.CompilerParams(vmem_limit_bytes=40 * 2**20),
        cost_estimate=pl.CostEstimate(flops=2_000_000_000, bytes_accessed=8_000_000, transcendentals=1_500_000),
        name="scan_forward",
    )(qkv, decays, lower, level, is_open)


def call_backward(qkv, decays, logits, grads, enter, leave, is_open, micro_count):
    rows = qkv.shape[0] // micro_count
    width = decays.shape[1]
    wide = qkv.shape[1] - 2 * width
    lower = jnp.asarray(lower_map(rows), bf16)
    upper = jnp.asarray(lower_map(rows).T, bf16)
    level = jnp.asarray(level_map(rows))
    whole = lambda m: (0, 0)
    mine = lambda m: (m, 0)
    mine3 = lambda m: (m, 0, 0)
    return pl.pallas_call(
        scan_backward,
        grid=(micro_count,),
        in_specs=[
            pl.BlockSpec((rows, qkv.shape[1]), mine),
            pl.BlockSpec((rows, width), mine),
            pl.BlockSpec((rows, width), mine),
            pl.BlockSpec((rows, wide), mine),
            pl.BlockSpec((1, wide, width), mine3),
            pl.BlockSpec((1, wide, width), mine3),
            pl.BlockSpec((rows, rows), whole),
            pl.BlockSpec((rows, rows), whole),
            pl.BlockSpec((rows, rows), whole),
            pl.BlockSpec(memory_space=pltpu.SMEM),
        ],
        out_specs=[
            pl.BlockSpec((rows, qkv.shape[1]), mine),
            pl.BlockSpec((rows, width), mine),
        ],
        out_shape=[
            jax.ShapeDtypeStruct((micro_count * rows, qkv.shape[1]), bf16),
            jax.ShapeDtypeStruct((micro_count * rows, width), f32),
        ],
        scratch_shapes=[
            pltpu.VMEM((rows, width), f32),
            pltpu.VMEM((rows // GROUP, wide, width), f32),
        ],
        compiler_params=pltpu.CompilerParams(vmem_limit_bytes=40 * 2**20),
        cost_estimate=pl.CostEstimate(flops=5_000_000_000, bytes_accessed=12_000_000, transcendentals=1_500_000),
        name="scan_backward",
    )(qkv, decays, logits, grads, enter, leave, lower, upper, level, is_open)


def pass_states(state, keep, reverse):
    ctx = ("z", "y")
    count = lax.axis_size(ctx)
    micro, wide, width = state.shape
    strip = wide // count
    parts = state.reshape(micro, count, strip, width).transpose(1, 0, 2, 3)
    parts = parts.reshape(count, micro * strip, width)
    keep_hi = keep.astype(bf16)
    keep_lo = (keep - keep_hi.astype(f32)).astype(bf16)
    extra = jnp.concatenate([keep_hi, keep_lo, jnp.zeros((16 - 2 * micro, width), bf16)])
    sent = jnp.concatenate(
        [parts, jnp.broadcast_to(extra[None], (count, 16, width))], axis=1
    )
    got = lax.all_to_all(sent, ctx, 0, 0)
    tail = got[:, micro * strip :, :].astype(f32)
    keeps = tail[:, :micro] + tail[:, micro : 2 * micro]
    states = got[:, : micro * strip, :].reshape(count, micro, strip, width)
    running = jnp.zeros((micro, strip, width), f32)
    entering = [None] * count
    order = range(count - 1, -1, -1) if reverse else range(count)
    for at in order:
        entering[at] = running.astype(bf16)
        running = running * keeps[at][:, None, :] + states[at].astype(f32)
    back = lax.all_to_all(jnp.stack(entering), ctx, 0, 0)
    return back.transpose(1, 0, 2, 3).reshape(micro, wide, width)


def gather_plane(piece):
    count = lax.axis_size("y")
    if count == 2:
        a, b = piece[0], piece[1]
        a_y, b_x = swap(a, "y"), swap(b, "x")
        a = jnp.stack([a, a_y])
        b = jnp.stack([b, b_x])
        a_x, b_y = swap(a, "x"), swap(b, "y")
        a = jnp.stack([a, a_x])
        b = jnp.stack([b, b_y], axis=1)
        here = jnp.stack([a, b])
    else:
        rows = [piece]
        for k in range(1, count):
            rows.append(lax.ppermute(piece, "y", [((i + k) % count, i) for i in range(count)]))
        here = jnp.stack(rows, axis=1)
        here = jnp.stack([here, swap(here, "x")], axis=1)
    return jnp.stack([here, swap(here, "c")])


def scatter_plane(parts):
    count = lax.axis_size("y")
    here = add_low(parts[0], swap(parts[1], "c"))
    if count == 2:
        a, b = here[0], here[1]
        a_got, b_got = swap(a[1], "x"), swap(b[:, 1], "y")
        a = add_low(a[0], a_got)
        b = add_low(b[:, 0], b_got)
        a_got, b_got = swap(a[1], "y"), swap(b[1], "x")
        a = a[0].astype(f32) + a_got.astype(f32)
        b = b[0].astype(f32) + b_got.astype(f32)
        return jnp.stack([a, b])
    here = add_low(here[:, 0], swap(here[:, 1], "x"))
    total = here[:, 0].astype(f32)
    for k in range(1, count):
        got = lax.ppermute(here[:, k], "y", [(i, (i + k) % count) for i in range(count)])
        total = total + got.astype(f32)
    return total


def scatter_head(part):
    micro, slots, width = part.shape
    c, x = lax.axis_index("c"), lax.axis_index("x")
    view = part.reshape(micro, 2, slots // 2, width)
    mine = lax.dynamic_index_in_dim(view, c, 1, keepdims=False)
    other = lax.dynamic_index_in_dim(view, 1 - c, 1, keepdims=False)
    mine = add_low(mine, swap(other, "c"))
    view = mine.reshape(micro, 2, slots // 4, width)
    mine = lax.dynamic_index_in_dim(view, x, 1, keepdims=False)
    other = lax.dynamic_index_in_dim(view, 1 - x, 1, keepdims=False)
    return mine.astype(f32) + swap(other, "x").astype(f32)


def gather_head(piece):
    micro, quarter, width = piece.shape
    both = both_in_order(piece, "x", 1)
    both = both_in_order(both, "c", 1)
    return both.reshape(micro, 4 * quarter, width)


def own_quarter(array):
    micro, slots, width = array.shape
    c, x = lax.axis_index("c"), lax.axis_index("x")
    view = array.reshape(micro, 4, slots // 4, width)
    return lax.dynamic_index_in_dim(view, 2 * c + x, 1, keepdims=False)


def others_y(piece):
    count = lax.axis_size("y")
    out = [piece]
    for k in range(1, count):
        out.append(lax.ppermute(piece, "y", [((i + k) % count, i) for i in range(count)]))
    return out


def relative_columns(array, k):
    count, y = lax.axis_size("y"), lax.axis_index("y")
    t, depth = array.shape
    view = array.reshape(t, NZ, count, depth // (NZ * count))
    at = lax.rem(y + k, count)
    return lax.dynamic_index_in_dim(view, at, 2, keepdims=False).reshape(t, -1)


def absolute_columns(parts):
    count, y = lax.axis_size("y"), lax.axis_index("y")
    t = parts[0].shape[0]
    views = [p.reshape(t, NZ, -1) for p in parts]
    if count == 2:
        stacked = jnp.where(y == 0, jnp.stack(views, 2), jnp.stack(views[::-1], 2))
    else:
        stacked = jnp.roll(jnp.stack(views, 2), y, axis=2)
    return stacked.reshape(t, -1)


def sum_rows(parts):
    count = lax.axis_size("y")
    total = parts[0].astype(f32)
    for k in range(1, count):
        got = lax.ppermute(parts[k], "y", [(i, (i + k) % count) for i in range(count)])
        total = total + got.astype(f32)
    return lax.psum_scatter(total.astype(bf16), "z", scatter_dimension=0, tiled=True).astype(f32)


def per_device(
    tokens, cotangent, lengths, norm_in, w_query, w_key, w_value, w_outgate, w_rank,
    w_decay, decay_bias, head_gain, w_out, norm_mid, w_gate, w_up, w_down,
):
    ctx = ("z", "y")
    ny = lax.axis_size("y")
    nctx = NZ * ny
    y = lax.axis_index("y")
    place = lax.axis_index(ctx)
    micro, slots, depth = tokens.shape
    groups = slots // GROUP
    rl = w_query.shape[0]
    width = w_query.shape[1]
    wide = w_value.shape[1]
    rank = w_rank.shape[1]
    ff = w_gate.shape[1]
    fl = ff // ny
    total = micro * slots

    w_qkv = jnp.concatenate([w_query, w_key, w_value], axis=1)
    w_go = jnp.concatenate([w_outgate, w_out.T], axis=1)
    qkv_parts = others_y(lax.all_gather(w_qkv, "z", axis=0, tiled=True))
    go_parts = others_y(lax.all_gather(w_go, "z", axis=0, tiled=True))

    small = jnp.concatenate(
        [norm_in, norm_mid, w_rank.T.reshape(-1), w_decay[0].reshape(-1), decay_bias[0], head_gain]
    )
    n_small = small.shape[0]
    pad = -n_small % 1024
    small = jnp.pad(small, (0, pad)).reshape(1, -1, 128)
    small = jnp.broadcast_to(small, (nctx,) + small.shape[1:])
    small = lax.all_to_all(small, ctx, 0, 0).reshape(nctx, -1)
    at = 0

    def take(size):
        nonlocal at
        at += size
        return small[:, at - size : at]

    gain_in = take(rl).reshape(1, depth).astype(f32)
    gain_mid = take(rl).reshape(1, depth).astype(f32)
    rank_t = take(rank * rl).reshape(nctx, rank, rl).transpose(1, 0, 2).reshape(rank, depth)
    dl = width // nctx
    decay_w = take(rank * dl).reshape(nctx, rank, dl).transpose(1, 0, 2).reshape(rank, width)
    bias = take(dl).reshape(1, width).astype(f32)
    gain_head = take(wide // nctx).reshape(1, wide).astype(f32)

    def unit_pieces(weight):
        return weight.reshape(rl, ny, fl).transpose(1, 0, 2)

    ff_local = jnp.concatenate(
        [unit_pieces(w_gate), unit_pieces(w_up), unit_pieces(w_down.T)], axis=2
    )
    ff_unit = jnp.zeros((ny, rl, 3 * fl), bf16)
    own = lax.dynamic_index_in_dim(ff_local, y, 0)
    ff_unit = lax.dynamic_update_slice_in_dim(ff_unit, own, y, 0)
    for k in range(1, ny):
        sent = lax.dynamic_index_in_dim(ff_local, lax.rem(y + k, ny), 0)
        got = lax.ppermute(sent, "y", [(i, (i + k) % ny) for i in range(ny)])
        ff_unit = lax.dynamic_update_slice_in_dim(ff_unit, got, lax.rem(y - k + ny, ny), 0)
    ff_full = lax.all_gather(ff_unit.reshape(ny * rl, 3 * fl), "z", axis=0, tiled=True)

    slot_ids = place * slots + jnp.arange(slots, dtype=jnp.int32)
    group_ids = place * groups + jnp.arange(groups, dtype=jnp.int32)
    end = jnp.zeros((micro, 1), jnp.int32)
    reset = group_ids[None, :] == end
    for i in range(lengths.shape[1]):
        end = end + lengths[:, i : i + 1]
        reset = reset | (group_ids[None, :] == end)
    is_open = 1.0 - reset.astype(f32)
    slot_mask = (slot_ids[None, :] < end * GROUP).astype(bf16)

    out_low = cotangent * slot_mask[:, :, None]
    c_at, x_at = lax.axis_index("c"), lax.axis_index("x")
    quarter = slots // 4
    view = out_low.reshape(micro, 2, 2, quarter, depth)
    near = lax.dynamic_index_in_dim(view, c_at, 1, keepdims=False)
    far = lax.dynamic_index_in_dim(view, 1 - c_at, 1, keepdims=False)

    def x_order(half):
        first = lax.dynamic_index_in_dim(half, x_at, 1, keepdims=False)
        second = lax.dynamic_index_in_dim(half, 1 - x_at, 1, keepdims=False)
        return jnp.stack([first, second], 1)

    near, far = x_order(near), x_order(far)
    near_y = others_y(near)[1:]
    near_y = jnp.stack(near_y, 2)
    far_y = swap(near_y, "c")
    plane_low = jnp.stack(
        [
            jnp.concatenate([near[:, :, None], near_y], 2),
            jnp.concatenate([far[:, :, None], far_y], 2),
        ]
    ).reshape(-1, depth)

    inputs = tokens.astype(f32).reshape(total, depth)
    r_in = inv_rms(inputs)
    normed_in = (inputs * r_in * gain_in).astype(bf16)
    normed_parts = [relative_columns(normed_in, k) for k in range(ny)]
    low_rank = nt(normed_in, rank_t).astype(bf16)
    logits = nn(low_rank, decay_w) + bias
    decays = jax.nn.log_sigmoid(logits) / 16.0
    qkv = sum(nn(n, w) for n, w in zip(normed_parts, qkv_parts)).astype(bf16)

    local_out, far_query, state, keep = call_forward(qkv, decays, is_open, micro)
    keep = keep[:, 0, :]
    enter = pass_states(state, keep, False)

    outgate = sum(nn(n, w[:, :wide]) for n, w in zip(normed_parts, go_parts))
    outgate = outgate.astype(bf16).astype(f32)
    mixed = local_out + jnp.concatenate(
        [nt(far_query[m * slots : (m + 1) * slots], enter[m]) for m in range(micro)]
    )
    r_head = inv_rms(mixed)
    gated = (mixed * r_head * gain_head * silu(outgate)).astype(bf16)
    attention = jnp.concatenate([nt(gated, w[:, wide:]) for w in go_parts], axis=1)
    attention = scatter_head(attention.astype(bf16).reshape(micro, slots, depth))
    attention = attention.reshape(micro * quarter, depth)
    step = depth // ny
    attention = absolute_columns([attention[:, k * step : (k + 1) * step] for k in range(ny)])
    inputs_own = own_quarter(tokens).reshape(-1, depth).astype(f32)
    residual = inputs_own + attention

    r_mid = inv_rms(residual)
    normed_mid = (residual * r_mid * gain_mid).astype(bf16)
    plane_mid = gather_plane(normed_mid.reshape(micro, quarter, depth))
    plane_shape = plane_mid.shape
    plane_mid = plane_mid.reshape(-1, depth)
    ff_gate, ff_up, ff_down_t = (ff_full[:, i * fl : (i + 1) * fl] for i in range(3))
    gate_proj = nn(plane_mid, ff_gate)
    up_proj = nn(plane_mid, ff_up)
    hidden = (silu(gate_proj) * up_proj).astype(bf16)
    hidden_grad = nn(plane_low, ff_down_t)
    gate_low = (hidden_grad * up_proj * silu_grad(gate_proj)).astype(bf16)
    up_low = (hidden_grad * silu(gate_proj)).astype(bf16)
    mid_part = (nt(gate_low, ff_gate) + nt(up_low, ff_up)).astype(bf16)
    mid_grad = scatter_plane(mid_part.reshape(plane_shape)).reshape(-1, depth)
    ff_grad = jnp.concatenate(
        [tn(plane_mid, gate_low), tn(plane_mid, up_low), tn(plane_low, hidden)], axis=1
    ).astype(bf16)
    ff_grad = lax.psum_scatter(ff_grad, "z", scatter_dimension=0, tiled=True)
    feed_part = nt(hidden, ff_down_t).astype(bf16)

    out_grad = own_quarter(out_low).reshape(-1, depth).astype(f32)
    resid_grad = out_grad + norm_back(residual, r_mid, gain_mid, mid_grad)
    grad_norm_mid = jnp.sum(mid_grad * residual * r_mid, axis=0)
    resid_low = gather_head(resid_grad.astype(bf16).reshape(micro, quarter, depth))
    resid_low = resid_low.reshape(total, depth)
    resid_parts = [relative_columns(resid_low, k) for k in range(ny)]
    gated_grad = sum(nn(n, w[:, wide:]) for n, w in zip(resid_parts, go_parts))

    unit = mixed * r_head
    gate_act = silu(outgate)
    unit_grad = gated_grad * gate_act
    outgate_low = (gated_grad * unit * gain_head * silu_grad(outgate)).astype(bf16)
    mixed_grad = norm_back(mixed, r_head, gain_head, unit_grad).astype(bf16)
    grad_gain = jnp.sum(unit_grad * unit, axis=0)
    state_grad = jnp.stack(
        [
            tn(mixed_grad[m * slots : (m + 1) * slots], far_query[m * slots : (m + 1) * slots])
            for m in range(micro)
        ]
    ).astype(bf16)
    leave = pass_states(state_grad, keep, True)
    qkv_low, logit_grad = call_backward(
        qkv, decays, logits, mixed_grad, enter, leave, is_open, micro
    )
    logit_low = logit_grad.astype(bf16)

    go_grads = [
        jnp.concatenate([tn(n, outgate_low), tn(r, gated)], axis=1).astype(bf16)
        for n, r in zip(normed_parts, resid_parts)
    ]
    go_grad = sum_rows(go_grads)

    rank_part = nt(logit_low, decay_w).astype(bf16)
    rank_pad = jnp.pad(rank_part, ((0, 0), (0, 128 - rank)))
    in_part = [
        (nt(qkv_low, wq) + nt(outgate_low, wg[:, :wide])).astype(bf16)
        for wq, wg in zip(qkv_parts, go_parts)
    ]
    in_sum = jnp.concatenate(in_part + [rank_pad], axis=1)
    in_sum = scatter_head(in_sum.reshape(micro, slots, depth + 128)).reshape(-1, depth + 128)
    qkv_grads = [tn(n, qkv_low).astype(bf16) for n in normed_parts]
    qkv_grad = sum_rows(qkv_grads)
    rank_low = in_sum[:, depth : depth + rank].astype(bf16)
    in_grad = absolute_columns([in_sum[:, k * step : (k + 1) * step] for k in range(ny)])
    in_grad = in_grad + nn(rank_low, rank_t)
    r_own = inv_rms(inputs_own)
    input_own = resid_grad + norm_back(inputs_own, r_own, gain_in, in_grad)
    grad_norm_in = jnp.sum(in_grad * inputs_own * r_own, axis=0)
    normed_own = own_quarter(normed_in.reshape(micro, slots, depth)).reshape(-1, depth)
    grad_rank_t = tn(rank_low, normed_own)
    input_grad = gather_head(input_own.astype(bf16).reshape(micro, quarter, depth)).astype(f32)

    feed = scatter_plane(feed_part.reshape(plane_shape)).reshape(-1, depth)
    block_own = (residual + feed).astype(bf16).reshape(micro, quarter, depth)
    block_out = gather_head(block_own)

    grad_decay = tn(low_rank, logit_low)
    grad_bias = jnp.sum(logit_low.astype(f32), axis=0)
    by_ctx = lambda v: v.reshape(nctx, -1)
    across = lambda v, n: v.reshape(v.shape[0], nctx, n).transpose(1, 0, 2).reshape(nctx, -1)
    summed = jnp.concatenate(
        [by_ctx(grad_norm_in), by_ctx(grad_norm_mid), across(grad_rank_t, rl), by_ctx(grad_gain)], axis=1
    )
    headed = jnp.concatenate([across(grad_decay, dl), by_ctx(grad_bias)], axis=1)
    n_summed, n_headed = summed.shape[1], headed.shape[1]
    pad_s, pad_h = -n_summed % 1024, -n_headed % 1024
    tail = jnp.concatenate(
        [jnp.pad(summed, ((0, 0), (0, pad_s))), jnp.pad(headed, ((0, 0), (0, pad_h)))], axis=1
    ).reshape(nctx, -1, 128)
    tail = jnp.sum(lax.all_to_all(tail, ctx, 0, 0), axis=0)
    cut = (n_summed + pad_s) // 128
    summed, headed = tail[:cut], tail[cut:].reshape(-1)
    summed = summed + swap(summed, "c")
    summed = (summed + swap(summed, "x")).reshape(-1)
    g_norm_in = summed[:rl]
    g_norm_mid = summed[rl : 2 * rl]
    g_rank = summed[2 * rl : (2 + rank) * rl].reshape(rank, rl).T
    g_gain = summed[(2 + rank) * rl : n_summed]
    g_decay = headed[: rank * dl].reshape(1, rank, dl)
    g_bias = headed[rank * dl : n_headed].reshape(1, dl)

    ff_grad = ff_grad.reshape(ny, rl, 3 * fl)
    pieces = jnp.zeros((ny, rl, 3 * fl), bf16)
    pieces = lax.dynamic_update_slice_in_dim(
        pieces, lax.dynamic_index_in_dim(ff_grad, y, 0), y, 0
    )
    for k in range(1, ny):
        sent = lax.dynamic_index_in_dim(ff_grad, lax.rem(y + k, ny), 0)
        got = lax.ppermute(sent, "y", [(i, (i + k) % ny) for i in range(ny)])
        pieces = lax.dynamic_update_slice_in_dim(pieces, got, lax.rem(y - k + ny, ny), 0)

    def joined(i):
        part = pieces[:, :, i * fl : (i + 1) * fl]
        return part.transpose(1, 0, 2).reshape(rl, ff)

    return (
        block_out,
        input_grad,
        g_norm_in,
        qkv_grad[:, :width],
        qkv_grad[:, width : 2 * width],
        qkv_grad[:, 2 * width :],
        go_grad[:, :wide],
        g_rank,
        g_decay,
        g_bias,
        g_gain,
        go_grad[:, wide:].T,
        g_norm_mid,
        joined(0).astype(f32),
        joined(1).astype(f32),
        joined(2).T.astype(f32),
    )


def solution(mesh):
    ctx = mesh.shape["ctx"]
    shape = (NZ, ctx // NZ, 2, mesh.shape["head"] // 2)
    fine = Mesh(mesh.devices.reshape(shape), ("z", "y", "x", "c"))
    c, h = ("z", "y"), ("x", "c")
    in_specs = (
        P(None, c, None), P(None, c, None), P(), P(c), P(c, h), P(c, h), P(c, h), P(c, h), P(c, None),
        P(h, None, c), P(h, c), P(c), P(h, c), P(c), P(c, h), P(c, h), P(h, c),
    )
    out_specs = (
        P(None, c, None), P(None, c, None), P(c), P(c, h), P(c, h), P(c, h), P(c, h), P(c, None),
        P(h, None, c), P(h, c), P(c), P(h, c), P(c), P(c, h), P(c, h), P(h, c),
    )
    return jax.shard_map(
        per_device, mesh=fine, in_specs=in_specs, out_specs=out_specs, check_vma=False
    )
```

```python
import functools

import numpy as np

import jax
import jax.numpy as jnp
from jax import lax
from jax.experimental import pallas as pl
from jax.experimental.pallas import tpu as pltpu
from jax.sharding import Mesh
from jax.sharding import PartitionSpec as P

GROUP = 64
EPS = 1e-06
LEVELS = (32, 16, 8, 4, 2, 1)
f32 = jnp.float32
bf16 = jnp.bfloat16
NZ = 4


def dot(a, b, dims):
    return lax.dot_general(a, b, (dims, ((), ())), preferred_element_type=f32)


def nn(a, b):
    return dot(a, b, ((1,), (0,)))


def nt(a, b):
    return dot(a, b, ((1,), (1,)))


def tn(a, b):
    return dot(a, b, ((0,), (0,)))


def swap(x, axis):
    return lax.ppermute(x, axis, [(0, 1), (1, 0)])


def after(value, *earlier):
    anywhere = pl.BlockSpec(memory_space=pl.ANY)
    return pl.pallas_call(
        lambda *refs: None,
        in_specs=[anywhere] * (1 + len(earlier)),
        out_specs=anywhere,
        out_shape=jax.ShapeDtypeStruct(value.shape, value.dtype),
        input_output_aliases={0: 0},
        cost_estimate=pl.CostEstimate(flops=0, bytes_accessed=0, transcendentals=0),
        name="after",
    )(value, *earlier)


def add_low(a, b):
    return (a.astype(f32) + b.astype(f32)).astype(bf16)


def both_in_order(piece, axis, dim):
    other = swap(piece, axis)
    first = lax.axis_index(axis) == 0
    return jnp.where(
        first, jnp.stack([piece, other], dim), jnp.stack([other, piece], dim)
    )


def silu(v):
    return v * jax.nn.sigmoid(v)


def silu_grad(v):
    sig = jax.nn.sigmoid(v)
    return sig * (1.0 + v * (1.0 - sig))


def inv_rms(v):
    return lax.rsqrt(jnp.mean(v * v, axis=-1, keepdims=True) + EPS)


def norm_back(h, r, gain, grad):
    scaled = gain * grad
    inner = jnp.mean(h * scaled, axis=-1, keepdims=True)
    return r * scaled - h * (r * r * r) * inner


def level_map(rows):
    t = np.arange(rows)[:, None]
    u = np.arange(rows)[None, :]
    out = np.zeros((rows, rows), np.int32)
    for at, half in enumerate(LEVELS):
        hit = (t // (2 * half) == u // (2 * half)) & ((t // half) % 2 == 1) & ((u // half) % 2 == 0)
        out[hit] = at + 1
    out[t == u] = len(LEVELS) + 1
    return out


def lower_map(rows):
    t = np.arange(rows)[:, None]
    u = np.arange(rows)[None, :]
    return ((t // GROUP == u // GROUP) & (t >= u)).astype(np.float32)


def ones_times(ones, value):
    hi = value.astype(bf16)
    rest = value - hi.astype(f32)
    mid = rest.astype(bf16)
    low = (rest - mid.astype(f32)).astype(bf16)
    return nn(ones, hi) + (nn(ones, mid) + nn(ones, low))


def level_decay(cum, half):
    rows, width = cum.shape
    span = max(2 * half, 8)
    parts = cum.reshape(rows // span, span, width)
    if half >= 4:
        mid = parts[:, half - 1 : half, :]
    else:
        at = lax.broadcasted_iota(jnp.int32, parts.shape, 1)
        mid = parts[:, half - 1 : half, :]
        for start in range(2 * half, span, 2 * half):
            mid = jnp.where(at >= start, parts[:, start + half - 1 : start + half, :], mid)
    return jnp.exp(-jnp.abs(parts - mid)).reshape(rows, width)


def block_of(array, at):
    return array[at * GROUP : (at + 1) * GROUP, :]


def scan_forward(qkv_ref, decay_ref, lower_ref, level_ref, open_ref, out_ref, query_ref, state_ref, keep_ref):
    step = pl.program_id(0)
    rows, width = decay_ref.shape
    count = rows // GROUP
    scale = width**-0.5
    queries = qkv_ref[:, :width].astype(f32) * scale
    keys = qkv_ref[:, width : 2 * width].astype(f32)
    values = qkv_ref[:, 2 * width :]
    levels = level_ref[...]
    cum = ones_times(lower_ref[...], decay_ref[...])
    scores = jnp.where(
        levels == len(LEVELS) + 1, nt(queries.astype(bf16), keys.astype(bf16)), 0.0
    )
    for at, half in enumerate(LEVELS):
        decay = level_decay(cum, half)
        part = nt((queries * decay).astype(bf16), (keys * decay).astype(bf16))
        scores = jnp.where(levels == at + 1, part, scores)
    local = nn(scores.astype(bf16), values)
    faded = queries * jnp.exp(cum)
    state = jnp.zeros((values.shape[1], width), f32)
    keep = jnp.ones((1, width), f32)
    for c in range(count):
        is_open = open_ref[step, c]
        state = state * is_open
        keep = keep * is_open
        faded_c = block_of(faded, c)
        cum_c = block_of(cum, c)
        last = cum_c[GROUP - 1 :, :]
        here = block_of(local, c)
        if c:
            here = here + nt(faded_c.astype(bf16), state.astype(bf16))
        out_ref[c * GROUP : (c + 1) * GROUP, :] = here
        query_ref[c * GROUP : (c + 1) * GROUP, :] = (faded_c * keep).astype(bf16)
        carried = (block_of(keys, c) * jnp.exp(last - cum_c)).astype(bf16)
        update = tn(block_of(values, c), carried)
        shrink = jnp.exp(last)
        state = state * shrink + update
        keep = keep * shrink
    state_ref[0] = state.astype(bf16)
    keep_ref[0] = jnp.broadcast_to(keep, keep_ref.shape[1:])


def scan_backward(qkv_ref, decay_ref, logit_ref, grad_ref, enter_ref, leave_ref, lower_ref, upper_ref, level_ref, open_ref, *rest):
    out_ref, logit_out_ref, local_ref, past_ref = rest[-4:]
    step = pl.program_id(0)
    rows, width = decay_ref.shape
    count = rows // GROUP
    scale = width**-0.5
    queries = qkv_ref[:, :width].astype(f32) * scale
    keys = qkv_ref[:, width : 2 * width].astype(f32)
    values = qkv_ref[:, 2 * width :]
    grads = grad_ref[...]
    levels = level_ref[...]
    cum = ones_times(lower_ref[...], decay_ref[...])
    pair_grad = nt(grads, values)
    on_diagonal = levels == len(LEVELS) + 1
    own = jnp.sum(jnp.where(on_diagonal, pair_grad, 0.0), axis=1, keepdims=True)
    scores = jnp.where(on_diagonal, nt(queries.astype(bf16), keys.astype(bf16)), 0.0)
    query_grad = jnp.zeros((rows, width), f32)
    key_grad = jnp.zeros((rows, width), f32)
    for at, half in enumerate(LEVELS):
        decay = level_decay(cum, half)
        query_l = (queries * decay).astype(bf16)
        key_l = (keys * decay).astype(bf16)
        hit = levels == at + 1
        scores = jnp.where(hit, nt(query_l, key_l), scores)
        grad_l = jnp.where(hit, pair_grad, 0.0).astype(bf16)
        query_grad = query_grad + nn(grad_l, key_l) * decay
        key_grad = key_grad + tn(grad_l, query_l) * decay
    value_grad = tn(scores.astype(bf16), grads)
    rising = jnp.exp(cum)
    faded = queries * rising
    state = enter_ref[0].astype(f32)
    for c in range(count):
        state = state * open_ref[step, c]
        past_ref[c] = state
        cum_c = block_of(cum, c)
        last = cum_c[GROUP - 1 :, :]
        if c < count - 1:
            carried = (block_of(keys, c) * jnp.exp(last - cum_c)).astype(bf16)
            state = state * jnp.exp(last) + tn(block_of(values, c), carried)
    after = leave_ref[0].astype(f32)
    for c in range(count - 1, -1, -1):
        span = slice(c * GROUP, (c + 1) * GROUP)
        past = past_ref[c]
        cum_c = block_of(cum, c)
        last = cum_c[GROUP - 1 :, :]
        shrink = jnp.exp(last)
        fading = jnp.exp(last - cum_c)
        keys_c = block_of(keys, c)
        queries_c = block_of(queries, c)
        grads_c = block_of(grads, c)
        after_low = after.astype(bf16)
        query_c = block_of(query_grad, c) + nn(grads_c, past.astype(bf16)) * block_of(rising, c)
        key_far = nn(block_of(values, c), after_low) * fading
        key_c = block_of(key_grad, c) + key_far
        value_c = block_of(value_grad, c) + nt((keys_c * fading).astype(bf16), after_low)
        own_c = block_of(own, c)
        out_ref[span, :width] = ((query_c + own_c * keys_c) * scale).astype(bf16)
        out_ref[span, width : 2 * width] = (key_c + own_c * queries_c).astype(bf16)
        out_ref[span, 2 * width :] = value_c.astype(bf16)
        local_ref[span, :] = queries_c * query_c - keys_c * key_c
        at_last = jnp.sum(keys_c * key_far, axis=0, keepdims=True) + shrink * jnp.sum(
            past * after, axis=0, keepdims=True
        )
        logit_out_ref[span, :] = jnp.broadcast_to(at_last, (GROUP, width))
        if c:
            after = (after * shrink + tn(grads_c, block_of(faded, c).astype(bf16))) * open_ref[step, c]
    decay_grad = ones_times(upper_ref[...], local_ref[...]) + logit_out_ref[...]
    logit_out_ref[...] = decay_grad * jax.nn.sigmoid(-logit_ref[...]) * (1.0 / 16.0)


def call_forward(qkv, decays, is_open, micro_count):
    rows = qkv.shape[0] // micro_count
    width = decays.shape[1]
    wide = qkv.shape[1] - 2 * width
    lower = jnp.asarray(lower_map(rows), bf16)
    level = jnp.asarray(level_map(rows))
    whole = lambda m: (0, 0)
    mine = lambda m: (m, 0)
    mine3 = lambda m: (m, 0, 0)
    return pl.pallas_call(
        scan_forward,
        grid=(micro_count,),
        in_specs=[
            pl.BlockSpec((rows, qkv.shape[1]), mine),
            pl.BlockSpec((rows, width), mine),
            pl.BlockSpec((rows, rows), whole),
            pl.BlockSpec((rows, rows), whole),
            pl.BlockSpec(memory_space=pltpu.SMEM),
        ],
        out_specs=[
            pl.BlockSpec((rows, wide), mine),
            pl.BlockSpec((rows, width), mine),
            pl.BlockSpec((1, wide, width), mine3),
            pl.BlockSpec((1, 8, width), mine3),
        ],
        out_shape=[
            jax.ShapeDtypeStruct((micro_count * rows, wide), f32),
            jax.ShapeDtypeStruct((micro_count * rows, width), bf16),
            jax.ShapeDtypeStruct((micro_count, wide, width), bf16),
            jax.ShapeDtypeStruct((micro_count, 8, width), f32),
        ],
        compiler_params=pltpu.CompilerParams(vmem_limit_bytes=40 * 2**20),
        cost_estimate=pl.CostEstimate(flops=2_000_000_000, bytes_accessed=8_000_000, transcendentals=1_500_000),
        name="scan_forward",
    )(qkv, decays, lower, level, is_open)


def call_backward(qkv, decays, logits, grads, enter, leave, is_open, micro_count, *earlier):
    rows = qkv.shape[0] // micro_count
    width = decays.shape[1]
    wide = qkv.shape[1] - 2 * width
    lower = jnp.asarray(lower_map(rows), bf16)
    upper = jnp.asarray(lower_map(rows).T, bf16)
    level = jnp.asarray(level_map(rows))
    whole = lambda m: (0, 0)
    mine = lambda m: (m, 0)
    mine3 = lambda m: (m, 0, 0)
    return pl.pallas_call(
        scan_backward,
        grid=(micro_count,),
        in_specs=[
            pl.BlockSpec((rows, qkv.shape[1]), mine),
            pl.BlockSpec((rows, width), mine),
            pl.BlockSpec((rows, width), mine),
            pl.BlockSpec((rows, wide), mine),
            pl.BlockSpec((1, wide, width), mine3),
            pl.BlockSpec((1, wide, width), mine3),
            pl.BlockSpec((rows, rows), whole),
            pl.BlockSpec((rows, rows), whole),
            pl.BlockSpec((rows, rows), whole),
            pl.BlockSpec(memory_space=pltpu.SMEM),
        ]
        + [pl.BlockSpec(memory_space=pl.ANY)] * len(earlier),
        out_specs=[
            pl.BlockSpec((rows, qkv.shape[1]), mine),
            pl.BlockSpec((rows, width), mine),
        ],
        out_shape=[
            jax.ShapeDtypeStruct((micro_count * rows, qkv.shape[1]), bf16),
            jax.ShapeDtypeStruct((micro_count * rows, width), f32),
        ],
        scratch_shapes=[
            pltpu.VMEM((rows, width), f32),
            pltpu.VMEM((rows // GROUP, wide, width), f32),
        ],
        compiler_params=pltpu.CompilerParams(vmem_limit_bytes=40 * 2**20),
        cost_estimate=pl.CostEstimate(flops=5_000_000_000, bytes_accessed=12_000_000, transcendentals=1_500_000),
        name="scan_backward",
    )(qkv, decays, logits, grads, enter, leave, lower, upper, level, is_open, *earlier)


def scan_states(got_ref, out_ref, *, micro, strip, reverse):
    count = got_ref.shape[0]
    width = got_ref.shape[2]
    running = [jnp.zeros((strip, width), f32) for _ in range(micro)]
    order = range(count - 1, -1, -1) if reverse else range(count)
    for at in order:
        tail = got_ref[at, micro * strip :, :].astype(f32)
        for m in range(micro):
            span = slice(m * strip, (m + 1) * strip)
            out_ref[at, span, :] = running[m].astype(bf16)
            keep = tail[m : m + 1, :] + tail[micro + m : micro + m + 1, :]
            running[m] = running[m] * keep + got_ref[at, span, :].astype(f32)


def pass_states(state, keep, reverse):
    ctx = ("z", "y")
    count = lax.axis_size(ctx)
    micro, wide, width = state.shape
    strip = wide // count
    parts = state.reshape(micro, count, strip, width).transpose(1, 0, 2, 3)
    parts = parts.reshape(count, micro * strip, width)
    keep_hi = keep.astype(bf16)
    keep_lo = (keep - keep_hi.astype(f32)).astype(bf16)
    extra = jnp.concatenate([keep_hi, keep_lo, jnp.zeros((16 - 2 * micro, width), bf16)])
    sent = jnp.concatenate(
        [parts, jnp.broadcast_to(extra[None], (count, 16, width))], axis=1
    )
    got = lax.all_to_all(sent, ctx, 0, 0)
    entering = pl.pallas_call(
        functools.partial(scan_states, micro=micro, strip=strip, reverse=reverse),
        out_shape=jax.ShapeDtypeStruct((count, micro * strip, width), bf16),
        compiler_params=pltpu.CompilerParams(vmem_limit_bytes=16 * 2**20),
        cost_estimate=pl.CostEstimate(flops=2_000_000, bytes_accessed=1_100_000, transcendentals=0),
        name="scan_states",
    )(got)
    back = lax.all_to_all(entering, ctx, 0, 0)
    return back.reshape(count, micro, strip, width).transpose(1, 0, 2, 3).reshape(micro, wide, width)


def feed_kernel(mid_ref, low_ref, weight_ref, *rest, units):
    pair_ref, hidden_ref, grad_ref = rest[-3:]
    both = nn(mid_ref[...], weight_ref[:, : 2 * units])
    gate, up = both[:, :units], both[:, units:]
    back = nn(low_ref[...], weight_ref[:, 2 * units :])
    sig = jax.nn.sigmoid(gate)
    act = gate * sig
    hidden_ref[...] = (act * up).astype(bf16)
    pair_ref[:, :units] = (back * up * (sig * (1.0 + gate * (1.0 - sig)))).astype(bf16)
    pair_ref[:, units:] = (back * act).astype(bf16)
    grad_ref[...] = nt(pair_ref[...], weight_ref[:, : 2 * units]).astype(bf16)


def call_feed(plane_mid, plane_low, weight, units, *earlier):
    rows, depth = plane_mid.shape
    tile = 256
    return pl.pallas_call(
        functools.partial(feed_kernel, units=units),
        grid=(rows // tile,),
        in_specs=[
            pl.BlockSpec((tile, depth), lambda i: (i, 0)),
            pl.BlockSpec((tile, depth), lambda i: (i, 0)),
            pl.BlockSpec(weight.shape, lambda i: (0, 0), pipeline_mode=pl.Buffered(1)),
        ]
        + [pl.BlockSpec(memory_space=pl.ANY)] * len(earlier),
        out_specs=[
            pl.BlockSpec((tile, 2 * units), lambda i: (i, 0)),
            pl.BlockSpec((tile, units), lambda i: (i, 0)),
            pl.BlockSpec((tile, depth), lambda i: (i, 0)),
        ],
        out_shape=[
            jax.ShapeDtypeStruct((rows, 2 * units), bf16),
            jax.ShapeDtypeStruct((rows, units), bf16),
            jax.ShapeDtypeStruct((rows, depth), bf16),
        ],
        compiler_params=pltpu.CompilerParams(vmem_limit_bytes=48 * 2**20),
        cost_estimate=pl.CostEstimate(
            flops=10 * rows * depth * units, bytes_accessed=28_000_000, transcendentals=rows * units
        ),
        name="feed_forward",
    )(plane_mid, plane_low, weight, *earlier)


def split_units(gate_ref, up_ref, down_ref, out_ref):
    parts, rows, width = out_ref.shape
    units = width // 3
    for k in range(parts):
        span = slice(k * units, (k + 1) * units)
        out_ref[k, :, :units] = gate_ref[:, span]
        out_ref[k, :, units : 2 * units] = up_ref[:, span]
        out_ref[k, :, 2 * units :] = down_ref[span, :].astype(f32).T.astype(bf16)


def call_split(w_gate, w_up, w_down, parts):
    rows, ff = w_gate.shape
    return pl.pallas_call(
        split_units,
        out_shape=jax.ShapeDtypeStruct((parts, rows, 3 * ff // parts), bf16),
        compiler_params=pltpu.CompilerParams(vmem_limit_bytes=32 * 2**20),
        cost_estimate=pl.CostEstimate(flops=0, bytes_accessed=12 * rows * ff, transcendentals=0),
        name="split_units",
    )(w_gate, w_up, w_down)


def join_units(in_ref, gate_ref, up_ref, down_ref):
    parts, rows, width = in_ref.shape
    units = width // 3
    for k in range(parts):
        span = slice(k * units, (k + 1) * units)
        gate_ref[:, span] = in_ref[k, :, :units].astype(f32)
        up_ref[:, span] = in_ref[k, :, units : 2 * units].astype(f32)
        down_ref[span, :] = in_ref[k, :, 2 * units :].astype(f32).T


def call_join(pieces):
    parts, rows, width = pieces.shape
    ff = width // 3 * parts
    return pl.pallas_call(
        join_units,
        out_shape=[
            jax.ShapeDtypeStruct((rows, ff), f32),
            jax.ShapeDtypeStruct((rows, ff), f32),
            jax.ShapeDtypeStruct((ff, rows), f32),
        ],
        compiler_params=pltpu.CompilerParams(vmem_limit_bytes=32 * 2**20),
        cost_estimate=pl.CostEstimate(flops=0, bytes_accessed=18 * rows * ff, transcendentals=0),
        name="join_units",
    )(pieces)


def feed_grad_kernel(*refs):
    out_ref = refs[-1]
    two = refs[2].shape[1]
    mid_a, low_a, pair_a, hidden_a, mid_b, low_b, pair_b, hidden_b = (r[...] for r in refs[:8])
    out_ref[:, :two] = (tn(mid_a, pair_a) + tn(mid_b, pair_b)).astype(bf16)
    out_ref[:, two:] = (tn(low_a, hidden_a) + tn(low_b, hidden_b)).astype(bf16)


def call_feed_grad(near, far, *earlier):
    rows, depth = near[0].shape
    two, units = near[2].shape[1], near[3].shape[1]
    tile = 256
    one = [
        pl.BlockSpec((rows, tile), lambda i: (0, i)),
        pl.BlockSpec((rows, tile), lambda i: (0, i)),
        pl.BlockSpec((rows, two), lambda i: (0, 0), pipeline_mode=pl.Buffered(1)),
        pl.BlockSpec((rows, units), lambda i: (0, 0), pipeline_mode=pl.Buffered(1)),
    ]
    return pl.pallas_call(
        feed_grad_kernel,
        grid=(depth // tile,),
        in_specs=one + one + [pl.BlockSpec(memory_space=pl.ANY)] * len(earlier),
        out_specs=pl.BlockSpec((tile, two + units), lambda i: (i, 0)),
        out_shape=jax.ShapeDtypeStruct((depth, two + units), bf16),
        compiler_params=pltpu.CompilerParams(vmem_limit_bytes=48 * 2**20),
        cost_estimate=pl.CostEstimate(
            flops=4 * rows * depth * (two + units), bytes_accessed=21_000_000, transcendentals=0
        ),
        name="feed_grad",
    )(*near, *far, *earlier)


def gather_plane(piece):
    count = lax.axis_size("y")
    if count == 2:
        a, b = piece[0], piece[1]
        a_y, b_x = swap(a, "y"), swap(b, "x")
        a, b = jnp.stack([a, a_y]), jnp.stack([b, b_x])
        a_x, b_y = swap(a, "x"), swap(b, "y")
        here = jnp.concatenate([a, a_x, b, b_y])
    else:
        rows = [piece]
        for k in range(1, count):
            rows.append(lax.ppermute(piece, "y", [((i + k) % count, i) for i in range(count)]))
        here = jnp.stack(rows, axis=1)
        here = jnp.stack([here, swap(here, "x")], axis=1)
        here = here.reshape((-1,) + piece.shape[1:])
    here = here.reshape(-1, piece.shape[-1])
    return here, swap(here, "c")


def scatter_plane(here, micro, quarter, *between):
    count = lax.axis_size("y")
    depth = here.shape[-1]
    if count == 2:
        here = here.reshape(2, 2, 2 * quarter, depth)
        a, b = here[0], here[1]
        a_got, b_got = swap(a[1], "x"), swap(b[1], "y")
        a = add_low(a[0], a_got).reshape(2, quarter, depth)
        b = add_low(b[0], b_got).reshape(2, quarter, depth)
        if between:
            a, b = after(a, *between), after(b, *between)
        a_got, b_got = swap(a[1], "y"), swap(b[1], "x")
        a = a[0].astype(f32) + a_got.astype(f32)
        b = b[0].astype(f32) + b_got.astype(f32)
        return jnp.stack([a, b])
    here = here.reshape(micro, 2, count, quarter, depth)
    here = add_low(here[:, 0], swap(here[:, 1], "x"))
    total = here[:, 0].astype(f32)
    for k in range(1, count):
        got = lax.ppermute(here[:, k], "y", [(i, (i + k) % count) for i in range(count)])
        total = total + got.astype(f32)
    return total


def scatter_head(part):
    micro, slots, width = part.shape
    c, x = lax.axis_index("c"), lax.axis_index("x")
    view = part.reshape(micro, 2, slots // 2, width)
    mine = lax.dynamic_index_in_dim(view, c, 1, keepdims=False)
    other = lax.dynamic_index_in_dim(view, 1 - c, 1, keepdims=False)
    mine = add_low(mine, swap(other, "c"))
    view = mine.reshape(micro, 2, slots // 4, width)
    mine = lax.dynamic_index_in_dim(view, x, 1, keepdims=False)
    other = lax.dynamic_index_in_dim(view, 1 - x, 1, keepdims=False)
    return mine.astype(f32) + swap(other, "x").astype(f32)


def gather_head(piece):
    micro, quarter, width = piece.shape
    both = both_in_order(piece, "x", 1)
    both = both_in_order(both, "c", 1)
    return both.reshape(micro, 4 * quarter, width)


def own_quarter(array):
    micro, slots, width = array.shape
    c, x = lax.axis_index("c"), lax.axis_index("x")
    view = array.reshape(micro, 4, slots // 4, width)
    return lax.dynamic_index_in_dim(view, 2 * c + x, 1, keepdims=False)


def others_y(piece):
    count = lax.axis_size("y")
    out = [piece]
    for k in range(1, count):
        out.append(lax.ppermute(piece, "y", [((i + k) % count, i) for i in range(count)]))
    return out


def to_relative(array):
    count, y = lax.axis_size("y"), lax.axis_index("y")
    t, depth = array.shape
    rl = depth // (NZ * count)
    if count == 2:
        even = jnp.concatenate([array[:, 2 * z * rl : (2 * z + 1) * rl] for z in range(NZ)], axis=1)
        odd = jnp.concatenate([array[:, (2 * z + 1) * rl : (2 * z + 2) * rl] for z in range(NZ)], axis=1)
        first = y == 0
        return jnp.concatenate([jnp.where(first, even, odd), jnp.where(first, odd, even)], axis=1)
    view = jnp.roll(array.reshape(t, NZ, count, rl), -y, axis=2)
    return view.transpose(0, 2, 1, 3).reshape(t, depth)


def to_absolute(array):
    count, y = lax.axis_size("y"), lax.axis_index("y")
    t, depth = array.shape
    rl = depth // (NZ * count)
    if count == 2:
        first = y == 0
        out = []
        for z in range(NZ):
            own = array[:, z * rl : (z + 1) * rl]
            other = array[:, (NZ + z) * rl : (NZ + z + 1) * rl]
            out += [jnp.where(first, own, other), jnp.where(first, other, own)]
        return jnp.concatenate(out, axis=1)
    view = array.reshape(t, count, NZ, rl).transpose(0, 2, 1, 3)
    return jnp.roll(view, y, axis=2).reshape(t, depth)


def vector_by_ctx(value):
    count, y = lax.axis_size("y"), lax.axis_index("y")
    view = value.reshape(value.shape[0], count, NZ, -1)
    if count == 2:
        view = jnp.where(y == 0, view, view[:, ::-1])
    else:
        view = jnp.roll(view, y, axis=1)
    return view.transpose(2, 1, 0, 3).reshape(NZ * count, value.shape[0], -1)


def vector_from_ctx(value):
    count, y = lax.axis_size("y"), lax.axis_index("y")
    view = value.reshape((NZ, count) + value.shape[1:]).transpose(2, 1, 0, 3)
    if count == 2:
        view = jnp.where(y == 0, view, view[:, ::-1])
    else:
        view = jnp.roll(view, -y, axis=1)
    return view.reshape(value.shape[1], -1)


def sum_y(parts):
    count = lax.axis_size("y")
    total = parts[0].astype(f32)
    for k in range(1, count):
        got = lax.ppermute(parts[k], "y", [(i, (i + k) % count) for i in range(count)])
        total = total + got.astype(f32)
    return total.astype(bf16)


def reduce_z(part):
    return lax.psum_scatter(part, "z", scatter_dimension=0, tiled=True)


def per_device(
    tokens, cotangent, lengths, norm_in, w_query, w_key, w_value, w_outgate, w_rank,
    w_decay, decay_bias, head_gain, w_out, norm_mid, w_gate, w_up, w_down,
):
    ctx = ("z", "y")
    ny = lax.axis_size("y")
    nctx = NZ * ny
    y = lax.axis_index("y")
    place = lax.axis_index(ctx)
    micro, slots, depth = tokens.shape
    groups = slots // GROUP
    rl = w_query.shape[0]
    width = w_query.shape[1]
    wide = w_value.shape[1]
    rank = w_rank.shape[1]
    ff = w_gate.shape[1]
    fl = ff // ny
    total = micro * slots

    w_qkv = jnp.concatenate([w_query, w_key, w_value], axis=1)
    qkv_rows = lax.all_gather(w_qkv, "z", axis=0, tiled=True)

    small = jnp.concatenate(
        [norm_in, norm_mid, w_rank.T.reshape(-1), w_decay[0].reshape(-1), decay_bias[0], head_gain]
    )
    n_small = small.shape[0]
    pad = -n_small % 1024
    small = after(jnp.pad(small, (0, pad)).reshape(1, -1, 128), qkv_rows)
    small = jnp.broadcast_to(small, (nctx,) + small.shape[1:])
    small = lax.all_to_all(small, ctx, 0, 0).reshape(nctx, -1)
    at = 0

    def take(size):
        nonlocal at
        at += size
        return small[:, at - size : at]

    by_row = vector_from_ctx(take((2 + rank) * rl).reshape(nctx, 2 + rank, rl))
    gain_in = by_row[:1].astype(f32)
    gain_mid = by_row[1:2].astype(f32)
    rank_t = by_row[2:]
    dl = width // nctx
    decay_w = take(rank * dl).reshape(nctx, rank, dl).transpose(1, 0, 2).reshape(rank, width)
    bias = take(dl).reshape(1, width).astype(f32)
    gain_head = take(wide // nctx).reshape(1, wide).astype(f32)

    ff_local = call_split(w_gate, w_up, w_down, ny)
    own = lax.dynamic_index_in_dim(ff_local, y, 0, keepdims=False)
    if ny == 2:
        got = swap(lax.dynamic_index_in_dim(ff_local, 1 - y, 0, keepdims=False), "y")
        ff_unit = jnp.where(y == 0, jnp.stack([own, got]), jnp.stack([got, own]))
    else:
        pieces = [own]
        for k in range(1, ny):
            sent = lax.dynamic_index_in_dim(ff_local, lax.rem(y + ny - k, ny), 0, keepdims=False)
            pieces.append(lax.ppermute(sent, "y", [((i + k) % ny, i) for i in range(ny)]))
        ff_unit = jnp.roll(jnp.stack(pieces), y, axis=0)
    ff_unit = ff_unit.reshape(ny * rl, 3 * fl)

    group_ids = place * groups + jnp.arange(groups, dtype=jnp.int32)
    end = jnp.zeros((micro, 1), jnp.int32)
    reset = group_ids[None, :] == end
    for i in range(lengths.shape[1]):
        end = end + lengths[:, i : i + 1]
        reset = reset | (group_ids[None, :] == end)
    is_open = 1.0 - reset.astype(f32)

    def mask_of(at):
        slot_ids = at * slots + jnp.arange(slots, dtype=jnp.int32)
        return (slot_ids[None, :] < end * GROUP).astype(bf16)[:, :, None]

    c_at, x_at = lax.axis_index("c"), lax.axis_index("x")
    quarter = slots // 4
    view = cotangent.reshape(micro, 2, slots // 2, depth)
    half_parts = others_y(lax.dynamic_index_in_dim(view, c_at, 1, keepdims=False))

    w_go = jnp.concatenate([w_outgate, w_out.T], axis=1)
    go_rows = lax.all_gather(w_go, "z", axis=0, tiled=True)
    ff_full = lax.all_gather(ff_unit, "z", axis=0, tiled=True)
    qkv_parts = others_y(after(qkv_rows, ff_unit, *half_parts[1:]))
    go_parts = others_y(go_rows)

    inputs = to_relative(tokens.reshape(total, depth)).astype(f32)
    r_in = inv_rms(inputs)
    normed_in = (inputs * r_in * gain_in).astype(bf16)
    step = depth // ny
    low_rank = nt(normed_in, rank_t).astype(bf16)
    logits = nn(low_rank, decay_w) + bias
    decays = jax.nn.log_sigmoid(logits) / 16.0

    def columns(array, k):
        return array[:, k * step : (k + 1) * step]

    qkv = sum(nn(columns(normed_in, k), w) for k, w in enumerate(qkv_parts)).astype(bf16)

    once = jnp.minimum(lengths[0, 0], 1)

    def recurrence(_, carry):
        local_out, far_query, state, keep = call_forward(qkv, decays, is_open, micro)
        keep = keep[:, 0, :]
        return local_out, far_query, pass_states(state, keep, False), keep

    local_out, far_query, enter, keep = lax.fori_loop(
        0,
        once,
        recurrence,
        (
            jnp.zeros((total, wide), f32),
            jnp.zeros((total, width), bf16),
            jnp.zeros((micro, wide, width), bf16),
            jnp.zeros((micro, width), f32),
        ),
    )

    out_low = cotangent * mask_of(place)
    low_parts = []
    for k, half in enumerate(half_parts):
        mask = mask_of(place - y + lax.rem(y + k, ny)).reshape(micro, 2, slots // 2, 1)
        mask = lax.dynamic_index_in_dim(mask, c_at, 1, keepdims=False)
        half = (half * mask).reshape(micro, 2, quarter, depth)
        low_parts.append(jnp.where(x_at == 0, half, half[:, ::-1]))
    if ny == 2:
        low_near = [
            jnp.stack([p[0] for p in low_parts], 1),
            jnp.stack([p[1] for p in low_parts], 0),
        ]
        low_near = jnp.stack(low_near).reshape(-1, depth)
    else:
        low_near = jnp.stack(low_parts, 2).reshape(-1, depth)
    low_far = swap(low_near, "c")

    outgate = sum(nn(columns(normed_in, k), w[:, :wide]) for k, w in enumerate(go_parts))
    outgate = outgate.astype(bf16).astype(f32)
    mixed = local_out + jnp.concatenate(
        [nt(far_query[m * slots : (m + 1) * slots], enter[m]) for m in range(micro)]
    )
    r_head = inv_rms(mixed)
    gated = (mixed * r_head * gain_head * silu(outgate)).astype(bf16)
    attention = jnp.concatenate([nt(gated, w[:, wide:]) for w in go_parts], axis=1)
    attention = scatter_head(attention.astype(bf16).reshape(micro, slots, depth))
    inputs_own = to_relative(own_quarter(tokens).reshape(-1, depth)).astype(f32)
    residual = inputs_own + attention.reshape(micro * quarter, depth)

    r_mid = inv_rms(residual)
    normed_mid = to_absolute((residual * r_mid * gain_mid).astype(bf16))
    mid_near, mid_far = gather_plane(normed_mid.reshape(micro, quarter, depth))
    pair_far, hidden_far, part_far = call_feed(mid_far, low_far, ff_full, fl)
    pair_near, hidden_near, part_near = call_feed(mid_near, low_near, ff_full, fl, part_far)
    mid_part = add_low(part_near, swap(part_far, "c"))
    ff_part = call_feed_grad(
        (mid_near, low_near, pair_near, hidden_near),
        (mid_far, low_far, pair_far, hidden_far),
        mid_part,
    )
    ff_grad = reduce_z(ff_part)
    mid_grad = scatter_plane(mid_part, micro, quarter, ff_part).reshape(-1, depth)
    mid_grad = to_relative(mid_grad)

    out_grad = to_relative(own_quarter(out_low).reshape(-1, depth)).astype(f32)
    resid_grad = out_grad + norm_back(residual, r_mid, gain_mid, mid_grad)
    grad_norm_mid = jnp.sum(mid_grad * residual * r_mid, axis=0)
    resid_low = gather_head(resid_grad.astype(bf16).reshape(micro, quarter, depth))
    resid_low = resid_low.reshape(total, depth)
    gated_grad = sum(nn(columns(resid_low, k), w[:, wide:]) for k, w in enumerate(go_parts))

    unit = mixed * r_head
    gate_act = silu(outgate)
    unit_grad = gated_grad * gate_act
    outgate_low = (gated_grad * unit * gain_head * silu_grad(outgate)).astype(bf16)
    mixed_grad = norm_back(mixed, r_head, gain_head, unit_grad).astype(bf16)
    grad_gain = jnp.sum(unit_grad * unit, axis=0)
    state_grad = jnp.stack(
        [
            tn(mixed_grad[m * slots : (m + 1) * slots], far_query[m * slots : (m + 1) * slots])
            for m in range(micro)
        ]
    ).astype(bf16)
    leave = pass_states(state_grad, keep, True)
    hidden_far, hidden_near = after(hidden_far, mixed_grad), after(hidden_near, mixed_grad)

    def feed_part(hidden):
        return nt(hidden, ff_full[:, 2 * fl :]).astype(bf16)

    feed_far = feed_part(hidden_far)
    feed_near = feed_part(hidden_near)
    feed = scatter_plane(add_low(feed_near, swap(feed_far, "c")), micro, quarter).reshape(-1, depth)
    go_grads = [
        jnp.concatenate(
            [tn(columns(normed_in, k), outgate_low), tn(columns(resid_low, k), gated)], axis=1
        ).astype(bf16)
        for k in range(ny)
    ]
    go_rows_grad = sum_y(go_grads)
    go_grad = reduce_z(go_rows_grad)
    qkv_low, logit_grad = call_backward(
        qkv, decays, logits, mixed_grad, enter, leave, is_open, micro, go_rows_grad, feed
    )
    logit_low = logit_grad.astype(bf16)

    qkv_grads = [tn(columns(normed_in, k), qkv_low).astype(bf16) for k in range(ny)]
    qkv_rows_grad = sum_y(qkv_grads)
    qkv_grad = reduce_z(qkv_rows_grad).astype(f32)

    rank_part = nt(logit_low, decay_w).astype(bf16)
    rank_pad = jnp.pad(rank_part, ((0, 0), (0, 128 - rank)))
    qkv_later = after(qkv_low, *qkv_grads)
    in_part = [
        (nt(qkv_later, wq) + nt(outgate_low, wg[:, :wide])).astype(bf16)
        for wq, wg in zip(qkv_parts, go_parts)
    ]
    in_sum = jnp.concatenate(in_part + [rank_pad], axis=1)
    in_sum = scatter_head(in_sum.reshape(micro, slots, depth + 128)).reshape(-1, depth + 128)
    rank_low = in_sum[:, depth : depth + rank].astype(bf16)
    in_grad = in_sum[:, :depth] + nn(rank_low, rank_t)
    r_own = inv_rms(inputs_own)
    input_own = resid_grad + norm_back(inputs_own, r_own, gain_in, in_grad)
    grad_norm_in = jnp.sum(in_grad * inputs_own * r_own, axis=0)
    normed_own = own_quarter(normed_in.reshape(micro, slots, depth)).reshape(-1, depth)
    grad_rank_t = tn(rank_low, normed_own)
    grad_rows = jnp.concatenate([grad_norm_in[None], grad_norm_mid[None], grad_rank_t])
    input_own = to_absolute(input_own.astype(bf16))
    input_grad = gather_head(input_own.reshape(micro, quarter, depth)).astype(f32)

    block_own = (to_absolute(residual) + feed).astype(bf16).reshape(micro, quarter, depth)
    block_out = gather_head(block_own)

    grad_decay = tn(low_rank, logit_low)
    grad_bias = jnp.sum(logit_low.astype(f32), axis=0)
    by_ctx = lambda v: v.reshape(nctx, -1)
    across = lambda v, n: v.reshape(v.shape[0], nctx, n).transpose(1, 0, 2).reshape(nctx, -1)
    summed = jnp.concatenate(
        [vector_by_ctx(grad_rows).reshape(nctx, -1), by_ctx(grad_gain)], axis=1
    )
    headed = jnp.concatenate([across(grad_decay, dl), by_ctx(grad_bias)], axis=1)
    n_summed, n_headed = summed.shape[1], headed.shape[1]
    pad_s, pad_h = -n_summed % 1024, -n_headed % 1024
    tail = jnp.concatenate(
        [jnp.pad(summed, ((0, 0), (0, pad_s))), jnp.pad(headed, ((0, 0), (0, pad_h)))], axis=1
    ).reshape(nctx, -1, 128)
    tail = jnp.sum(lax.all_to_all(tail, ctx, 0, 0), axis=0)
    cut = (n_summed + pad_s) // 128
    summed, headed = tail[:cut], tail[cut:].reshape(-1)
    summed = summed + swap(summed, "c")
    summed = (summed + swap(summed, "x")).reshape(-1)
    g_norm_in = summed[:rl]
    g_norm_mid = summed[rl : 2 * rl]
    g_rank = summed[2 * rl : (2 + rank) * rl].reshape(rank, rl).T
    g_gain = summed[(2 + rank) * rl : n_summed]
    g_decay = headed[: rank * dl].reshape(1, rank, dl)
    g_bias = headed[rank * dl : n_headed].reshape(1, dl)

    ff_grad = after(ff_grad, qkv_rows_grad)
    ff_grad = ff_grad.reshape(ny, rl, 3 * fl)
    pieces = jnp.zeros((ny, rl, 3 * fl), bf16)
    pieces = lax.dynamic_update_slice_in_dim(
        pieces, lax.dynamic_index_in_dim(ff_grad, y, 0), y, 0
    )
    for k in range(1, ny):
        sent = lax.dynamic_index_in_dim(ff_grad, lax.rem(y + k, ny), 0)
        got = lax.ppermute(sent, "y", [(i, (i + k) % ny) for i in range(ny)])
        pieces = lax.dynamic_update_slice_in_dim(pieces, got, lax.rem(y - k + ny, ny), 0)

    g_gate, g_up, g_down = call_join(pieces)
    return (
        block_out,
        input_grad,
        g_norm_in,
        qkv_grad[:, :width],
        qkv_grad[:, width : 2 * width],
        qkv_grad[:, 2 * width :],
        go_grad[:, :wide].astype(f32),
        g_rank,
        g_decay,
        g_bias,
        g_gain,
        go_grad[:, wide:].T.astype(f32),
        g_norm_mid,
        g_gate,
        g_up,
        g_down,
    )


def solution(mesh):
    ctx = mesh.shape["ctx"]
    shape = (NZ, ctx // NZ, 2, mesh.shape["head"] // 2)
    fine = Mesh(mesh.devices.reshape(shape), ("z", "y", "x", "c"))
    c, h = ("z", "y"), ("x", "c")
    in_specs = (
        P(None, c, None), P(None, c, None), P(), P(c), P(c, h), P(c, h), P(c, h), P(c, h), P(c, None),
        P(h, None, c), P(h, c), P(c), P(h, c), P(c), P(c, h), P(c, h), P(h, c),
    )
    out_specs = (
        P(None, c, None), P(None, c, None), P(c), P(c, h), P(c, h), P(c, h), P(c, h), P(c, None),
        P(h, None, c), P(h, c), P(c), P(h, c), P(c), P(c, h), P(c, h), P(h, c),
    )
    return jax.shard_map(
        per_device, mesh=fine, in_specs=in_specs, out_specs=out_specs, check_vma=False
    )
```

```python
import functools

import numpy as np

import jax
import jax.numpy as jnp
from jax import lax
from jax.experimental import pallas as pl
from jax.experimental.pallas import tpu as pltpu
from jax.sharding import Mesh
from jax.sharding import PartitionSpec as P

GROUP = 64
EPS = 1e-06
LEVELS = (32, 16, 8, 4, 2, 1)
f32 = jnp.float32
bf16 = jnp.bfloat16
NZ = 4


def dot(a, b, dims):
    return lax.dot_general(a, b, (dims, ((), ())), preferred_element_type=f32)


def nn(a, b):
    return dot(a, b, ((1,), (0,)))


def nt(a, b):
    return dot(a, b, ((1,), (1,)))


def tn(a, b):
    return dot(a, b, ((0,), (0,)))


def swap(x, axis):
    return lax.ppermute(x, axis, [(0, 1), (1, 0)])


def after(value, *earlier):
    anywhere = pl.BlockSpec(memory_space=pl.ANY)
    return pl.pallas_call(
        lambda *refs: None,
        in_specs=[anywhere] * (1 + len(earlier)),
        out_specs=anywhere,
        out_shape=jax.ShapeDtypeStruct(value.shape, value.dtype),
        input_output_aliases={0: 0},
        cost_estimate=pl.CostEstimate(flops=0, bytes_accessed=0, transcendentals=0),
        name="after",
    )(value, *earlier)


def as_one(runs, work):
    shapes = jax.eval_shape(work)
    return lax.cond(
        runs, work, lambda: jax.tree.map(lambda s: jnp.zeros(s.shape, s.dtype), shapes)
    )


def add_low(a, b):
    return (a.astype(f32) + b.astype(f32)).astype(bf16)


def both_in_order(piece, axis, dim):
    other = swap(piece, axis)
    first = lax.axis_index(axis) == 0
    return jnp.where(
        first, jnp.stack([piece, other], dim), jnp.stack([other, piece], dim)
    )


def silu(v):
    return v * jax.nn.sigmoid(v)


def silu_grad(v):
    sig = jax.nn.sigmoid(v)
    return sig * (1.0 + v * (1.0 - sig))


def inv_rms(v):
    return lax.rsqrt(jnp.mean(v * v, axis=-1, keepdims=True) + EPS)


def norm_back(h, r, gain, grad):
    scaled = gain * grad
    inner = jnp.mean(h * scaled, axis=-1, keepdims=True)
    return r * scaled - h * (r * r * r) * inner


def level_map(rows):
    t = np.arange(rows)[:, None]
    u = np.arange(rows)[None, :]
    out = np.zeros((rows, rows), np.int32)
    for at, half in enumerate(LEVELS):
        hit = (t // (2 * half) == u // (2 * half)) & ((t // half) % 2 == 1) & ((u // half) % 2 == 0)
        out[hit] = at + 1
    out[t == u] = len(LEVELS) + 1
    return out


def lower_map(rows):
    t = np.arange(rows)[:, None]
    u = np.arange(rows)[None, :]
    return ((t // GROUP == u // GROUP) & (t >= u)).astype(np.float32)


def ones_times(ones, value):
    hi = value.astype(bf16)
    rest = value - hi.astype(f32)
    mid = rest.astype(bf16)
    low = (rest - mid.astype(f32)).astype(bf16)
    return nn(ones, hi) + (nn(ones, mid) + nn(ones, low))


def level_decay(cum, half):
    rows, width = cum.shape
    span = max(2 * half, 8)
    parts = cum.reshape(rows // span, span, width)
    if half >= 4:
        mid = parts[:, half - 1 : half, :]
    else:
        at = lax.broadcasted_iota(jnp.int32, parts.shape, 1)
        mid = parts[:, half - 1 : half, :]
        for start in range(2 * half, span, 2 * half):
            mid = jnp.where(at >= start, parts[:, start + half - 1 : start + half, :], mid)
    return jnp.exp(-jnp.abs(parts - mid)).reshape(rows, width)


def block_of(array, at):
    return array[at * GROUP : (at + 1) * GROUP, :]


def scan_forward(qkv_ref, decay_ref, lower_ref, level_ref, open_ref, out_ref, query_ref, state_ref, keep_ref):
    step = pl.program_id(0)
    rows, width = decay_ref.shape
    count = rows // GROUP
    scale = width**-0.5
    queries = qkv_ref[:, :width].astype(f32) * scale
    keys = qkv_ref[:, width : 2 * width].astype(f32)
    values = qkv_ref[:, 2 * width :]
    levels = level_ref[...]
    cum = ones_times(lower_ref[...], decay_ref[...])
    scores = jnp.where(
        levels == len(LEVELS) + 1, nt(queries.astype(bf16), keys.astype(bf16)), 0.0
    )
    for at, half in enumerate(LEVELS):
        decay = level_decay(cum, half)
        part = nt((queries * decay).astype(bf16), (keys * decay).astype(bf16))
        scores = jnp.where(levels == at + 1, part, scores)
    local = nn(scores.astype(bf16), values)
    faded = queries * jnp.exp(cum)
    state = jnp.zeros((values.shape[1], width), f32)
    keep = jnp.ones((1, width), f32)
    for c in range(count):
        is_open = open_ref[step, c]
        state = state * is_open
        keep = keep * is_open
        faded_c = block_of(faded, c)
        cum_c = block_of(cum, c)
        last = cum_c[GROUP - 1 :, :]
        here = block_of(local, c)
        if c:
            here = here + nt(faded_c.astype(bf16), state.astype(bf16))
        out_ref[c * GROUP : (c + 1) * GROUP, :] = here
        query_ref[c * GROUP : (c + 1) * GROUP, :] = (faded_c * keep).astype(bf16)
        carried = (block_of(keys, c) * jnp.exp(last - cum_c)).astype(bf16)
        update = tn(block_of(values, c), carried)
        shrink = jnp.exp(last)
        state = state * shrink + update
        keep = keep * shrink
    state_ref[0] = state.astype(bf16)
    keep_ref[0] = jnp.broadcast_to(keep, keep_ref.shape[1:])


def scan_backward(qkv_ref, decay_ref, logit_ref, grad_ref, enter_ref, leave_ref, lower_ref, upper_ref, level_ref, open_ref, *rest):
    out_ref, logit_out_ref, local_ref, past_ref = rest[-4:]
    step = pl.program_id(0)
    rows, width = decay_ref.shape
    count = rows // GROUP
    scale = width**-0.5
    queries = qkv_ref[:, :width].astype(f32) * scale
    keys = qkv_ref[:, width : 2 * width].astype(f32)
    values = qkv_ref[:, 2 * width :]
    grads = grad_ref[...]
    levels = level_ref[...]
    cum = ones_times(lower_ref[...], decay_ref[...])
    pair_grad = nt(grads, values)
    on_diagonal = levels == len(LEVELS) + 1
    own = jnp.sum(jnp.where(on_diagonal, pair_grad, 0.0), axis=1, keepdims=True)
    scores = jnp.where(on_diagonal, nt(queries.astype(bf16), keys.astype(bf16)), 0.0)
    query_grad = jnp.zeros((rows, width), f32)
    key_grad = jnp.zeros((rows, width), f32)
    for at, half in enumerate(LEVELS):
        decay = level_decay(cum, half)
        query_l = (queries * decay).astype(bf16)
        key_l = (keys * decay).astype(bf16)
        hit = levels == at + 1
        scores = jnp.where(hit, nt(query_l, key_l), scores)
        grad_l = jnp.where(hit, pair_grad, 0.0).astype(bf16)
        query_grad = query_grad + nn(grad_l, key_l) * decay
        key_grad = key_grad + tn(grad_l, query_l) * decay
    value_grad = tn(scores.astype(bf16), grads)
    rising = jnp.exp(cum)
    faded = queries * rising
    state = enter_ref[0].astype(f32)
    for c in range(count):
        state = state * open_ref[step, c]
        past_ref[c] = state
        cum_c = block_of(cum, c)
        last = cum_c[GROUP - 1 :, :]
        if c < count - 1:
            carried = (block_of(keys, c) * jnp.exp(last - cum_c)).astype(bf16)
            state = state * jnp.exp(last) + tn(block_of(values, c), carried)
    after = leave_ref[0].astype(f32)
    for c in range(count - 1, -1, -1):
        span = slice(c * GROUP, (c + 1) * GROUP)
        past = past_ref[c]
        cum_c = block_of(cum, c)
        last = cum_c[GROUP - 1 :, :]
        shrink = jnp.exp(last)
        fading = jnp.exp(last - cum_c)
        keys_c = block_of(keys, c)
        queries_c = block_of(queries, c)
        grads_c = block_of(grads, c)
        after_low = after.astype(bf16)
        query_c = block_of(query_grad, c) + nn(grads_c, past.astype(bf16)) * block_of(rising, c)
        key_far = nn(block_of(values, c), after_low) * fading
        key_c = block_of(key_grad, c) + key_far
        value_c = block_of(value_grad, c) + nt((keys_c * fading).astype(bf16), after_low)
        own_c = block_of(own, c)
        out_ref[span, :width] = ((query_c + own_c * keys_c) * scale).astype(bf16)
        out_ref[span, width : 2 * width] = (key_c + own_c * queries_c).astype(bf16)
        out_ref[span, 2 * width :] = value_c.astype(bf16)
        local_ref[span, :] = queries_c * query_c - keys_c * key_c
        at_last = jnp.sum(keys_c * key_far, axis=0, keepdims=True) + shrink * jnp.sum(
            past * after, axis=0, keepdims=True
        )
        logit_out_ref[span, :] = jnp.broadcast_to(at_last, (GROUP, width))
        if c:
            after = (after * shrink + tn(grads_c, block_of(faded, c).astype(bf16))) * open_ref[step, c]
    decay_grad = ones_times(upper_ref[...], local_ref[...]) + logit_out_ref[...]
    logit_out_ref[...] = decay_grad * jax.nn.sigmoid(-logit_ref[...]) * (1.0 / 16.0)


def call_forward(qkv, decays, is_open, micro_count):
    rows = qkv.shape[0] // micro_count
    width = decays.shape[1]
    wide = qkv.shape[1] - 2 * width
    lower = jnp.asarray(lower_map(rows), bf16)
    level = jnp.asarray(level_map(rows))
    whole = lambda m: (0, 0)
    mine = lambda m: (m, 0)
    mine3 = lambda m: (m, 0, 0)
    return pl.pallas_call(
        scan_forward,
        grid=(micro_count,),
        in_specs=[
            pl.BlockSpec((rows, qkv.shape[1]), mine),
            pl.BlockSpec((rows, width), mine),
            pl.BlockSpec((rows, rows), whole),
            pl.BlockSpec((rows, rows), whole),
            pl.BlockSpec(memory_space=pltpu.SMEM),
        ],
        out_specs=[
            pl.BlockSpec((rows, wide), mine),
            pl.BlockSpec((rows, width), mine),
            pl.BlockSpec((1, wide, width), mine3),
            pl.BlockSpec((1, 8, width), mine3),
        ],
        out_shape=[
            jax.ShapeDtypeStruct((micro_count * rows, wide), f32),
            jax.ShapeDtypeStruct((micro_count * rows, width), bf16),
            jax.ShapeDtypeStruct((micro_count, wide, width), bf16),
            jax.ShapeDtypeStruct((micro_count, 8, width), f32),
        ],
        compiler_params=pltpu.CompilerParams(vmem_limit_bytes=40 * 2**20),
        cost_estimate=pl.CostEstimate(flops=2_000_000_000, bytes_accessed=8_000_000, transcendentals=1_500_000),
        name="scan_forward",
    )(qkv, decays, lower, level, is_open)


def call_backward(qkv, decays, logits, grads, enter, leave, is_open, micro_count, *earlier):
    rows = qkv.shape[0] // micro_count
    width = decays.shape[1]
    wide = qkv.shape[1] - 2 * width
    lower = jnp.asarray(lower_map(rows), bf16)
    upper = jnp.asarray(lower_map(rows).T, bf16)
    level = jnp.asarray(level_map(rows))
    whole = lambda m: (0, 0)
    mine = lambda m: (m, 0)
    mine3 = lambda m: (m, 0, 0)
    return pl.pallas_call(
        scan_backward,
        grid=(micro_count,),
        in_specs=[
            pl.BlockSpec((rows, qkv.shape[1]), mine),
            pl.BlockSpec((rows, width), mine),
            pl.BlockSpec((rows, width), mine),
            pl.BlockSpec((rows, wide), mine),
            pl.BlockSpec((1, wide, width), mine3),
            pl.BlockSpec((1, wide, width), mine3),
            pl.BlockSpec((rows, rows), whole),
            pl.BlockSpec((rows, rows), whole),
            pl.BlockSpec((rows, rows), whole),
            pl.BlockSpec(memory_space=pltpu.SMEM),
        ]
        + [pl.BlockSpec(memory_space=pl.ANY)] * len(earlier),
        out_specs=[
            pl.BlockSpec((rows, qkv.shape[1]), mine),
            pl.BlockSpec((rows, width), mine),
        ],
        out_shape=[
            jax.ShapeDtypeStruct((micro_count * rows, qkv.shape[1]), bf16),
            jax.ShapeDtypeStruct((micro_count * rows, width), f32),
        ],
        scratch_shapes=[
            pltpu.VMEM((rows, width), f32),
            pltpu.VMEM((rows // GROUP, wide, width), f32),
        ],
        compiler_params=pltpu.CompilerParams(vmem_limit_bytes=40 * 2**20),
        cost_estimate=pl.CostEstimate(flops=5_000_000_000, bytes_accessed=12_000_000, transcendentals=1_500_000),
        name="scan_backward",
    )(qkv, decays, logits, grads, enter, leave, lower, upper, level, is_open, *earlier)


def scan_states(got_ref, out_ref, *, micro, strip, reverse):
    count = got_ref.shape[0]
    width = got_ref.shape[2]
    running = [jnp.zeros((strip, width), f32) for _ in range(micro)]
    order = range(count - 1, -1, -1) if reverse else range(count)
    for at in order:
        tail = got_ref[at, micro * strip :, :].astype(f32)
        for m in range(micro):
            span = slice(m * strip, (m + 1) * strip)
            out_ref[at, span, :] = running[m].astype(bf16)
            keep = tail[m : m + 1, :] + tail[micro + m : micro + m + 1, :]
            running[m] = running[m] * keep + got_ref[at, span, :].astype(f32)


def spread_states(state, keep, reverse):
    ctx = ("z", "y")
    count = lax.axis_size(ctx)
    micro, wide, width = state.shape
    strip = wide // count
    parts = state.reshape(micro, count, strip, width).transpose(1, 0, 2, 3)
    parts = parts.reshape(count, micro * strip, width)
    keep_hi = keep.astype(bf16)
    keep_lo = (keep - keep_hi.astype(f32)).astype(bf16)
    extra = jnp.concatenate([keep_hi, keep_lo, jnp.zeros((16 - 2 * micro, width), bf16)])
    sent = jnp.concatenate(
        [parts, jnp.broadcast_to(extra[None], (count, 16, width))], axis=1
    )
    got = lax.all_to_all(sent, ctx, 0, 0)
    return pl.pallas_call(
        functools.partial(scan_states, micro=micro, strip=strip, reverse=reverse),
        out_shape=jax.ShapeDtypeStruct((count, micro * strip, width), bf16),
        compiler_params=pltpu.CompilerParams(vmem_limit_bytes=16 * 2**20),
        cost_estimate=pl.CostEstimate(flops=2_000_000, bytes_accessed=1_100_000, transcendentals=0),
        name="scan_states",
    )(got)


def collect_states(entering, micro):
    count, _, width = entering.shape
    strip = entering.shape[1] // micro
    back = lax.all_to_all(entering, ("z", "y"), 0, 0)
    return back.reshape(count, micro, strip, width).transpose(1, 0, 2, 3).reshape(micro, -1, width)


def feed_kernel(mid_ref, low_ref, weight_ref, *rest, units):
    pair_ref, hidden_ref, grad_ref = rest[-3:]
    both = nn(mid_ref[...], weight_ref[:, : 2 * units])
    gate, up = both[:, :units], both[:, units:]
    back = nn(low_ref[...], weight_ref[:, 2 * units :])
    sig = jax.nn.sigmoid(gate)
    act = gate * sig
    hidden_ref[...] = (act * up).astype(bf16)
    pair_ref[:, :units] = (back * up * (sig * (1.0 + gate * (1.0 - sig)))).astype(bf16)
    pair_ref[:, units:] = (back * act).astype(bf16)
    grad_ref[...] = nt(pair_ref[...], weight_ref[:, : 2 * units]).astype(bf16)


def call_feed(plane_mid, plane_low, weight, units, *earlier):
    rows, depth = plane_mid.shape
    tile = 256
    return pl.pallas_call(
        functools.partial(feed_kernel, units=units),
        grid=(rows // tile,),
        in_specs=[
            pl.BlockSpec((tile, depth), lambda i: (i, 0)),
            pl.BlockSpec((tile, depth), lambda i: (i, 0)),
            pl.BlockSpec(weight.shape, lambda i: (0, 0), pipeline_mode=pl.Buffered(1)),
        ]
        + [pl.BlockSpec(memory_space=pl.ANY)] * len(earlier),
        out_specs=[
            pl.BlockSpec((tile, 2 * units), lambda i: (i, 0)),
            pl.BlockSpec((tile, units), lambda i: (i, 0)),
            pl.BlockSpec((tile, depth), lambda i: (i, 0)),
        ],
        out_shape=[
            jax.ShapeDtypeStruct((rows, 2 * units), bf16),
            jax.ShapeDtypeStruct((rows, units), bf16),
            jax.ShapeDtypeStruct((rows, depth), bf16),
        ],
        compiler_params=pltpu.CompilerParams(vmem_limit_bytes=48 * 2**20),
        cost_estimate=pl.CostEstimate(
            flops=10 * rows * depth * units, bytes_accessed=28_000_000, transcendentals=rows * units
        ),
        name="feed_forward",
    )(plane_mid, plane_low, weight, *earlier)


def split_units(gate_ref, up_ref, down_ref, out_ref):
    parts, rows, width = out_ref.shape
    units = width // 3
    for k in range(parts):
        span = slice(k * units, (k + 1) * units)
        out_ref[k, :, :units] = gate_ref[:, span]
        out_ref[k, :, units : 2 * units] = up_ref[:, span]
        out_ref[k, :, 2 * units :] = down_ref[span, :].astype(f32).T.astype(bf16)


def call_split(w_gate, w_up, w_down, parts):
    rows, ff = w_gate.shape
    return pl.pallas_call(
        split_units,
        out_shape=jax.ShapeDtypeStruct((parts, rows, 3 * ff // parts), bf16),
        compiler_params=pltpu.CompilerParams(vmem_limit_bytes=32 * 2**20),
        cost_estimate=pl.CostEstimate(flops=0, bytes_accessed=12 * rows * ff, transcendentals=0),
        name="split_units",
    )(w_gate, w_up, w_down)


def join_units(in_ref, gate_ref, up_ref, down_ref):
    parts, rows, width = in_ref.shape
    units = width // 3
    for k in range(parts):
        span = slice(k * units, (k + 1) * units)
        gate_ref[:, span] = in_ref[k, :, :units].astype(f32)
        up_ref[:, span] = in_ref[k, :, units : 2 * units].astype(f32)
        down_ref[span, :] = in_ref[k, :, 2 * units :].astype(f32).T


def call_join(pieces):
    parts, rows, width = pieces.shape
    ff = width // 3 * parts
    return pl.pallas_call(
        join_units,
        out_shape=[
            jax.ShapeDtypeStruct((rows, ff), f32),
            jax.ShapeDtypeStruct((rows, ff), f32),
            jax.ShapeDtypeStruct((ff, rows), f32),
        ],
        compiler_params=pltpu.CompilerParams(vmem_limit_bytes=32 * 2**20),
        cost_estimate=pl.CostEstimate(flops=0, bytes_accessed=18 * rows * ff, transcendentals=0),
        name="join_units",
    )(pieces)


def feed_grad_kernel(*refs):
    out_ref = refs[-1]
    two = refs[2].shape[1]
    mid_a, low_a, pair_a, hidden_a, mid_b, low_b, pair_b, hidden_b = (r[...] for r in refs[:8])
    out_ref[:, :two] = (tn(mid_a, pair_a) + tn(mid_b, pair_b)).astype(bf16)
    out_ref[:, two:] = (tn(low_a, hidden_a) + tn(low_b, hidden_b)).astype(bf16)


def call_feed_grad(near, far, *earlier):
    rows, depth = near[0].shape
    two, units = near[2].shape[1], near[3].shape[1]
    tile = 256
    one = [
        pl.BlockSpec((rows, tile), lambda i: (0, i)),
        pl.BlockSpec((rows, tile), lambda i: (0, i)),
        pl.BlockSpec((rows, two), lambda i: (0, 0), pipeline_mode=pl.Buffered(1)),
        pl.BlockSpec((rows, units), lambda i: (0, 0), pipeline_mode=pl.Buffered(1)),
    ]
    return pl.pallas_call(
        feed_grad_kernel,
        grid=(depth // tile,),
        in_specs=one + one + [pl.BlockSpec(memory_space=pl.ANY)] * len(earlier),
        out_specs=pl.BlockSpec((tile, two + units), lambda i: (i, 0)),
        out_shape=jax.ShapeDtypeStruct((depth, two + units), bf16),
        compiler_params=pltpu.CompilerParams(vmem_limit_bytes=48 * 2**20),
        cost_estimate=pl.CostEstimate(
            flops=4 * rows * depth * (two + units), bytes_accessed=21_000_000, transcendentals=0
        ),
        name="feed_grad",
    )(*near, *far, *earlier)


def gather_plane(piece):
    count = lax.axis_size("y")
    if count == 2:
        a, b = piece[0], piece[1]
        a_y, b_x = swap(a, "y"), swap(b, "x")
        a, b = jnp.stack([a, a_y]), jnp.stack([b, b_x])
        a_x, b_y = swap(a, "x"), swap(b, "y")
        here = jnp.concatenate([a, a_x, b, b_y])
    else:
        rows = [piece]
        for k in range(1, count):
            rows.append(lax.ppermute(piece, "y", [((i + k) % count, i) for i in range(count)]))
        here = jnp.stack(rows, axis=1)
        here = jnp.stack([here, swap(here, "x")], axis=1)
        here = here.reshape((-1,) + piece.shape[1:])
    here = here.reshape(-1, piece.shape[-1])
    return here, swap(here, "c")


def scatter_first(here, micro, quarter):
    count = lax.axis_size("y")
    depth = here.shape[-1]
    if count == 2:
        here = here.reshape(2, 2, 2 * quarter, depth)
        a, b = here[0], here[1]
        a_got, b_got = swap(a[1], "x"), swap(b[1], "y")
        return add_low(a[0], a_got), add_low(b[0], b_got)
    here = here.reshape(micro, 2, count, quarter, depth)
    here = add_low(here[:, 0], swap(here[:, 1], "x"))
    return here[:, :1], here[:, 1:]


def scatter_second(a, b, quarter):
    count = lax.axis_size("y")
    if count == 2:
        a, b = (v.reshape(2, quarter, -1) for v in (a, b))
        a_got, b_got = swap(a[1], "y"), swap(b[1], "x")
        a = a[0].astype(f32) + a_got.astype(f32)
        b = b[0].astype(f32) + b_got.astype(f32)
        return jnp.stack([a, b])
    total = a[:, 0].astype(f32)
    for k in range(1, count):
        got = lax.ppermute(b[:, k - 1], "y", [(i, (i + k) % count) for i in range(count)])
        total = total + got.astype(f32)
    return total


def scatter_head(part):
    micro, slots, width = part.shape
    c, x = lax.axis_index("c"), lax.axis_index("x")
    view = part.reshape(micro, 2, slots // 2, width)
    mine = lax.dynamic_index_in_dim(view, c, 1, keepdims=False)
    other = lax.dynamic_index_in_dim(view, 1 - c, 1, keepdims=False)
    mine = add_low(mine, swap(other, "c"))
    view = mine.reshape(micro, 2, slots // 4, width)
    mine = lax.dynamic_index_in_dim(view, x, 1, keepdims=False)
    other = lax.dynamic_index_in_dim(view, 1 - x, 1, keepdims=False)
    return mine.astype(f32) + swap(other, "x").astype(f32)


def gather_head(piece):
    micro, quarter, width = piece.shape
    both = both_in_order(piece, "x", 1)
    both = both_in_order(both, "c", 1)
    return both.reshape(micro, 4 * quarter, width)


def own_quarter(array):
    micro, slots, width = array.shape
    c, x = lax.axis_index("c"), lax.axis_index("x")
    view = array.reshape(micro, 4, slots // 4, width)
    return lax.dynamic_index_in_dim(view, 2 * c + x, 1, keepdims=False)


def others_y(piece):
    count = lax.axis_size("y")
    out = [piece]
    for k in range(1, count):
        out.append(lax.ppermute(piece, "y", [((i + k) % count, i) for i in range(count)]))
    return out


def to_relative(array):
    count, y = lax.axis_size("y"), lax.axis_index("y")
    t, depth = array.shape
    rl = depth // (NZ * count)
    if count == 2:
        even = jnp.concatenate([array[:, 2 * z * rl : (2 * z + 1) * rl] for z in range(NZ)], axis=1)
        odd = jnp.concatenate([array[:, (2 * z + 1) * rl : (2 * z + 2) * rl] for z in range(NZ)], axis=1)
        first = y == 0
        return jnp.concatenate([jnp.where(first, even, odd), jnp.where(first, odd, even)], axis=1)
    view = jnp.roll(array.reshape(t, NZ, count, rl), -y, axis=2)
    return view.transpose(0, 2, 1, 3).reshape(t, depth)


def to_absolute(array):
    count, y = lax.axis_size("y"), lax.axis_index("y")
    t, depth = array.shape
    rl = depth // (NZ * count)
    if count == 2:
        first = y == 0
        out = []
        for z in range(NZ):
            own = array[:, z * rl : (z + 1) * rl]
            other = array[:, (NZ + z) * rl : (NZ + z + 1) * rl]
            out += [jnp.where(first, own, other), jnp.where(first, other, own)]
        return jnp.concatenate(out, axis=1)
    view = array.reshape(t, count, NZ, rl).transpose(0, 2, 1, 3)
    return jnp.roll(view, y, axis=2).reshape(t, depth)


def vector_by_ctx(value):
    count, y = lax.axis_size("y"), lax.axis_index("y")
    view = value.reshape(value.shape[0], count, NZ, -1)
    if count == 2:
        view = jnp.where(y == 0, view, view[:, ::-1])
    else:
        view = jnp.roll(view, y, axis=1)
    return view.transpose(2, 1, 0, 3).reshape(NZ * count, value.shape[0], -1)


def vector_from_ctx(value):
    count, y = lax.axis_size("y"), lax.axis_index("y")
    view = value.reshape((NZ, count) + value.shape[1:]).transpose(2, 1, 0, 3)
    if count == 2:
        view = jnp.where(y == 0, view, view[:, ::-1])
    else:
        view = jnp.roll(view, -y, axis=1)
    return view.reshape(value.shape[1], -1)


def sum_y(parts, *between):
    count = lax.axis_size("y")
    total = (after(parts[0], *between) if between else parts[0]).astype(f32)
    for k in range(1, count):
        got = lax.ppermute(parts[k], "y", [(i, (i + k) % count) for i in range(count)])
        total = total + got.astype(f32)
    return total.astype(bf16)


def reduce_z(part):
    return lax.psum_scatter(part, "z", scatter_dimension=0, tiled=True)


def per_device(
    tokens, cotangent, lengths, norm_in, w_query, w_key, w_value, w_outgate, w_rank,
    w_decay, decay_bias, head_gain, w_out, norm_mid, w_gate, w_up, w_down,
):
    ctx = ("z", "y")
    ny = lax.axis_size("y")
    nctx = NZ * ny
    y = lax.axis_index("y")
    place = lax.axis_index(ctx)
    micro, slots, depth = tokens.shape
    groups = slots // GROUP
    rl = w_query.shape[0]
    width = w_query.shape[1]
    wide = w_value.shape[1]
    rank = w_rank.shape[1]
    ff = w_gate.shape[1]
    fl = ff // ny
    total = micro * slots

    w_qkv = jnp.concatenate([w_query, w_key, w_value], axis=1)
    qkv_rows = lax.all_gather(w_qkv, "z", axis=0, tiled=True)
    w_go = jnp.concatenate([w_outgate, w_out.T], axis=1)
    go_rows = lax.all_gather(w_go, "z", axis=0, tiled=True)

    small = jnp.concatenate(
        [norm_in, norm_mid, w_rank.T.reshape(-1), w_decay[0].reshape(-1), decay_bias[0], head_gain]
    )
    n_small = small.shape[0]
    pad = -n_small % 1024
    small = jnp.pad(small, (0, pad)).reshape(1, -1, 128)
    small = jnp.broadcast_to(small, (nctx,) + small.shape[1:])
    small = lax.all_to_all(small, ctx, 0, 0).reshape(nctx, -1)
    at = 0

    def take(size):
        nonlocal at
        at += size
        return small[:, at - size : at]

    by_row = vector_from_ctx(take((2 + rank) * rl).reshape(nctx, 2 + rank, rl))
    gain_in = by_row[:1].astype(f32)
    gain_mid = by_row[1:2].astype(f32)
    rank_t = by_row[2:]
    dl = width // nctx
    decay_w = take(rank * dl).reshape(nctx, rank, dl).transpose(1, 0, 2).reshape(rank, width)
    bias = take(dl).reshape(1, width).astype(f32)
    gain_head = take(wide // nctx).reshape(1, wide).astype(f32)

    ff_local = call_split(w_gate, w_up, w_down, ny)
    own = lax.dynamic_index_in_dim(ff_local, y, 0, keepdims=False)
    if ny == 2:
        got = swap(lax.dynamic_index_in_dim(ff_local, 1 - y, 0, keepdims=False), "y")
        ff_unit = jnp.where(y == 0, jnp.stack([own, got]), jnp.stack([got, own]))
    else:
        pieces = [own]
        for k in range(1, ny):
            sent = lax.dynamic_index_in_dim(ff_local, lax.rem(y + ny - k, ny), 0, keepdims=False)
            pieces.append(lax.ppermute(sent, "y", [((i + k) % ny, i) for i in range(ny)]))
        ff_unit = jnp.roll(jnp.stack(pieces), y, axis=0)
    ff_unit = ff_unit.reshape(ny * rl, 3 * fl)

    group_ids = place * groups + jnp.arange(groups, dtype=jnp.int32)
    end = jnp.zeros((micro, 1), jnp.int32)
    reset = group_ids[None, :] == end
    for i in range(lengths.shape[1]):
        end = end + lengths[:, i : i + 1]
        reset = reset | (group_ids[None, :] == end)
    is_open = 1.0 - reset.astype(f32)

    def mask_of(at):
        slot_ids = at * slots + jnp.arange(slots, dtype=jnp.int32)
        return (slot_ids[None, :] < end * GROUP).astype(bf16)[:, :, None]

    c_at, x_at = lax.axis_index("c"), lax.axis_index("x")
    quarter = slots // 4
    view = cotangent.reshape(micro, 2, slots // 2, depth)
    half_parts = others_y(lax.dynamic_index_in_dim(view, c_at, 1, keepdims=False))

    ff_full = lax.all_gather(ff_unit, "z", axis=0, tiled=True)
    qkv_parts = others_y(qkv_rows)
    go_parts = others_y(go_rows)

    inputs = to_relative(tokens.reshape(total, depth)).astype(f32)
    r_in = inv_rms(inputs)
    normed_in = (inputs * r_in * gain_in).astype(bf16)
    step = depth // ny
    low_rank = nt(normed_in, rank_t).astype(bf16)
    logits = nn(low_rank, decay_w) + bias
    decays = jax.nn.log_sigmoid(logits) / 16.0

    def columns(array, k):
        return array[:, k * step : (k + 1) * step]

    qkv = sum(nn(columns(normed_in, k), w) for k, w in enumerate(qkv_parts)).astype(bf16)

    runs = lengths[0, 0] >= 1

    def recurrence():
        local_out, far_query, state, keep = call_forward(qkv, decays, is_open, micro)
        keep = keep[:, 0, :]
        return local_out, far_query, collect_states(spread_states(state, keep, False), micro), keep

    local_out, far_query, enter, keep = as_one(runs, recurrence)

    out_low = cotangent * mask_of(place)
    low_parts = []
    for k, half in enumerate(half_parts):
        mask = mask_of(place - y + lax.rem(y + k, ny)).reshape(micro, 2, slots // 2, 1)
        mask = lax.dynamic_index_in_dim(mask, c_at, 1, keepdims=False)
        half = (half * mask).reshape(micro, 2, quarter, depth)
        low_parts.append(jnp.where(x_at == 0, half, half[:, ::-1]))
    if ny == 2:
        low_near = [
            jnp.stack([p[0] for p in low_parts], 1),
            jnp.stack([p[1] for p in low_parts], 0),
        ]
        low_near = jnp.stack(low_near).reshape(-1, depth)
    else:
        low_near = jnp.stack(low_parts, 2).reshape(-1, depth)
    low_far = swap(low_near, "c")

    outgate = sum(nn(columns(normed_in, k), w[:, :wide]) for k, w in enumerate(go_parts))
    outgate = outgate.astype(bf16).astype(f32)
    mixed = local_out + jnp.concatenate(
        [nt(far_query[m * slots : (m + 1) * slots], enter[m]) for m in range(micro)]
    )
    r_head = inv_rms(mixed)
    gated = (mixed * r_head * gain_head * silu(outgate)).astype(bf16)
    attention = jnp.concatenate([nt(gated, w[:, wide:]) for w in go_parts], axis=1)
    attention = scatter_head(attention.astype(bf16).reshape(micro, slots, depth))
    inputs_own = to_relative(own_quarter(tokens).reshape(-1, depth)).astype(f32)
    residual = inputs_own + attention.reshape(micro * quarter, depth)

    r_mid = inv_rms(residual)
    normed_mid = to_absolute((residual * r_mid * gain_mid).astype(bf16))
    mid_near, mid_far = gather_plane(normed_mid.reshape(micro, quarter, depth))
    pair_far, hidden_far, part_far = call_feed(mid_far, low_far, ff_full, fl)
    pair_near, hidden_near, part_near = call_feed(mid_near, low_near, ff_full, fl, part_far)
    mid_part = add_low(part_near, swap(part_far, "c"))
    def feed_back():
        ff_part = call_feed_grad(
            (mid_near, low_near, pair_near, hidden_near),
            (mid_far, low_far, pair_far, hidden_far),
        )
        return ff_part, *scatter_first(mid_part, micro, quarter)

    ff_part, mid_a, mid_b = as_one(runs, feed_back)
    ff_grad = reduce_z(ff_part)

    def feed_part(hidden):
        return nt(hidden, ff_full[:, 2 * fl :]).astype(bf16)

    def blocks_back():
        mid_grad = to_relative(scatter_second(mid_a, mid_b, quarter).reshape(-1, depth))

        out_grad = to_relative(own_quarter(out_low).reshape(-1, depth)).astype(f32)
        resid_grad = out_grad + norm_back(residual, r_mid, gain_mid, mid_grad)
        grad_norm_mid = jnp.sum(mid_grad * residual * r_mid, axis=0)
        resid_low = gather_head(resid_grad.astype(bf16).reshape(micro, quarter, depth))
        resid_low = resid_low.reshape(total, depth)
        gated_grad = sum(nn(columns(resid_low, k), w[:, wide:]) for k, w in enumerate(go_parts))

        unit = mixed * r_head
        gate_act = silu(outgate)
        unit_grad = gated_grad * gate_act
        outgate_low = (gated_grad * unit * gain_head * silu_grad(outgate)).astype(bf16)
        mixed_grad = norm_back(mixed, r_head, gain_head, unit_grad).astype(bf16)
        grad_gain = jnp.sum(unit_grad * unit, axis=0)
        state_grad = jnp.stack(
            [
                tn(mixed_grad[m * slots : (m + 1) * slots], far_query[m * slots : (m + 1) * slots])
                for m in range(micro)
            ]
        ).astype(bf16)
        entering = spread_states(state_grad, keep, True)
        leave = collect_states(entering, micro)
        go_grads = [
            jnp.concatenate(
                [tn(columns(normed_in, k), outgate_low), tn(columns(resid_low, k), gated)], axis=1
            ).astype(bf16)
            for k in range(ny)
        ]
        go_rows_grad = sum_y(go_grads[:1] + [after(g, entering) for g in go_grads[1:]])
        feed_far = swap(feed_part(after(hidden_far, mixed_grad)), "c")
        feed_rows = add_low(feed_part(after(hidden_near, mixed_grad)), feed_far)
        feed = scatter_second(*scatter_first(feed_rows, micro, quarter), quarter)
        qkv_low, logit_grad = call_backward(
            qkv, decays, logits, mixed_grad, enter, leave, is_open, micro
        )
        logit_low = logit_grad.astype(bf16)
        qkv_grads = [tn(columns(normed_in, k), qkv_low).astype(bf16) for k in range(ny)]
        rank_part = nt(logit_low, decay_w).astype(bf16)
        rank_pad = jnp.pad(rank_part, ((0, 0), (0, 128 - rank)))
        qkv_later = after(qkv_low, *qkv_grads)
        in_part = [
            (nt(qkv_later, wq) + nt(outgate_low, wg[:, :wide])).astype(bf16)
            for wq, wg in zip(qkv_parts, go_parts)
        ]
        in_part = jnp.concatenate(in_part + [rank_pad], axis=1).reshape(micro, slots, depth + 128)
        return resid_grad, grad_norm_mid, grad_gain, go_rows_grad, qkv_grads, in_part, logit_low, feed

    resid_grad, grad_norm_mid, grad_gain, go_rows_grad, qkv_grads, in_part, logit_low, feed = as_one(
        runs, blocks_back
    )
    go_grad = reduce_z(go_rows_grad)

    def input_back():
        in_sum = scatter_head(in_part).reshape(-1, depth + 128)
        rank_low = in_sum[:, depth : depth + rank].astype(bf16)
        in_grad = in_sum[:, :depth] + nn(rank_low, rank_t)
        r_own = inv_rms(inputs_own)
        input_own = resid_grad + norm_back(inputs_own, r_own, gain_in, in_grad)
        grad_norm_in = jnp.sum(in_grad * inputs_own * r_own, axis=0)
        normed_own = own_quarter(normed_in.reshape(micro, slots, depth)).reshape(-1, depth)
        grad_rank_t = tn(rank_low, normed_own)
        grad_rows = jnp.concatenate([grad_norm_in[None], grad_norm_mid[None], grad_rank_t])
        input_own = to_absolute(input_own.astype(bf16))
        input_low = gather_head(input_own.reshape(micro, quarter, depth))
        return sum_y(qkv_grads), grad_rows, input_low

    qkv_rows_grad, grad_rows, input_low = input_back()
    qkv_rows_grad = after(qkv_rows_grad, ff_grad)
    qkv_grad = reduce_z(qkv_rows_grad)

    by_ctx = lambda v: v.reshape(nctx, -1)
    across = lambda v, n: v.reshape(v.shape[0], nctx, n).transpose(1, 0, 2).reshape(nctx, -1)

    def finish():
        ff_rows = after(ff_grad, qkv_rows_grad).reshape(ny, rl, 3 * fl)
        pieces = jnp.zeros((ny, rl, 3 * fl), bf16)
        pieces = lax.dynamic_update_slice_in_dim(
            pieces, lax.dynamic_index_in_dim(ff_rows, y, 0), y, 0
        )
        for k in range(1, ny):
            sent = lax.dynamic_index_in_dim(ff_rows, lax.rem(y + k, ny), 0)
            got = lax.ppermute(sent, "y", [(i, (i + k) % ny) for i in range(ny)])
            pieces = lax.dynamic_update_slice_in_dim(pieces, got, lax.rem(y - k + ny, ny), 0)
        block_own = to_absolute((residual + to_relative(feed.reshape(-1, depth))).astype(bf16))
        block_out = gather_head(block_own.reshape(micro, quarter, depth))
        grad_decay = tn(low_rank, logit_low)
        grad_bias = jnp.sum(logit_low.astype(f32), axis=0)
        summed = jnp.concatenate(
            [vector_by_ctx(grad_rows).reshape(nctx, -1), by_ctx(grad_gain)], axis=1
        )
        headed = jnp.concatenate([across(grad_decay, dl), by_ctx(grad_bias)], axis=1)
        n_summed, n_headed = summed.shape[1], headed.shape[1]
        pad_s, pad_h = -n_summed % 1024, -n_headed % 1024
        tail = jnp.concatenate(
            [jnp.pad(summed, ((0, 0), (0, pad_s))), jnp.pad(headed, ((0, 0), (0, pad_h)))], axis=1
        ).reshape(nctx, -1, 128)
        tail = jnp.sum(lax.all_to_all(tail, ctx, 0, 0), axis=0)
        cut = (n_summed + pad_s) // 128
        summed, headed = tail[:cut], tail[cut:].reshape(-1)
        summed = summed + swap(summed, "c")
        summed = (summed + swap(summed, "x")).reshape(-1)
        return (
            block_out,
            input_low.astype(f32),
            *call_join(pieces),
            summed[: 2 * rl],
            summed[2 * rl : (2 + rank) * rl].reshape(rank, rl).T,
            summed[(2 + rank) * rl : n_summed],
            headed[: rank * dl].reshape(1, rank, dl),
            headed[rank * dl : n_headed].reshape(1, dl),
        )

    block_out, input_grad, g_gate, g_up, g_down, g_norms, g_rank, g_gain, g_decay, g_bias = finish()
    g_norm_in, g_norm_mid = g_norms[:rl], g_norms[rl:]
    qkv_grad = qkv_grad.astype(f32)
    return (
        block_out,
        input_grad,
        g_norm_in,
        qkv_grad[:, :width],
        qkv_grad[:, width : 2 * width],
        qkv_grad[:, 2 * width :],
        go_grad[:, :wide].astype(f32),
        g_rank,
        g_decay,
        g_bias,
        g_gain,
        go_grad[:, wide:].T.astype(f32),
        g_norm_mid,
        g_gate,
        g_up,
        g_down,
    )


def solution(mesh):
    ctx = mesh.shape["ctx"]
    shape = (NZ, ctx // NZ, 2, mesh.shape["head"] // 2)
    fine = Mesh(mesh.devices.reshape(shape), ("z", "y", "x", "c"))
    c, h = ("z", "y"), ("x", "c")
    in_specs = (
        P(None, c, None), P(None, c, None), P(), P(c), P(c, h), P(c, h), P(c, h), P(c, h), P(c, None),
        P(h, None, c), P(h, c), P(c), P(h, c), P(c), P(c, h), P(c, h), P(h, c),
    )
    out_specs = (
        P(None, c, None), P(None, c, None), P(c), P(c, h), P(c, h), P(c, h), P(c, h), P(c, None),
        P(h, None, c), P(h, c), P(c), P(h, c), P(c), P(c, h), P(c, h), P(h, c),
    )
    return jax.shard_map(
        per_device, mesh=fine, in_specs=in_specs, out_specs=out_specs, check_vma=False
    )
```

```python
import functools

import numpy as np

import jax
import jax.numpy as jnp
from jax import lax
from jax.experimental import pallas as pl
from jax.experimental.pallas import tpu as pltpu
from jax.sharding import Mesh
from jax.sharding import PartitionSpec as P

GROUP = 64
EPS = 1e-06
LEVELS = (32, 16, 8, 4, 2, 1)
f32 = jnp.float32
bf16 = jnp.bfloat16
NZ = 4


def dot(a, b, dims):
    return lax.dot_general(a, b, (dims, ((), ())), preferred_element_type=f32)


def nn(a, b):
    return dot(a, b, ((1,), (0,)))


def nt(a, b):
    return dot(a, b, ((1,), (1,)))


def tn(a, b):
    return dot(a, b, ((0,), (0,)))


def swap(x, axis):
    return lax.ppermute(x, axis, [(0, 1), (1, 0)])


def after(value, *earlier):
    anywhere = pl.BlockSpec(memory_space=pl.ANY)
    return pl.pallas_call(
        lambda *refs: None,
        in_specs=[anywhere] * (1 + len(earlier)),
        out_specs=anywhere,
        out_shape=jax.ShapeDtypeStruct(value.shape, value.dtype),
        input_output_aliases={0: 0},
        cost_estimate=pl.CostEstimate(flops=0, bytes_accessed=0, transcendentals=0),
        name="after",
    )(value, *earlier)


def as_one(runs, work):
    shapes = jax.eval_shape(work)
    return lax.cond(
        runs, work, lambda: jax.tree.map(lambda s: jnp.zeros(s.shape, s.dtype), shapes)
    )


def add_low(a, b):
    return (a.astype(f32) + b.astype(f32)).astype(bf16)


def both_in_order(piece, axis, dim):
    other = swap(piece, axis)
    first = lax.axis_index(axis) == 0
    return jnp.where(
        first, jnp.stack([piece, other], dim), jnp.stack([other, piece], dim)
    )


def silu(v):
    return v * jax.nn.sigmoid(v)


def silu_grad(v):
    sig = jax.nn.sigmoid(v)
    return sig * (1.0 + v * (1.0 - sig))


def inv_rms(v):
    return lax.rsqrt(jnp.mean(v * v, axis=-1, keepdims=True) + EPS)


def norm_back(h, r, gain, grad):
    scaled = gain * grad
    inner = jnp.mean(h * scaled, axis=-1, keepdims=True)
    return r * scaled - h * (r * r * r) * inner


def level_map(rows):
    t = np.arange(rows)[:, None]
    u = np.arange(rows)[None, :]
    out = np.zeros((rows, rows), np.int32)
    for at, half in enumerate(LEVELS):
        hit = (t // (2 * half) == u // (2 * half)) & ((t // half) % 2 == 1) & ((u // half) % 2 == 0)
        out[hit] = at + 1
    out[t == u] = len(LEVELS) + 1
    return out


def lower_map(rows):
    t = np.arange(rows)[:, None]
    u = np.arange(rows)[None, :]
    return ((t // GROUP == u // GROUP) & (t >= u)).astype(np.float32)


def ones_times(ones, value):
    hi = value.astype(bf16)
    rest = value - hi.astype(f32)
    mid = rest.astype(bf16)
    low = (rest - mid.astype(f32)).astype(bf16)
    return nn(ones, hi) + (nn(ones, mid) + nn(ones, low))


def level_decay(cum, half):
    rows, width = cum.shape
    span = max(2 * half, 8)
    parts = cum.reshape(rows // span, span, width)
    if half >= 4:
        mid = parts[:, half - 1 : half, :]
    else:
        at = lax.broadcasted_iota(jnp.int32, parts.shape, 1)
        mid = parts[:, half - 1 : half, :]
        for start in range(2 * half, span, 2 * half):
            mid = jnp.where(at >= start, parts[:, start + half - 1 : start + half, :], mid)
    return jnp.exp(-jnp.abs(parts - mid)).reshape(rows, width)


def block_of(array, at):
    return array[at * GROUP : (at + 1) * GROUP, :]


def scan_forward(qkv_ref, decay_ref, lower_ref, level_ref, open_ref, out_ref, query_ref, state_ref, keep_ref):
    step = pl.program_id(0)
    rows, width = decay_ref.shape
    count = rows // GROUP
    scale = width**-0.5
    queries = qkv_ref[:, :width].astype(f32) * scale
    keys = qkv_ref[:, width : 2 * width].astype(f32)
    values = qkv_ref[:, 2 * width :]
    levels = level_ref[...]
    cum = ones_times(lower_ref[...], decay_ref[...])
    scores = jnp.where(
        levels == len(LEVELS) + 1, nt(queries.astype(bf16), keys.astype(bf16)), 0.0
    )
    for at, half in enumerate(LEVELS):
        decay = level_decay(cum, half)
        part = nt((queries * decay).astype(bf16), (keys * decay).astype(bf16))
        scores = jnp.where(levels == at + 1, part, scores)
    local = nn(scores.astype(bf16), values)
    faded = queries * jnp.exp(cum)
    state = jnp.zeros((values.shape[1], width), f32)
    keep = jnp.ones((1, width), f32)
    for c in range(count):
        is_open = open_ref[step, c]
        state = state * is_open
        keep = keep * is_open
        faded_c = block_of(faded, c)
        cum_c = block_of(cum, c)
        last = cum_c[GROUP - 1 :, :]
        here = block_of(local, c)
        if c:
            here = here + nt(faded_c.astype(bf16), state.astype(bf16))
        out_ref[c * GROUP : (c + 1) * GROUP, :] = here
        query_ref[c * GROUP : (c + 1) * GROUP, :] = (faded_c * keep).astype(bf16)
        carried = (block_of(keys, c) * jnp.exp(last - cum_c)).astype(bf16)
        update = tn(block_of(values, c), carried)
        shrink = jnp.exp(last)
        state = state * shrink + update
        keep = keep * shrink
    state_ref[0] = state.astype(bf16)
    keep_ref[0] = jnp.broadcast_to(keep, keep_ref.shape[1:])


def scan_backward(qkv_ref, decay_ref, logit_ref, grad_ref, enter_ref, leave_ref, lower_ref, upper_ref, level_ref, open_ref, *rest):
    out_ref, logit_out_ref, local_ref, past_ref = rest[-4:]
    step = pl.program_id(0)
    rows, width = decay_ref.shape
    count = rows // GROUP
    scale = width**-0.5
    queries = qkv_ref[:, :width].astype(f32) * scale
    keys = qkv_ref[:, width : 2 * width].astype(f32)
    values = qkv_ref[:, 2 * width :]
    grads = grad_ref[...]
    levels = level_ref[...]
    cum = ones_times(lower_ref[...], decay_ref[...])
    pair_grad = nt(grads, values)
    on_diagonal = levels == len(LEVELS) + 1
    own = jnp.sum(jnp.where(on_diagonal, pair_grad, 0.0), axis=1, keepdims=True)
    scores = jnp.where(on_diagonal, nt(queries.astype(bf16), keys.astype(bf16)), 0.0)
    query_grad = jnp.zeros((rows, width), f32)
    key_grad = jnp.zeros((rows, width), f32)
    for at, half in enumerate(LEVELS):
        decay = level_decay(cum, half)
        query_l = (queries * decay).astype(bf16)
        key_l = (keys * decay).astype(bf16)
        hit = levels == at + 1
        scores = jnp.where(hit, nt(query_l, key_l), scores)
        grad_l = jnp.where(hit, pair_grad, 0.0).astype(bf16)
        query_grad = query_grad + nn(grad_l, key_l) * decay
        key_grad = key_grad + tn(grad_l, query_l) * decay
    value_grad = tn(scores.astype(bf16), grads)
    rising = jnp.exp(cum)
    faded = queries * rising
    state = enter_ref[0].astype(f32)
    for c in range(count):
        state = state * open_ref[step, c]
        past_ref[c] = state
        cum_c = block_of(cum, c)
        last = cum_c[GROUP - 1 :, :]
        if c < count - 1:
            carried = (block_of(keys, c) * jnp.exp(last - cum_c)).astype(bf16)
            state = state * jnp.exp(last) + tn(block_of(values, c), carried)
    after = leave_ref[0].astype(f32)
    for c in range(count - 1, -1, -1):
        span = slice(c * GROUP, (c + 1) * GROUP)
        past = past_ref[c]
        cum_c = block_of(cum, c)
        last = cum_c[GROUP - 1 :, :]
        shrink = jnp.exp(last)
        fading = jnp.exp(last - cum_c)
        keys_c = block_of(keys, c)
        queries_c = block_of(queries, c)
        grads_c = block_of(grads, c)
        after_low = after.astype(bf16)
        query_c = block_of(query_grad, c) + nn(grads_c, past.astype(bf16)) * block_of(rising, c)
        key_far = nn(block_of(values, c), after_low) * fading
        key_c = block_of(key_grad, c) + key_far
        value_c = block_of(value_grad, c) + nt((keys_c * fading).astype(bf16), after_low)
        own_c = block_of(own, c)
        out_ref[span, :width] = ((query_c + own_c * keys_c) * scale).astype(bf16)
        out_ref[span, width : 2 * width] = (key_c + own_c * queries_c).astype(bf16)
        out_ref[span, 2 * width :] = value_c.astype(bf16)
        local_ref[span, :] = queries_c * query_c - keys_c * key_c
        at_last = jnp.sum(keys_c * key_far, axis=0, keepdims=True) + shrink * jnp.sum(
            past * after, axis=0, keepdims=True
        )
        logit_out_ref[span, :] = jnp.broadcast_to(at_last, (GROUP, width))
        if c:
            after = (after * shrink + tn(grads_c, block_of(faded, c).astype(bf16))) * open_ref[step, c]
    decay_grad = ones_times(upper_ref[...], local_ref[...]) + logit_out_ref[...]
    logit_out_ref[...] = decay_grad * jax.nn.sigmoid(-logit_ref[...]) * (1.0 / 16.0)


def call_forward(qkv, decays, is_open, micro_count):
    rows = qkv.shape[0] // micro_count
    width = decays.shape[1]
    wide = qkv.shape[1] - 2 * width
    lower = jnp.asarray(lower_map(rows), bf16)
    level = jnp.asarray(level_map(rows))
    whole = lambda m: (0, 0)
    mine = lambda m: (m, 0)
    mine3 = lambda m: (m, 0, 0)
    return pl.pallas_call(
        scan_forward,
        grid=(micro_count,),
        in_specs=[
            pl.BlockSpec((rows, qkv.shape[1]), mine),
            pl.BlockSpec((rows, width), mine),
            pl.BlockSpec((rows, rows), whole),
            pl.BlockSpec((rows, rows), whole),
            pl.BlockSpec(memory_space=pltpu.SMEM),
        ],
        out_specs=[
            pl.BlockSpec((rows, wide), mine),
            pl.BlockSpec((rows, width), mine),
            pl.BlockSpec((1, wide, width), mine3),
            pl.BlockSpec((1, 8, width), mine3),
        ],
        out_shape=[
            jax.ShapeDtypeStruct((micro_count * rows, wide), f32),
            jax.ShapeDtypeStruct((micro_count * rows, width), bf16),
            jax.ShapeDtypeStruct((micro_count, wide, width), bf16),
            jax.ShapeDtypeStruct((micro_count, 8, width), f32),
        ],
        compiler_params=pltpu.CompilerParams(vmem_limit_bytes=40 * 2**20),
        cost_estimate=pl.CostEstimate(flops=2_000_000_000, bytes_accessed=8_000_000, transcendentals=1_500_000),
        name="scan_forward",
    )(qkv, decays, lower, level, is_open)


def call_backward(qkv, decays, logits, grads, enter, leave, is_open, micro_count, *earlier):
    rows = qkv.shape[0] // micro_count
    width = decays.shape[1]
    wide = qkv.shape[1] - 2 * width
    lower = jnp.asarray(lower_map(rows), bf16)
    upper = jnp.asarray(lower_map(rows).T, bf16)
    level = jnp.asarray(level_map(rows))
    whole = lambda m: (0, 0)
    mine = lambda m: (m, 0)
    mine3 = lambda m: (m, 0, 0)
    return pl.pallas_call(
        scan_backward,
        grid=(micro_count,),
        in_specs=[
            pl.BlockSpec((rows, qkv.shape[1]), mine),
            pl.BlockSpec((rows, width), mine),
            pl.BlockSpec((rows, width), mine),
            pl.BlockSpec((rows, wide), mine),
            pl.BlockSpec((1, wide, width), mine3),
            pl.BlockSpec((1, wide, width), mine3),
            pl.BlockSpec((rows, rows), whole),
            pl.BlockSpec((rows, rows), whole),
            pl.BlockSpec((rows, rows), whole),
            pl.BlockSpec(memory_space=pltpu.SMEM),
        ]
        + [pl.BlockSpec(memory_space=pl.ANY)] * len(earlier),
        out_specs=[
            pl.BlockSpec((rows, qkv.shape[1]), mine),
            pl.BlockSpec((rows, width), mine),
        ],
        out_shape=[
            jax.ShapeDtypeStruct((micro_count * rows, qkv.shape[1]), bf16),
            jax.ShapeDtypeStruct((micro_count * rows, width), f32),
        ],
        scratch_shapes=[
            pltpu.VMEM((rows, width), f32),
            pltpu.VMEM((rows // GROUP, wide, width), f32),
        ],
        compiler_params=pltpu.CompilerParams(vmem_limit_bytes=40 * 2**20),
        cost_estimate=pl.CostEstimate(flops=5_000_000_000, bytes_accessed=12_000_000, transcendentals=1_500_000),
        name="scan_backward",
    )(qkv, decays, logits, grads, enter, leave, lower, upper, level, is_open, *earlier)


def scan_states(got_ref, out_ref, *, micro, strip, reverse):
    count = got_ref.shape[0]
    width = got_ref.shape[2]
    running = [jnp.zeros((strip, width), f32) for _ in range(micro)]
    order = range(count - 1, -1, -1) if reverse else range(count)
    for at in order:
        tail = got_ref[at, micro * strip :, :].astype(f32)
        for m in range(micro):
            span = slice(m * strip, (m + 1) * strip)
            out_ref[at, span, :] = running[m].astype(bf16)
            keep = tail[m : m + 1, :] + tail[micro + m : micro + m + 1, :]
            running[m] = running[m] * keep + got_ref[at, span, :].astype(f32)


def spread_states(state, keep, reverse):
    ctx = ("z", "y")
    count = lax.axis_size(ctx)
    micro, wide, width = state.shape
    strip = wide // count
    parts = state.reshape(micro, count, strip, width).transpose(1, 0, 2, 3)
    parts = parts.reshape(count, micro * strip, width)
    keep_hi = keep.astype(bf16)
    keep_lo = (keep - keep_hi.astype(f32)).astype(bf16)
    extra = jnp.concatenate([keep_hi, keep_lo, jnp.zeros((16 - 2 * micro, width), bf16)])
    sent = jnp.concatenate(
        [parts, jnp.broadcast_to(extra[None], (count, 16, width))], axis=1
    )
    got = lax.all_to_all(sent, ctx, 0, 0)
    return pl.pallas_call(
        functools.partial(scan_states, micro=micro, strip=strip, reverse=reverse),
        out_shape=jax.ShapeDtypeStruct((count, micro * strip, width), bf16),
        compiler_params=pltpu.CompilerParams(vmem_limit_bytes=16 * 2**20),
        cost_estimate=pl.CostEstimate(flops=2_000_000, bytes_accessed=1_100_000, transcendentals=0),
        name="scan_states",
    )(got)


def collect_states(entering, micro):
    count, _, width = entering.shape
    strip = entering.shape[1] // micro
    back = lax.all_to_all(entering, ("z", "y"), 0, 0)
    return back.reshape(count, micro, strip, width).transpose(1, 0, 2, 3).reshape(micro, -1, width)


def feed_kernel(mid_ref, low_ref, weight_ref, *rest, units):
    pair_ref, hidden_ref, grad_ref = rest[-3:]
    both = nn(mid_ref[...], weight_ref[:, : 2 * units])
    gate, up = both[:, :units], both[:, units:]
    back = nn(low_ref[...], weight_ref[:, 2 * units :])
    sig = jax.nn.sigmoid(gate)
    act = gate * sig
    hidden_ref[...] = (act * up).astype(bf16)
    pair_ref[:, :units] = (back * up * (sig * (1.0 + gate * (1.0 - sig)))).astype(bf16)
    pair_ref[:, units:] = (back * act).astype(bf16)
    grad_ref[...] = nt(pair_ref[...], weight_ref[:, : 2 * units]).astype(bf16)


def call_feed(plane_mid, plane_low, weight, units, *earlier):
    rows, depth = plane_mid.shape
    tile = 256
    return pl.pallas_call(
        functools.partial(feed_kernel, units=units),
        grid=(rows // tile,),
        in_specs=[
            pl.BlockSpec((tile, depth), lambda i: (i, 0)),
            pl.BlockSpec((tile, depth), lambda i: (i, 0)),
            pl.BlockSpec(weight.shape, lambda i: (0, 0), pipeline_mode=pl.Buffered(1)),
        ]
        + [pl.BlockSpec(memory_space=pl.ANY)] * len(earlier),
        out_specs=[
            pl.BlockSpec((tile, 2 * units), lambda i: (i, 0)),
            pl.BlockSpec((tile, units), lambda i: (i, 0)),
            pl.BlockSpec((tile, depth), lambda i: (i, 0)),
        ],
        out_shape=[
            jax.ShapeDtypeStruct((rows, 2 * units), bf16),
            jax.ShapeDtypeStruct((rows, units), bf16),
            jax.ShapeDtypeStruct((rows, depth), bf16),
        ],
        compiler_params=pltpu.CompilerParams(vmem_limit_bytes=48 * 2**20),
        cost_estimate=pl.CostEstimate(
            flops=10 * rows * depth * units, bytes_accessed=28_000_000, transcendentals=rows * units
        ),
        name="feed_forward",
    )(plane_mid, plane_low, weight, *earlier)


def split_units(gate_ref, up_ref, down_ref, out_ref):
    parts, rows, width = out_ref.shape
    units = width // 3
    for k in range(parts):
        span = slice(k * units, (k + 1) * units)
        out_ref[k, :, :units] = gate_ref[:, span]
        out_ref[k, :, units : 2 * units] = up_ref[:, span]
        out_ref[k, :, 2 * units :] = down_ref[span, :].astype(f32).T.astype(bf16)


def call_split(w_gate, w_up, w_down, parts):
    rows, ff = w_gate.shape
    return pl.pallas_call(
        split_units,
        out_shape=jax.ShapeDtypeStruct((parts, rows, 3 * ff // parts), bf16),
        compiler_params=pltpu.CompilerParams(vmem_limit_bytes=32 * 2**20),
        cost_estimate=pl.CostEstimate(flops=0, bytes_accessed=12 * rows * ff, transcendentals=0),
        name="split_units",
    )(w_gate, w_up, w_down)


def join_units(in_ref, gate_ref, up_ref, down_ref):
    parts, rows, width = in_ref.shape
    units = width // 3
    for k in range(parts):
        span = slice(k * units, (k + 1) * units)
        gate_ref[:, span] = in_ref[k, :, :units].astype(f32)
        up_ref[:, span] = in_ref[k, :, units : 2 * units].astype(f32)
        down_ref[span, :] = in_ref[k, :, 2 * units :].astype(f32).T


def call_join(pieces):
    parts, rows, width = pieces.shape
    ff = width // 3 * parts
    return pl.pallas_call(
        join_units,
        out_shape=[
            jax.ShapeDtypeStruct((rows, ff), f32),
            jax.ShapeDtypeStruct((rows, ff), f32),
            jax.ShapeDtypeStruct((ff, rows), f32),
        ],
        compiler_params=pltpu.CompilerParams(vmem_limit_bytes=32 * 2**20),
        cost_estimate=pl.CostEstimate(flops=0, bytes_accessed=18 * rows * ff, transcendentals=0),
        name="join_units",
    )(pieces)


def pick_rows(at_ref, in_ref, out_ref):
    out_ref[...] = in_ref[0]


def call_pick(pieces, at):
    _, rows, width = pieces.shape
    return pl.pallas_call(
        pick_rows,
        grid_spec=pltpu.PrefetchScalarGridSpec(
            num_scalar_prefetch=1,
            grid=(1,),
            in_specs=[pl.BlockSpec((1, rows, width), lambda i, at: (at[0], 0, 0))],
            out_specs=pl.BlockSpec((rows, width), lambda i, at: (0, 0)),
        ),
        out_shape=jax.ShapeDtypeStruct((rows, width), pieces.dtype),
        compiler_params=pltpu.CompilerParams(vmem_limit_bytes=16 * 2**20),
        cost_estimate=pl.CostEstimate(flops=0, bytes_accessed=4 * rows * width, transcendentals=0),
        name="pick_rows",
    )(at.reshape(1), pieces)


def join_two(at_ref, own_ref, got_ref, gate_ref, up_ref, down_ref):
    units = own_ref.shape[2] // 3
    first = at_ref[0] == 0
    for k in range(2):
        mine = jnp.logical_xor(first, k == 1)
        span = slice(k * units, (k + 1) * units)

        @pl.when(mine)
        def _():
            value = own_ref[0].astype(f32)
            gate_ref[:, span] = value[:, :units]
            up_ref[:, span] = value[:, units : 2 * units]
            down_ref[span, :] = value[:, 2 * units :].T

        @pl.when(jnp.logical_not(mine))
        def _():
            value = got_ref[...].astype(f32)
            gate_ref[:, span] = value[:, :units]
            up_ref[:, span] = value[:, units : 2 * units]
            down_ref[span, :] = value[:, 2 * units :].T


def call_join_two(pieces, got, at):
    _, rows, width = pieces.shape
    ff = width // 3 * 2
    return pl.pallas_call(
        join_two,
        grid_spec=pltpu.PrefetchScalarGridSpec(
            num_scalar_prefetch=1,
            grid=(1,),
            in_specs=[
                pl.BlockSpec((1, rows, width), lambda i, at: (at[0], 0, 0)),
                pl.BlockSpec((rows, width), lambda i, at: (0, 0)),
            ],
            out_specs=[
                pl.BlockSpec((rows, ff), lambda i, at: (0, 0)),
                pl.BlockSpec((rows, ff), lambda i, at: (0, 0)),
                pl.BlockSpec((ff, rows), lambda i, at: (0, 0)),
            ],
        ),
        out_shape=[
            jax.ShapeDtypeStruct((rows, ff), f32),
            jax.ShapeDtypeStruct((rows, ff), f32),
            jax.ShapeDtypeStruct((ff, rows), f32),
        ],
        compiler_params=pltpu.CompilerParams(vmem_limit_bytes=32 * 2**20),
        cost_estimate=pl.CostEstimate(flops=0, bytes_accessed=18 * rows * ff, transcendentals=0),
        name="join_two",
    )(at.reshape(1), pieces, got)


def widen_rows(in_ref, query_ref, key_ref, value_ref):
    width = query_ref.shape[1]
    query_ref[...] = in_ref[:, :width].astype(f32)
    key_ref[...] = in_ref[:, width : 2 * width].astype(f32)
    value_ref[...] = in_ref[:, 2 * width :].astype(f32)


def widen_turned(in_ref, gate_ref, out_ref):
    wide = gate_ref.shape[1]
    gate_ref[...] = in_ref[:, :wide].astype(f32)
    out_ref[...] = in_ref[:, wide:].astype(f32).T


def call_widen(kernel, value, shapes):
    return pl.pallas_call(
        kernel,
        out_shape=[jax.ShapeDtypeStruct(shape, f32) for shape in shapes],
        compiler_params=pltpu.CompilerParams(vmem_limit_bytes=16 * 2**20),
        cost_estimate=pl.CostEstimate(flops=0, bytes_accessed=6 * value.size, transcendentals=0),
        name="widen",
    )(value)


def feed_grad_kernel(*refs):
    out_ref = refs[-1]
    two = refs[2].shape[1]
    mid_a, low_a, pair_a, hidden_a, mid_b, low_b, pair_b, hidden_b = (r[...] for r in refs[:8])
    out_ref[:, :two] = (tn(mid_a, pair_a) + tn(mid_b, pair_b)).astype(bf16)
    out_ref[:, two:] = (tn(low_a, hidden_a) + tn(low_b, hidden_b)).astype(bf16)


def call_feed_grad(near, far, *earlier):
    rows, depth = near[0].shape
    two, units = near[2].shape[1], near[3].shape[1]
    tile = 256
    one = [
        pl.BlockSpec((rows, tile), lambda i: (0, i)),
        pl.BlockSpec((rows, tile), lambda i: (0, i)),
        pl.BlockSpec((rows, two), lambda i: (0, 0), pipeline_mode=pl.Buffered(1)),
        pl.BlockSpec((rows, units), lambda i: (0, 0), pipeline_mode=pl.Buffered(1)),
    ]
    return pl.pallas_call(
        feed_grad_kernel,
        grid=(depth // tile,),
        in_specs=one + one + [pl.BlockSpec(memory_space=pl.ANY)] * len(earlier),
        out_specs=pl.BlockSpec((tile, two + units), lambda i: (i, 0)),
        out_shape=jax.ShapeDtypeStruct((depth, two + units), bf16),
        compiler_params=pltpu.CompilerParams(vmem_limit_bytes=48 * 2**20),
        cost_estimate=pl.CostEstimate(
            flops=4 * rows * depth * (two + units), bytes_accessed=21_000_000, transcendentals=0
        ),
        name="feed_grad",
    )(*near, *far, *earlier)


def gather_plane(piece):
    count = lax.axis_size("y")
    if count == 2:
        a, b = piece[0], piece[1]
        a_y, b_x = swap(a, "y"), swap(b, "x")
        a, b = jnp.stack([a, a_y]), jnp.stack([b, b_x])
        a_x, b_y = swap(a, "x"), swap(b, "y")
        here = jnp.concatenate([a, a_x, b, b_y])
    else:
        rows = [piece]
        for k in range(1, count):
            rows.append(lax.ppermute(piece, "y", [((i + k) % count, i) for i in range(count)]))
        here = jnp.stack(rows, axis=1)
        here = jnp.stack([here, swap(here, "x")], axis=1)
        here = here.reshape((-1,) + piece.shape[1:])
    here = here.reshape(-1, piece.shape[-1])
    return here, swap(here, "c")


def scatter_first(here, micro, quarter):
    count = lax.axis_size("y")
    depth = here.shape[-1]
    if count == 2:
        here = here.reshape(2, 2, 2 * quarter, depth)
        a, b = here[0], here[1]
        a_got, b_got = swap(a[1], "x"), swap(b[1], "y")
        return add_low(a[0], a_got), add_low(b[0], b_got)
    here = here.reshape(micro, 2, count, quarter, depth)
    here = add_low(here[:, 0], swap(here[:, 1], "x"))
    return here[:, :1], here[:, 1:]


def scatter_second(a, b, quarter):
    count = lax.axis_size("y")
    if count == 2:
        a, b = (v.reshape(2, quarter, -1) for v in (a, b))
        a_got, b_got = swap(a[1], "y"), swap(b[1], "x")
        a = a[0].astype(f32) + a_got.astype(f32)
        b = b[0].astype(f32) + b_got.astype(f32)
        return jnp.stack([a, b])
    total = a[:, 0].astype(f32)
    for k in range(1, count):
        got = lax.ppermute(b[:, k - 1], "y", [(i, (i + k) % count) for i in range(count)])
        total = total + got.astype(f32)
    return total


def scatter_head(part):
    micro, slots, width = part.shape
    c, x = lax.axis_index("c"), lax.axis_index("x")
    view = part.reshape(micro, 2, slots // 2, width)
    mine = lax.dynamic_index_in_dim(view, c, 1, keepdims=False)
    other = lax.dynamic_index_in_dim(view, 1 - c, 1, keepdims=False)
    mine = add_low(mine, swap(other, "c"))
    view = mine.reshape(micro, 2, slots // 4, width)
    mine = lax.dynamic_index_in_dim(view, x, 1, keepdims=False)
    other = lax.dynamic_index_in_dim(view, 1 - x, 1, keepdims=False)
    return mine.astype(f32) + swap(other, "x").astype(f32)


def gather_head(piece):
    micro, quarter, width = piece.shape
    both = both_in_order(piece, "x", 1)
    both = both_in_order(both, "c", 1)
    return both.reshape(micro, 4 * quarter, width)


def own_quarter(array):
    micro, slots, width = array.shape
    c, x = lax.axis_index("c"), lax.axis_index("x")
    view = array.reshape(micro, 4, slots // 4, width)
    return lax.dynamic_index_in_dim(view, 2 * c + x, 1, keepdims=False)


def others_y(piece):
    count = lax.axis_size("y")
    out = [piece]
    for k in range(1, count):
        out.append(lax.ppermute(piece, "y", [((i + k) % count, i) for i in range(count)]))
    return out


def to_relative(array):
    count, y = lax.axis_size("y"), lax.axis_index("y")
    t, depth = array.shape
    rl = depth // (NZ * count)
    if count == 2:
        even = jnp.concatenate([array[:, 2 * z * rl : (2 * z + 1) * rl] for z in range(NZ)], axis=1)
        odd = jnp.concatenate([array[:, (2 * z + 1) * rl : (2 * z + 2) * rl] for z in range(NZ)], axis=1)
        first = y == 0
        return jnp.concatenate([jnp.where(first, even, odd), jnp.where(first, odd, even)], axis=1)
    view = jnp.roll(array.reshape(t, NZ, count, rl), -y, axis=2)
    return view.transpose(0, 2, 1, 3).reshape(t, depth)


def to_absolute(array):
    count, y = lax.axis_size("y"), lax.axis_index("y")
    t, depth = array.shape
    rl = depth // (NZ * count)
    if count == 2:
        first = y == 0
        out = []
        for z in range(NZ):
            own = array[:, z * rl : (z + 1) * rl]
            other = array[:, (NZ + z) * rl : (NZ + z + 1) * rl]
            out += [jnp.where(first, own, other), jnp.where(first, other, own)]
        return jnp.concatenate(out, axis=1)
    view = array.reshape(t, count, NZ, rl).transpose(0, 2, 1, 3)
    return jnp.roll(view, y, axis=2).reshape(t, depth)


def vector_by_ctx(value):
    count, y = lax.axis_size("y"), lax.axis_index("y")
    view = value.reshape(value.shape[0], count, NZ, -1)
    if count == 2:
        view = jnp.where(y == 0, view, view[:, ::-1])
    else:
        view = jnp.roll(view, y, axis=1)
    return view.transpose(2, 1, 0, 3).reshape(NZ * count, value.shape[0], -1)


def vector_from_ctx(value):
    count, y = lax.axis_size("y"), lax.axis_index("y")
    view = value.reshape((NZ, count) + value.shape[1:]).transpose(2, 1, 0, 3)
    if count == 2:
        view = jnp.where(y == 0, view, view[:, ::-1])
    else:
        view = jnp.roll(view, -y, axis=1)
    return view.reshape(value.shape[1], -1)


def sum_y(parts, *between):
    count = lax.axis_size("y")
    total = (after(parts[0], *between) if between else parts[0]).astype(f32)
    for k in range(1, count):
        got = lax.ppermute(parts[k], "y", [(i, (i + k) % count) for i in range(count)])
        total = total + got.astype(f32)
    return total.astype(bf16)


def reduce_z(part):
    return lax.psum_scatter(part, "z", scatter_dimension=0, tiled=True)


def per_device(
    tokens, cotangent, lengths, norm_in, w_query, w_key, w_value, w_outgate, w_rank,
    w_decay, decay_bias, head_gain, w_out, norm_mid, w_gate, w_up, w_down,
):
    ctx = ("z", "y")
    ny = lax.axis_size("y")
    nctx = NZ * ny
    y = lax.axis_index("y")
    place = lax.axis_index(ctx)
    micro, slots, depth = tokens.shape
    groups = slots // GROUP
    rl = w_query.shape[0]
    width = w_query.shape[1]
    wide = w_value.shape[1]
    rank = w_rank.shape[1]
    ff = w_gate.shape[1]
    fl = ff // ny
    total = micro * slots

    w_qkv = jnp.concatenate([w_query, w_key, w_value], axis=1)
    qkv_rows = lax.all_gather(w_qkv, "z", axis=0, tiled=True)
    w_go = jnp.concatenate([w_outgate, w_out.T], axis=1)
    go_rows = lax.all_gather(w_go, "z", axis=0, tiled=True)

    small = jnp.concatenate(
        [norm_in, norm_mid, w_rank.T.reshape(-1), w_decay[0].reshape(-1), decay_bias[0], head_gain]
    )
    n_small = small.shape[0]
    pad = -n_small % 1024
    small = jnp.pad(small, (0, pad)).reshape(1, -1, 128)
    small = jnp.broadcast_to(small, (nctx,) + small.shape[1:])
    small = lax.all_to_all(small, ctx, 0, 0).reshape(nctx, -1)
    at = 0

    def take(size):
        nonlocal at
        at += size
        return small[:, at - size : at]

    by_row = vector_from_ctx(take((2 + rank) * rl).reshape(nctx, 2 + rank, rl))
    gain_in = by_row[:1].astype(f32)
    gain_mid = by_row[1:2].astype(f32)
    rank_t = by_row[2:]
    dl = width // nctx
    decay_w = take(rank * dl).reshape(nctx, rank, dl).transpose(1, 0, 2).reshape(rank, width)
    bias = take(dl).reshape(1, width).astype(f32)
    gain_head = take(wide // nctx).reshape(1, wide).astype(f32)

    ff_local = call_split(w_gate, w_up, w_down, ny)
    own = lax.dynamic_index_in_dim(ff_local, y, 0, keepdims=False)
    if ny == 2:
        got = swap(lax.dynamic_index_in_dim(ff_local, 1 - y, 0, keepdims=False), "y")
        ff_unit = jnp.where(y == 0, jnp.stack([own, got]), jnp.stack([got, own]))
    else:
        pieces = [own]
        for k in range(1, ny):
            sent = lax.dynamic_index_in_dim(ff_local, lax.rem(y + ny - k, ny), 0, keepdims=False)
            pieces.append(lax.ppermute(sent, "y", [((i + k) % ny, i) for i in range(ny)]))
        ff_unit = jnp.roll(jnp.stack(pieces), y, axis=0)
    ff_unit = ff_unit.reshape(ny * rl, 3 * fl)

    group_ids = place * groups + jnp.arange(groups, dtype=jnp.int32)
    end = jnp.zeros((micro, 1), jnp.int32)
    reset = group_ids[None, :] == end
    for i in range(lengths.shape[1]):
        end = end + lengths[:, i : i + 1]
        reset = reset | (group_ids[None, :] == end)
    is_open = 1.0 - reset.astype(f32)

    def mask_of(at):
        slot_ids = at * slots + jnp.arange(slots, dtype=jnp.int32)
        return (slot_ids[None, :] < end * GROUP).astype(bf16)[:, :, None]

    c_at, x_at = lax.axis_index("c"), lax.axis_index("x")
    quarter = slots // 4
    view = cotangent.reshape(micro, 2, slots // 2, depth)
    half_parts = others_y(lax.dynamic_index_in_dim(view, c_at, 1, keepdims=False))

    ff_full = lax.all_gather(ff_unit, "z", axis=0, tiled=True)
    qkv_parts = others_y(qkv_rows)
    go_parts = others_y(go_rows)

    inputs = to_relative(tokens.reshape(total, depth)).astype(f32)
    r_in = inv_rms(inputs)
    normed_in = (inputs * r_in * gain_in).astype(bf16)
    step = depth // ny
    low_rank = nt(normed_in, rank_t).astype(bf16)
    logits = nn(low_rank, decay_w) + bias
    decays = jax.nn.log_sigmoid(logits) / 16.0

    def columns(array, k):
        return array[:, k * step : (k + 1) * step]

    qkv = sum(nn(columns(normed_in, k), w) for k, w in enumerate(qkv_parts)).astype(bf16)

    runs = lengths[0, 0] >= 1

    def recurrence():
        local_out, far_query, state, keep = call_forward(qkv, decays, is_open, micro)
        keep = keep[:, 0, :]
        return local_out, far_query, collect_states(spread_states(state, keep, False), micro), keep

    local_out, far_query, enter, keep = as_one(runs, recurrence)

    out_low = cotangent * mask_of(place)
    low_parts = []
    for k, half in enumerate(half_parts):
        mask = mask_of(place - y + lax.rem(y + k, ny)).reshape(micro, 2, slots // 2, 1)
        mask = lax.dynamic_index_in_dim(mask, c_at, 1, keepdims=False)
        half = (half * mask).reshape(micro, 2, quarter, depth)
        low_parts.append(jnp.where(x_at == 0, half, half[:, ::-1]))
    if ny == 2:
        low_near = [
            jnp.stack([p[0] for p in low_parts], 1),
            jnp.stack([p[1] for p in low_parts], 0),
        ]
        low_near = jnp.stack(low_near).reshape(-1, depth)
    else:
        low_near = jnp.stack(low_parts, 2).reshape(-1, depth)
    low_far = swap(low_near, "c")

    outgate = sum(nn(columns(normed_in, k), w[:, :wide]) for k, w in enumerate(go_parts))
    outgate = outgate.astype(bf16).astype(f32)
    mixed = local_out + jnp.concatenate(
        [nt(far_query[m * slots : (m + 1) * slots], enter[m]) for m in range(micro)]
    )
    r_head = inv_rms(mixed)
    gated = (mixed * r_head * gain_head * silu(outgate)).astype(bf16)
    attention = jnp.concatenate([nt(gated, w[:, wide:]) for w in go_parts], axis=1)
    attention = scatter_head(attention.astype(bf16).reshape(micro, slots, depth))
    inputs_own = to_relative(own_quarter(tokens).reshape(-1, depth)).astype(f32)
    residual = inputs_own + attention.reshape(micro * quarter, depth)

    r_mid = inv_rms(residual)
    normed_mid = to_absolute((residual * r_mid * gain_mid).astype(bf16))
    mid_near, mid_far = gather_plane(normed_mid.reshape(micro, quarter, depth))
    pair_far, hidden_far, part_far = call_feed(mid_far, low_far, ff_full, fl)
    pair_near, hidden_near, part_near = call_feed(mid_near, low_near, ff_full, fl, part_far)
    mid_part = add_low(part_near, swap(part_far, "c"))
    def feed_back():
        ff_part = call_feed_grad(
            (mid_near, low_near, pair_near, hidden_near),
            (mid_far, low_far, pair_far, hidden_far),
        )
        return ff_part, *scatter_first(mid_part, micro, quarter)

    ff_part, mid_a, mid_b = as_one(runs, feed_back)
    ff_grad = reduce_z(ff_part)

    def feed_part(hidden):
        return nt(hidden, ff_full[:, 2 * fl :]).astype(bf16)

    def blocks_back():
        mid_grad = to_relative(scatter_second(mid_a, mid_b, quarter).reshape(-1, depth))

        out_grad = to_relative(own_quarter(out_low).reshape(-1, depth)).astype(f32)
        resid_grad = out_grad + norm_back(residual, r_mid, gain_mid, mid_grad)
        grad_norm_mid = jnp.sum(mid_grad * residual * r_mid, axis=0)
        resid_low = gather_head(resid_grad.astype(bf16).reshape(micro, quarter, depth))
        resid_low = resid_low.reshape(total, depth)
        gated_grad = sum(nn(columns(resid_low, k), w[:, wide:]) for k, w in enumerate(go_parts))

        unit = mixed * r_head
        gate_act = silu(outgate)
        unit_grad = gated_grad * gate_act
        outgate_low = (gated_grad * unit * gain_head * silu_grad(outgate)).astype(bf16)
        mixed_grad = norm_back(mixed, r_head, gain_head, unit_grad).astype(bf16)
        grad_gain = jnp.sum(unit_grad * unit, axis=0)
        state_grad = jnp.stack(
            [
                tn(mixed_grad[m * slots : (m + 1) * slots], far_query[m * slots : (m + 1) * slots])
                for m in range(micro)
            ]
        ).astype(bf16)
        entering = spread_states(state_grad, keep, True)
        leave = collect_states(entering, micro)
        go_grads = [
            jnp.concatenate(
                [tn(columns(normed_in, k), outgate_low), tn(columns(resid_low, k), gated)], axis=1
            ).astype(bf16)
            for k in range(ny)
        ]
        go_rows_grad = sum_y(go_grads[:1] + [after(g, entering) for g in go_grads[1:]])
        feed_far = swap(feed_part(after(hidden_far, mixed_grad)), "c")
        feed_rows = add_low(feed_part(after(hidden_near, mixed_grad)), feed_far)
        feed = scatter_second(*scatter_first(feed_rows, micro, quarter), quarter)
        qkv_low, logit_grad = call_backward(
            qkv, decays, logits, mixed_grad, enter, leave, is_open, micro
        )
        logit_low = logit_grad.astype(bf16)
        qkv_grads = [tn(columns(normed_in, k), qkv_low).astype(bf16) for k in range(ny)]
        rank_part = nt(logit_low, decay_w).astype(bf16)
        rank_pad = jnp.pad(rank_part, ((0, 0), (0, 128 - rank)))
        qkv_later = after(qkv_low, *qkv_grads)
        in_part = [
            (nt(qkv_later, wq) + nt(outgate_low, wg[:, :wide])).astype(bf16)
            for wq, wg in zip(qkv_parts, go_parts)
        ]
        in_part = jnp.concatenate(in_part + [rank_pad], axis=1).reshape(micro, slots, depth + 128)
        return resid_grad, grad_norm_mid, grad_gain, go_rows_grad, qkv_grads, in_part, logit_low, feed

    resid_grad, grad_norm_mid, grad_gain, go_rows_grad, qkv_grads, in_part, logit_low, feed = as_one(
        runs, blocks_back
    )
    go_grad = reduce_z(go_rows_grad)

    def input_back():
        in_sum = scatter_head(in_part).reshape(-1, depth + 128)
        rank_low = in_sum[:, depth : depth + rank].astype(bf16)
        in_grad = in_sum[:, :depth] + nn(rank_low, rank_t)
        r_own = inv_rms(inputs_own)
        input_own = resid_grad + norm_back(inputs_own, r_own, gain_in, in_grad)
        grad_norm_in = jnp.sum(in_grad * inputs_own * r_own, axis=0)
        normed_own = own_quarter(normed_in.reshape(micro, slots, depth)).reshape(-1, depth)
        grad_rank_t = tn(rank_low, normed_own)
        grad_rows = jnp.concatenate([grad_norm_in[None], grad_norm_mid[None], grad_rank_t])
        input_own = to_absolute(input_own.astype(bf16))
        input_low = gather_head(input_own.reshape(micro, quarter, depth))
        return sum_y(qkv_grads), grad_rows, input_low

    qkv_rows_grad, grad_rows, input_low = input_back()
    qkv_rows_grad = after(qkv_rows_grad, ff_grad)
    qkv_grad = reduce_z(qkv_rows_grad)

    by_ctx = lambda v: v.reshape(nctx, -1)
    across = lambda v, n: v.reshape(v.shape[0], nctx, n).transpose(1, 0, 2).reshape(nctx, -1)

    def finish():
        ff_rows = after(ff_grad, qkv_rows_grad).reshape(ny, rl, 3 * fl)
        if ny == 2:
            joined = call_join_two(ff_rows, swap(call_pick(ff_rows, 1 - y), "y"), y)
        else:
            pieces = jnp.zeros((ny, rl, 3 * fl), bf16)
            pieces = lax.dynamic_update_slice_in_dim(
                pieces, lax.dynamic_index_in_dim(ff_rows, y, 0), y, 0
            )
            for k in range(1, ny):
                sent = lax.dynamic_index_in_dim(ff_rows, lax.rem(y + k, ny), 0)
                got = lax.ppermute(sent, "y", [(i, (i + k) % ny) for i in range(ny)])
                pieces = lax.dynamic_update_slice_in_dim(pieces, got, lax.rem(y - k + ny, ny), 0)
            joined = call_join(pieces)
        block_own = to_absolute((residual + to_relative(feed.reshape(-1, depth))).astype(bf16))
        block_out = gather_head(block_own.reshape(micro, quarter, depth))
        grad_decay = tn(low_rank, logit_low)
        grad_bias = jnp.sum(logit_low.astype(f32), axis=0)
        summed = jnp.concatenate(
            [vector_by_ctx(grad_rows).reshape(nctx, -1), by_ctx(grad_gain)], axis=1
        )
        headed = jnp.concatenate([across(grad_decay, dl), by_ctx(grad_bias)], axis=1)
        n_summed, n_headed = summed.shape[1], headed.shape[1]
        pad_s, pad_h = -n_summed % 1024, -n_headed % 1024
        tail = jnp.concatenate(
            [jnp.pad(summed, ((0, 0), (0, pad_s))), jnp.pad(headed, ((0, 0), (0, pad_h)))], axis=1
        ).reshape(nctx, -1, 128)
        tail = jnp.sum(lax.all_to_all(tail, ctx, 0, 0), axis=0)
        cut = (n_summed + pad_s) // 128
        summed, headed = tail[:cut], tail[cut:].reshape(-1)
        summed = summed + swap(summed, "c")
        summed = (summed + swap(summed, "x")).reshape(-1)
        return (
            block_out,
            input_low.astype(f32),
            *joined,
            summed[: 2 * rl],
            summed[2 * rl : (2 + rank) * rl].reshape(rank, rl).T,
            summed[(2 + rank) * rl : n_summed],
            headed[: rank * dl].reshape(1, rank, dl),
            headed[rank * dl : n_headed].reshape(1, dl),
        )

    block_out, input_grad, g_gate, g_up, g_down, g_norms, g_rank, g_gain, g_decay, g_bias = finish()
    g_norm_in, g_norm_mid = g_norms[:rl], g_norms[rl:]
    g_query, g_key, g_value = call_widen(widen_rows, qkv_grad, [(rl, width), (rl, width), (rl, wide)])
    g_outgate, g_out = call_widen(widen_turned, go_grad, [(rl, wide), (wide, rl)])
    return (
        block_out,
        input_grad,
        g_norm_in,
        g_query,
        g_key,
        g_value,
        g_outgate,
        g_rank,
        g_decay,
        g_bias,
        g_gain,
        g_out,
        g_norm_mid,
        g_gate,
        g_up,
        g_down,
    )


def solution(mesh):
    ctx = mesh.shape["ctx"]
    shape = (NZ, ctx // NZ, 2, mesh.shape["head"] // 2)
    fine = Mesh(mesh.devices.reshape(shape), ("z", "y", "x", "c"))
    c, h = ("z", "y"), ("x", "c")
    in_specs = (
        P(None, c, None), P(None, c, None), P(), P(c), P(c, h), P(c, h), P(c, h), P(c, h), P(c, None),
        P(h, None, c), P(h, c), P(c), P(h, c), P(c), P(c, h), P(c, h), P(h, c),
    )
    out_specs = (
        P(None, c, None), P(None, c, None), P(c), P(c, h), P(c, h), P(c, h), P(c, h), P(c, None),
        P(h, None, c), P(h, c), P(c), P(h, c), P(c), P(c, h), P(c, h), P(h, c),
    )
    return jax.shard_map(
        per_device, mesh=fine, in_specs=in_specs, out_specs=out_specs, check_vma=False
    )
```

```python
import functools

import numpy as np

import jax
import jax.numpy as jnp
from jax import lax
from jax.experimental import pallas as pl
from jax.experimental.pallas import tpu as pltpu
from jax.sharding import Mesh
from jax.sharding import PartitionSpec as P

GROUP = 64
EPS = 1e-06
LEVELS = (32, 16, 8, 4, 2, 1)
f32 = jnp.float32
bf16 = jnp.bfloat16
NZ = 4


def dot(a, b, dims):
    return lax.dot_general(a, b, (dims, ((), ())), preferred_element_type=f32)


def nn(a, b):
    return dot(a, b, ((1,), (0,)))


def nt(a, b):
    return dot(a, b, ((1,), (1,)))


def tn(a, b):
    return dot(a, b, ((0,), (0,)))


def swap(x, axis):
    return lax.ppermute(x, axis, [(0, 1), (1, 0)])


def after(value, *earlier):
    anywhere = pl.BlockSpec(memory_space=pl.ANY)
    return pl.pallas_call(
        lambda *refs: None,
        in_specs=[anywhere] * (1 + len(earlier)),
        out_specs=anywhere,
        out_shape=jax.ShapeDtypeStruct(value.shape, value.dtype),
        input_output_aliases={0: 0},
        cost_estimate=pl.CostEstimate(flops=0, bytes_accessed=0, transcendentals=0),
        name="after",
    )(value, *earlier)


def as_one(runs, work):
    shapes = jax.eval_shape(work)
    return lax.cond(
        runs, work, lambda: jax.tree.map(lambda s: jnp.zeros(s.shape, s.dtype), shapes)
    )


def add_low(a, b):
    return (a.astype(f32) + b.astype(f32)).astype(bf16)


def both_in_order(piece, axis, dim):
    other = swap(piece, axis)
    first = lax.axis_index(axis) == 0
    return jnp.where(
        first, jnp.stack([piece, other], dim), jnp.stack([other, piece], dim)
    )


def silu(v):
    return v * jax.nn.sigmoid(v)


def silu_grad(v):
    sig = jax.nn.sigmoid(v)
    return sig * (1.0 + v * (1.0 - sig))


def inv_rms(v):
    return lax.rsqrt(jnp.mean(v * v, axis=-1, keepdims=True) + EPS)


def norm_back(h, r, gain, grad):
    scaled = gain * grad
    inner = jnp.mean(h * scaled, axis=-1, keepdims=True)
    return r * scaled - h * (r * r * r) * inner


def level_map(rows):
    t = np.arange(rows)[:, None]
    u = np.arange(rows)[None, :]
    out = np.zeros((rows, rows), np.int32)
    for at, half in enumerate(LEVELS):
        hit = (t // (2 * half) == u // (2 * half)) & ((t // half) % 2 == 1) & ((u // half) % 2 == 0)
        out[hit] = at + 1
    out[t == u] = len(LEVELS) + 1
    return out


def lower_map(rows):
    t = np.arange(rows)[:, None]
    u = np.arange(rows)[None, :]
    return ((t // GROUP == u // GROUP) & (t >= u)).astype(np.float32)


def ones_times(ones, value):
    hi = value.astype(bf16)
    rest = value - hi.astype(f32)
    mid = rest.astype(bf16)
    low = (rest - mid.astype(f32)).astype(bf16)
    return nn(ones, hi) + (nn(ones, mid) + nn(ones, low))


def level_decay(cum, half):
    rows, width = cum.shape
    span = max(2 * half, 8)
    parts = cum.reshape(rows // span, span, width)
    if half >= 4:
        mid = parts[:, half - 1 : half, :]
    else:
        at = lax.broadcasted_iota(jnp.int32, parts.shape, 1)
        mid = parts[:, half - 1 : half, :]
        for start in range(2 * half, span, 2 * half):
            mid = jnp.where(at >= start, parts[:, start + half - 1 : start + half, :], mid)
    return jnp.exp(-jnp.abs(parts - mid)).reshape(rows, width)


def block_of(array, at):
    return array[at * GROUP : (at + 1) * GROUP, :]


def scan_forward(qkv_ref, decay_ref, lower_ref, level_ref, open_ref, out_ref, query_ref, state_ref, keep_ref):
    step = pl.program_id(0)
    rows, width = decay_ref.shape
    count = rows // GROUP
    scale = width**-0.5
    queries = qkv_ref[:, :width].astype(f32) * scale
    keys = qkv_ref[:, width : 2 * width].astype(f32)
    values = qkv_ref[:, 2 * width :]
    levels = level_ref[...]
    cum = ones_times(lower_ref[...], decay_ref[...])
    scores = jnp.where(
        levels == len(LEVELS) + 1, nt(queries.astype(bf16), keys.astype(bf16)), 0.0
    )
    for at, half in enumerate(LEVELS):
        decay = level_decay(cum, half)
        part = nt((queries * decay).astype(bf16), (keys * decay).astype(bf16))
        scores = jnp.where(levels == at + 1, part, scores)
    local = nn(scores.astype(bf16), values)
    faded = queries * jnp.exp(cum)
    state = jnp.zeros((values.shape[1], width), f32)
    keep = jnp.ones((1, width), f32)
    for c in range(count):
        is_open = open_ref[step, c]
        state = state * is_open
        keep = keep * is_open
        faded_c = block_of(faded, c)
        cum_c = block_of(cum, c)
        last = cum_c[GROUP - 1 :, :]
        here = block_of(local, c)
        if c:
            here = here + nt(faded_c.astype(bf16), state.astype(bf16))
        out_ref[c * GROUP : (c + 1) * GROUP, :] = here
        query_ref[c * GROUP : (c + 1) * GROUP, :] = (faded_c * keep).astype(bf16)
        carried = (block_of(keys, c) * jnp.exp(last - cum_c)).astype(bf16)
        update = tn(block_of(values, c), carried)
        shrink = jnp.exp(last)
        state = state * shrink + update
        keep = keep * shrink
    state_ref[0] = state.astype(bf16)
    keep_ref[0] = jnp.broadcast_to(keep, keep_ref.shape[1:])


def scan_backward(qkv_ref, decay_ref, logit_ref, grad_ref, enter_ref, leave_ref, lower_ref, upper_ref, level_ref, open_ref, *rest):
    out_ref, logit_out_ref, local_ref, past_ref = rest[-4:]
    step = pl.program_id(0)
    rows, width = decay_ref.shape
    count = rows // GROUP
    scale = width**-0.5
    queries = qkv_ref[:, :width].astype(f32) * scale
    keys = qkv_ref[:, width : 2 * width].astype(f32)
    values = qkv_ref[:, 2 * width :]
    grads = grad_ref[...]
    levels = level_ref[...]
    cum = ones_times(lower_ref[...], decay_ref[...])
    pair_grad = nt(grads, values)
    on_diagonal = levels == len(LEVELS) + 1
    own = jnp.sum(jnp.where(on_diagonal, pair_grad, 0.0), axis=1, keepdims=True)
    scores = jnp.where(on_diagonal, nt(queries.astype(bf16), keys.astype(bf16)), 0.0)
    query_grad = jnp.zeros((rows, width), f32)
    key_grad = jnp.zeros((rows, width), f32)
    for at, half in enumerate(LEVELS):
        decay = level_decay(cum, half)
        query_l = (queries * decay).astype(bf16)
        key_l = (keys * decay).astype(bf16)
        hit = levels == at + 1
        scores = jnp.where(hit, nt(query_l, key_l), scores)
        grad_l = jnp.where(hit, pair_grad, 0.0).astype(bf16)
        query_grad = query_grad + nn(grad_l, key_l) * decay
        key_grad = key_grad + tn(grad_l, query_l) * decay
    value_grad = tn(scores.astype(bf16), grads)
    rising = jnp.exp(cum)
    faded = queries * rising
    state = enter_ref[0].astype(f32)
    for c in range(count):
        state = state * open_ref[step, c]
        past_ref[c] = state
        cum_c = block_of(cum, c)
        last = cum_c[GROUP - 1 :, :]
        if c < count - 1:
            carried = (block_of(keys, c) * jnp.exp(last - cum_c)).astype(bf16)
            state = state * jnp.exp(last) + tn(block_of(values, c), carried)
    after = leave_ref[0].astype(f32)
    for c in range(count - 1, -1, -1):
        span = slice(c * GROUP, (c + 1) * GROUP)
        past = past_ref[c]
        cum_c = block_of(cum, c)
        last = cum_c[GROUP - 1 :, :]
        shrink = jnp.exp(last)
        fading = jnp.exp(last - cum_c)
        keys_c = block_of(keys, c)
        queries_c = block_of(queries, c)
        grads_c = block_of(grads, c)
        after_low = after.astype(bf16)
        query_c = block_of(query_grad, c) + nn(grads_c, past.astype(bf16)) * block_of(rising, c)
        key_far = nn(block_of(values, c), after_low) * fading
        key_c = block_of(key_grad, c) + key_far
        value_c = block_of(value_grad, c) + nt((keys_c * fading).astype(bf16), after_low)
        own_c = block_of(own, c)
        out_ref[span, :width] = ((query_c + own_c * keys_c) * scale).astype(bf16)
        out_ref[span, width : 2 * width] = (key_c + own_c * queries_c).astype(bf16)
        out_ref[span, 2 * width :] = value_c.astype(bf16)
        local_ref[span, :] = queries_c * query_c - keys_c * key_c
        at_last = jnp.sum(keys_c * key_far, axis=0, keepdims=True) + shrink * jnp.sum(
            past * after, axis=0, keepdims=True
        )
        logit_out_ref[span, :] = jnp.broadcast_to(at_last, (GROUP, width))
        if c:
            after = (after * shrink + tn(grads_c, block_of(faded, c).astype(bf16))) * open_ref[step, c]
    decay_grad = ones_times(upper_ref[...], local_ref[...]) + logit_out_ref[...]
    logit_out_ref[...] = decay_grad * jax.nn.sigmoid(-logit_ref[...]) * (1.0 / 16.0)


def call_forward(qkv, decays, is_open, micro_count):
    rows = qkv.shape[0] // micro_count
    width = decays.shape[1]
    wide = qkv.shape[1] - 2 * width
    lower = jnp.asarray(lower_map(rows), bf16)
    level = jnp.asarray(level_map(rows))
    whole = lambda m: (0, 0)
    mine = lambda m: (m, 0)
    mine3 = lambda m: (m, 0, 0)
    return pl.pallas_call(
        scan_forward,
        grid=(micro_count,),
        in_specs=[
            pl.BlockSpec((rows, qkv.shape[1]), mine),
            pl.BlockSpec((rows, width), mine),
            pl.BlockSpec((rows, rows), whole),
            pl.BlockSpec((rows, rows), whole),
            pl.BlockSpec(memory_space=pltpu.SMEM),
        ],
        out_specs=[
            pl.BlockSpec((rows, wide), mine),
            pl.BlockSpec((rows, width), mine),
            pl.BlockSpec((1, wide, width), mine3),
            pl.BlockSpec((1, 8, width), mine3),
        ],
        out_shape=[
            jax.ShapeDtypeStruct((micro_count * rows, wide), f32),
            jax.ShapeDtypeStruct((micro_count * rows, width), bf16),
            jax.ShapeDtypeStruct((micro_count, wide, width), bf16),
            jax.ShapeDtypeStruct((micro_count, 8, width), f32),
        ],
        compiler_params=pltpu.CompilerParams(vmem_limit_bytes=40 * 2**20),
        cost_estimate=pl.CostEstimate(flops=2_000_000_000, bytes_accessed=8_000_000, transcendentals=1_500_000),
        name="scan_forward",
    )(qkv, decays, lower, level, is_open)


def call_backward(qkv, decays, logits, grads, enter, leave, is_open, micro_count, *earlier):
    rows = qkv.shape[0] // micro_count
    width = decays.shape[1]
    wide = qkv.shape[1] - 2 * width
    lower = jnp.asarray(lower_map(rows), bf16)
    upper = jnp.asarray(lower_map(rows).T, bf16)
    level = jnp.asarray(level_map(rows))
    whole = lambda m: (0, 0)
    mine = lambda m: (m, 0)
    mine3 = lambda m: (m, 0, 0)
    return pl.pallas_call(
        scan_backward,
        grid=(micro_count,),
        in_specs=[
            pl.BlockSpec((rows, qkv.shape[1]), mine),
            pl.BlockSpec((rows, width), mine),
            pl.BlockSpec((rows, width), mine),
            pl.BlockSpec((rows, wide), mine),
            pl.BlockSpec((1, wide, width), mine3),
            pl.BlockSpec((1, wide, width), mine3),
            pl.BlockSpec((rows, rows), whole),
            pl.BlockSpec((rows, rows), whole),
            pl.BlockSpec((rows, rows), whole),
            pl.BlockSpec(memory_space=pltpu.SMEM),
        ]
        + [pl.BlockSpec(memory_space=pl.ANY)] * len(earlier),
        out_specs=[
            pl.BlockSpec((rows, qkv.shape[1]), mine),
            pl.BlockSpec((rows, width), mine),
        ],
        out_shape=[
            jax.ShapeDtypeStruct((micro_count * rows, qkv.shape[1]), bf16),
            jax.ShapeDtypeStruct((micro_count * rows, width), f32),
        ],
        scratch_shapes=[
            pltpu.VMEM((rows, width), f32),
            pltpu.VMEM((rows // GROUP, wide, width), f32),
        ],
        compiler_params=pltpu.CompilerParams(vmem_limit_bytes=40 * 2**20),
        cost_estimate=pl.CostEstimate(flops=5_000_000_000, bytes_accessed=12_000_000, transcendentals=1_500_000),
        name="scan_backward",
    )(qkv, decays, logits, grads, enter, leave, lower, upper, level, is_open, *earlier)


def scan_states(got_ref, out_ref, *, micro, strip, reverse):
    count = got_ref.shape[0]
    width = got_ref.shape[2]
    running = [jnp.zeros((strip, width), f32) for _ in range(micro)]
    order = range(count - 1, -1, -1) if reverse else range(count)
    for at in order:
        tail = got_ref[at, micro * strip :, :].astype(f32)
        for m in range(micro):
            span = slice(m * strip, (m + 1) * strip)
            out_ref[at, span, :] = running[m].astype(bf16)
            keep = tail[m : m + 1, :] + tail[micro + m : micro + m + 1, :]
            running[m] = running[m] * keep + got_ref[at, span, :].astype(f32)


def spread_states(state, keep, reverse):
    ctx = ("z", "y")
    count = lax.axis_size(ctx)
    micro, wide, width = state.shape
    strip = wide // count
    parts = state.reshape(micro, count, strip, width).transpose(1, 0, 2, 3)
    parts = parts.reshape(count, micro * strip, width)
    keep_hi = keep.astype(bf16)
    keep_lo = (keep - keep_hi.astype(f32)).astype(bf16)
    extra = jnp.concatenate([keep_hi, keep_lo, jnp.zeros((16 - 2 * micro, width), bf16)])
    sent = jnp.concatenate(
        [parts, jnp.broadcast_to(extra[None], (count, 16, width))], axis=1
    )
    got = lax.all_to_all(sent, ctx, 0, 0)
    return pl.pallas_call(
        functools.partial(scan_states, micro=micro, strip=strip, reverse=reverse),
        out_shape=jax.ShapeDtypeStruct((count, micro * strip, width), bf16),
        compiler_params=pltpu.CompilerParams(vmem_limit_bytes=16 * 2**20),
        cost_estimate=pl.CostEstimate(flops=2_000_000, bytes_accessed=1_100_000, transcendentals=0),
        name="scan_states",
    )(got)


def collect_states(entering, micro):
    count, _, width = entering.shape
    strip = entering.shape[1] // micro
    back = lax.all_to_all(entering, ("z", "y"), 0, 0)
    return back.reshape(count, micro, strip, width).transpose(1, 0, 2, 3).reshape(micro, -1, width)


def feed_kernel(mid_ref, low_ref, weight_ref, *rest, units):
    pair_ref, hidden_ref, grad_ref = rest[-3:]
    both = nn(mid_ref[...], weight_ref[:, : 2 * units])
    gate, up = both[:, :units], both[:, units:]
    back = nn(low_ref[...], weight_ref[:, 2 * units :])
    sig = jax.nn.sigmoid(gate)
    act = gate * sig
    hidden_ref[...] = (act * up).astype(bf16)
    pair_ref[:, :units] = (back * up * (sig * (1.0 + gate * (1.0 - sig)))).astype(bf16)
    pair_ref[:, units:] = (back * act).astype(bf16)
    grad_ref[...] = nt(pair_ref[...], weight_ref[:, : 2 * units]).astype(bf16)


def call_feed(plane_mid, plane_low, weight, units, *earlier):
    rows, depth = plane_mid.shape
    tile = 256
    return pl.pallas_call(
        functools.partial(feed_kernel, units=units),
        grid=(rows // tile,),
        in_specs=[
            pl.BlockSpec((tile, depth), lambda i: (i, 0)),
            pl.BlockSpec((tile, depth), lambda i: (i, 0)),
            pl.BlockSpec(weight.shape, lambda i: (0, 0), pipeline_mode=pl.Buffered(1)),
        ]
        + [pl.BlockSpec(memory_space=pl.ANY)] * len(earlier),
        out_specs=[
            pl.BlockSpec((tile, 2 * units), lambda i: (i, 0)),
            pl.BlockSpec((tile, units), lambda i: (i, 0)),
            pl.BlockSpec((tile, depth), lambda i: (i, 0)),
        ],
        out_shape=[
            jax.ShapeDtypeStruct((rows, 2 * units), bf16),
            jax.ShapeDtypeStruct((rows, units), bf16),
            jax.ShapeDtypeStruct((rows, depth), bf16),
        ],
        compiler_params=pltpu.CompilerParams(vmem_limit_bytes=48 * 2**20),
        cost_estimate=pl.CostEstimate(
            flops=10 * rows * depth * units, bytes_accessed=28_000_000, transcendentals=rows * units
        ),
        name="feed_forward",
    )(plane_mid, plane_low, weight, *earlier)


def split_units(gate_ref, up_ref, down_ref, out_ref):
    parts, rows, width = out_ref.shape
    units = width // 3
    for k in range(parts):
        span = slice(k * units, (k + 1) * units)
        out_ref[k, :, :units] = gate_ref[:, span]
        out_ref[k, :, units : 2 * units] = up_ref[:, span]
        out_ref[k, :, 2 * units :] = down_ref[span, :].astype(f32).T.astype(bf16)


def call_split(w_gate, w_up, w_down, parts):
    rows, ff = w_gate.shape
    return pl.pallas_call(
        split_units,
        out_shape=jax.ShapeDtypeStruct((parts, rows, 3 * ff // parts), bf16),
        compiler_params=pltpu.CompilerParams(vmem_limit_bytes=32 * 2**20),
        cost_estimate=pl.CostEstimate(flops=0, bytes_accessed=12 * rows * ff, transcendentals=0),
        name="split_units",
    )(w_gate, w_up, w_down)


def join_units(in_ref, gate_ref, up_ref, down_ref):
    parts, rows, width = in_ref.shape
    units = width // 3
    for k in range(parts):
        span = slice(k * units, (k + 1) * units)
        gate_ref[:, span] = in_ref[k, :, :units].astype(f32)
        up_ref[:, span] = in_ref[k, :, units : 2 * units].astype(f32)
        down_ref[span, :] = in_ref[k, :, 2 * units :].astype(f32).T


def call_join(pieces):
    parts, rows, width = pieces.shape
    ff = width // 3 * parts
    return pl.pallas_call(
        join_units,
        out_shape=[
            jax.ShapeDtypeStruct((rows, ff), f32),
            jax.ShapeDtypeStruct((rows, ff), f32),
            jax.ShapeDtypeStruct((ff, rows), f32),
        ],
        compiler_params=pltpu.CompilerParams(vmem_limit_bytes=32 * 2**20),
        cost_estimate=pl.CostEstimate(flops=0, bytes_accessed=18 * rows * ff, transcendentals=0),
        name="join_units",
    )(pieces)


def pick_rows(at_ref, in_ref, out_ref):
    out_ref[:, : in_ref.shape[2]] = in_ref[0]


def call_pick(pieces, at):
    _, rows, width = pieces.shape
    full = width + -width % 128
    return pl.pallas_call(
        pick_rows,
        grid_spec=pltpu.PrefetchScalarGridSpec(
            num_scalar_prefetch=1,
            grid=(1,),
            in_specs=[pl.BlockSpec((1, rows, width), lambda i, at: (at[0], 0, 0))],
            out_specs=pl.BlockSpec((rows, full), lambda i, at: (0, 0)),
        ),
        out_shape=jax.ShapeDtypeStruct((rows, full), pieces.dtype),
        compiler_params=pltpu.CompilerParams(vmem_limit_bytes=16 * 2**20),
        cost_estimate=pl.CostEstimate(flops=0, bytes_accessed=4 * rows * width, transcendentals=0),
        name="pick_rows",
    )(at.reshape(1), pieces)


def join_two(at_ref, own_ref, got_ref, gate_ref, up_ref, down_ref):
    units = own_ref.shape[2] // 3
    first = at_ref[0] == 0
    for k in range(2):
        mine = jnp.logical_xor(first, k == 1)
        span = slice(k * units, (k + 1) * units)

        @pl.when(mine)
        def _():
            value = own_ref[0].astype(f32)
            gate_ref[:, span] = value[:, :units]
            up_ref[:, span] = value[:, units : 2 * units]
            down_ref[span, :] = value[:, 2 * units : 3 * units].T

        @pl.when(jnp.logical_not(mine))
        def _():
            value = got_ref[...].astype(f32)
            gate_ref[:, span] = value[:, :units]
            up_ref[:, span] = value[:, units : 2 * units]
            down_ref[span, :] = value[:, 2 * units : 3 * units].T


def call_join_two(pieces, got, at):
    _, rows, width = pieces.shape
    ff = width // 3 * 2
    return pl.pallas_call(
        join_two,
        grid_spec=pltpu.PrefetchScalarGridSpec(
            num_scalar_prefetch=1,
            grid=(1,),
            in_specs=[
                pl.BlockSpec((1, rows, width), lambda i, at: (at[0], 0, 0)),
                pl.BlockSpec(got.shape, lambda i, at: (0, 0)),
            ],
            out_specs=[
                pl.BlockSpec((rows, ff), lambda i, at: (0, 0)),
                pl.BlockSpec((rows, ff), lambda i, at: (0, 0)),
                pl.BlockSpec((ff, rows), lambda i, at: (0, 0)),
            ],
        ),
        out_shape=[
            jax.ShapeDtypeStruct((rows, ff), f32),
            jax.ShapeDtypeStruct((rows, ff), f32),
            jax.ShapeDtypeStruct((ff, rows), f32),
        ],
        compiler_params=pltpu.CompilerParams(vmem_limit_bytes=32 * 2**20),
        cost_estimate=pl.CostEstimate(flops=0, bytes_accessed=18 * rows * ff, transcendentals=0),
        name="join_two",
    )(at.reshape(1), pieces, got)


def widen_rows(in_ref, query_ref, key_ref, value_ref):
    width = query_ref.shape[1]
    query_ref[...] = in_ref[:, :width].astype(f32)
    key_ref[...] = in_ref[:, width : 2 * width].astype(f32)
    value_ref[...] = in_ref[:, 2 * width :].astype(f32)


def widen_turned(in_ref, gate_ref, out_ref):
    wide = gate_ref.shape[1]
    gate_ref[...] = in_ref[:, :wide].astype(f32)
    out_ref[...] = in_ref[:, wide:].astype(f32).T


def call_widen(kernel, value, shapes):
    return pl.pallas_call(
        kernel,
        out_shape=[jax.ShapeDtypeStruct(shape, f32) for shape in shapes],
        compiler_params=pltpu.CompilerParams(vmem_limit_bytes=16 * 2**20),
        cost_estimate=pl.CostEstimate(flops=0, bytes_accessed=6 * value.size, transcendentals=0),
        name="widen",
    )(value)


def feed_grad_kernel(*refs):
    out_ref = refs[-1]
    two = refs[2].shape[1]
    mid_a, low_a, pair_a, hidden_a, mid_b, low_b, pair_b, hidden_b = (r[...] for r in refs[:8])
    out_ref[:, :two] = (tn(mid_a, pair_a) + tn(mid_b, pair_b)).astype(bf16)
    out_ref[:, two:] = (tn(low_a, hidden_a) + tn(low_b, hidden_b)).astype(bf16)


def call_feed_grad(near, far, *earlier):
    rows, depth = near[0].shape
    two, units = near[2].shape[1], near[3].shape[1]
    tile = 256
    one = [
        pl.BlockSpec((rows, tile), lambda i: (0, i)),
        pl.BlockSpec((rows, tile), lambda i: (0, i)),
        pl.BlockSpec((rows, two), lambda i: (0, 0), pipeline_mode=pl.Buffered(1)),
        pl.BlockSpec((rows, units), lambda i: (0, 0), pipeline_mode=pl.Buffered(1)),
    ]
    return pl.pallas_call(
        feed_grad_kernel,
        grid=(depth // tile,),
        in_specs=one + one + [pl.BlockSpec(memory_space=pl.ANY)] * len(earlier),
        out_specs=pl.BlockSpec((tile, two + units), lambda i: (i, 0)),
        out_shape=jax.ShapeDtypeStruct((depth, two + units), bf16),
        compiler_params=pltpu.CompilerParams(vmem_limit_bytes=48 * 2**20),
        cost_estimate=pl.CostEstimate(
            flops=4 * rows * depth * (two + units), bytes_accessed=21_000_000, transcendentals=0
        ),
        name="feed_grad",
    )(*near, *far, *earlier)


def gather_plane(piece):
    count = lax.axis_size("y")
    if count == 2:
        a, b = piece[0], piece[1]
        a_y, b_x = swap(a, "y"), swap(b, "x")
        a, b = jnp.stack([a, a_y]), jnp.stack([b, b_x])
        a_x, b_y = swap(a, "x"), swap(b, "y")
        here = jnp.concatenate([a, a_x, b, b_y])
    else:
        rows = [piece]
        for k in range(1, count):
            rows.append(lax.ppermute(piece, "y", [((i + k) % count, i) for i in range(count)]))
        here = jnp.stack(rows, axis=1)
        here = jnp.stack([here, swap(here, "x")], axis=1)
        here = here.reshape((-1,) + piece.shape[1:])
    here = here.reshape(-1, piece.shape[-1])
    return here, swap(here, "c")


def scatter_first(here, micro, quarter):
    count = lax.axis_size("y")
    depth = here.shape[-1]
    if count == 2:
        here = here.reshape(2, 2, 2 * quarter, depth)
        a, b = here[0], here[1]
        a_got, b_got = swap(a[1], "x"), swap(b[1], "y")
        return add_low(a[0], a_got), add_low(b[0], b_got)
    here = here.reshape(micro, 2, count, quarter, depth)
    here = add_low(here[:, 0], swap(here[:, 1], "x"))
    return here[:, :1], here[:, 1:]


def scatter_second(a, b, quarter):
    count = lax.axis_size("y")
    if count == 2:
        a, b = (v.reshape(2, quarter, -1) for v in (a, b))
        a_got, b_got = swap(a[1], "y"), swap(b[1], "x")
        a = a[0].astype(f32) + a_got.astype(f32)
        b = b[0].astype(f32) + b_got.astype(f32)
        return jnp.stack([a, b])
    total = a[:, 0].astype(f32)
    for k in range(1, count):
        got = lax.ppermute(b[:, k - 1], "y", [(i, (i + k) % count) for i in range(count)])
        total = total + got.astype(f32)
    return total


def scatter_head(part):
    micro, slots, width = part.shape
    c, x = lax.axis_index("c"), lax.axis_index("x")
    view = part.reshape(micro, 2, slots // 2, width)
    mine = lax.dynamic_index_in_dim(view, c, 1, keepdims=False)
    other = lax.dynamic_index_in_dim(view, 1 - c, 1, keepdims=False)
    mine = add_low(mine, swap(other, "c"))
    view = mine.reshape(micro, 2, slots // 4, width)
    mine = lax.dynamic_index_in_dim(view, x, 1, keepdims=False)
    other = lax.dynamic_index_in_dim(view, 1 - x, 1, keepdims=False)
    return mine.astype(f32) + swap(other, "x").astype(f32)


def gather_head(piece):
    micro, quarter, width = piece.shape
    both = both_in_order(piece, "x", 1)
    both = both_in_order(both, "c", 1)
    return both.reshape(micro, 4 * quarter, width)


def own_quarter(array):
    micro, slots, width = array.shape
    c, x = lax.axis_index("c"), lax.axis_index("x")
    view = array.reshape(micro, 4, slots // 4, width)
    return lax.dynamic_index_in_dim(view, 2 * c + x, 1, keepdims=False)


def others_y(piece):
    count = lax.axis_size("y")
    out = [piece]
    for k in range(1, count):
        out.append(lax.ppermute(piece, "y", [((i + k) % count, i) for i in range(count)]))
    return out


def to_relative(array):
    count, y = lax.axis_size("y"), lax.axis_index("y")
    t, depth = array.shape
    rl = depth // (NZ * count)
    if count == 2:
        even = jnp.concatenate([array[:, 2 * z * rl : (2 * z + 1) * rl] for z in range(NZ)], axis=1)
        odd = jnp.concatenate([array[:, (2 * z + 1) * rl : (2 * z + 2) * rl] for z in range(NZ)], axis=1)
        first = y == 0
        return jnp.concatenate([jnp.where(first, even, odd), jnp.where(first, odd, even)], axis=1)
    view = jnp.roll(array.reshape(t, NZ, count, rl), -y, axis=2)
    return view.transpose(0, 2, 1, 3).reshape(t, depth)


def to_absolute(array):
    count, y = lax.axis_size("y"), lax.axis_index("y")
    t, depth = array.shape
    rl = depth // (NZ * count)
    if count == 2:
        first = y == 0
        out = []
        for z in range(NZ):
            own = array[:, z * rl : (z + 1) * rl]
            other = array[:, (NZ + z) * rl : (NZ + z + 1) * rl]
            out += [jnp.where(first, own, other), jnp.where(first, other, own)]
        return jnp.concatenate(out, axis=1)
    view = array.reshape(t, count, NZ, rl).transpose(0, 2, 1, 3)
    return jnp.roll(view, y, axis=2).reshape(t, depth)


def vector_by_ctx(value):
    count, y = lax.axis_size("y"), lax.axis_index("y")
    view = value.reshape(value.shape[0], count, NZ, -1)
    if count == 2:
        view = jnp.where(y == 0, view, view[:, ::-1])
    else:
        view = jnp.roll(view, y, axis=1)
    return view.transpose(2, 1, 0, 3).reshape(NZ * count, value.shape[0], -1)


def vector_from_ctx(value):
    count, y = lax.axis_size("y"), lax.axis_index("y")
    view = value.reshape((NZ, count) + value.shape[1:]).transpose(2, 1, 0, 3)
    if count == 2:
        view = jnp.where(y == 0, view, view[:, ::-1])
    else:
        view = jnp.roll(view, -y, axis=1)
    return view.reshape(value.shape[1], -1)


def sum_y(parts, *between):
    count = lax.axis_size("y")
    total = (after(parts[0], *between) if between else parts[0]).astype(f32)
    for k in range(1, count):
        got = lax.ppermute(parts[k], "y", [(i, (i + k) % count) for i in range(count)])
        total = total + got.astype(f32)
    return total.astype(bf16)


def reduce_z(part):
    return lax.psum_scatter(part, "z", scatter_dimension=0, tiled=True)


def per_device(
    tokens, cotangent, lengths, norm_in, w_query, w_key, w_value, w_outgate, w_rank,
    w_decay, decay_bias, head_gain, w_out, norm_mid, w_gate, w_up, w_down,
):
    ctx = ("z", "y")
    ny = lax.axis_size("y")
    nctx = NZ * ny
    y = lax.axis_index("y")
    place = lax.axis_index(ctx)
    micro, slots, depth = tokens.shape
    groups = slots // GROUP
    rl = w_query.shape[0]
    width = w_query.shape[1]
    wide = w_value.shape[1]
    rank = w_rank.shape[1]
    ff = w_gate.shape[1]
    fl = ff // ny
    total = micro * slots

    w_qkv = jnp.concatenate([w_query, w_key, w_value], axis=1)
    qkv_rows = lax.all_gather(w_qkv, "z", axis=0, tiled=True)
    w_go = jnp.concatenate([w_outgate, w_out.T], axis=1)
    go_rows = lax.all_gather(w_go, "z", axis=0, tiled=True)

    small = jnp.concatenate(
        [norm_in, norm_mid, w_rank.T.reshape(-1), w_decay[0].reshape(-1), decay_bias[0], head_gain]
    )
    n_small = small.shape[0]
    pad = -n_small % 1024
    small = jnp.pad(small, (0, pad)).reshape(1, -1, 128)
    small = jnp.broadcast_to(small, (nctx,) + small.shape[1:])
    small = lax.all_to_all(small, ctx, 0, 0).reshape(nctx, -1)
    at = 0

    def take(size):
        nonlocal at
        at += size
        return small[:, at - size : at]

    by_row = vector_from_ctx(take((2 + rank) * rl).reshape(nctx, 2 + rank, rl))
    gain_in = by_row[:1].astype(f32)
    gain_mid = by_row[1:2].astype(f32)
    rank_t = by_row[2:]
    dl = width // nctx
    decay_w = take(rank * dl).reshape(nctx, rank, dl).transpose(1, 0, 2).reshape(rank, width)
    bias = take(dl).reshape(1, width).astype(f32)
    gain_head = take(wide // nctx).reshape(1, wide).astype(f32)

    ff_local = call_split(w_gate, w_up, w_down, ny)
    own = lax.dynamic_index_in_dim(ff_local, y, 0, keepdims=False)
    if ny == 2:
        got = swap(lax.dynamic_index_in_dim(ff_local, 1 - y, 0, keepdims=False), "y")
        ff_unit = jnp.where(y == 0, jnp.stack([own, got]), jnp.stack([got, own]))
    else:
        pieces = [own]
        for k in range(1, ny):
            sent = lax.dynamic_index_in_dim(ff_local, lax.rem(y + ny - k, ny), 0, keepdims=False)
            pieces.append(lax.ppermute(sent, "y", [((i + k) % ny, i) for i in range(ny)]))
        ff_unit = jnp.roll(jnp.stack(pieces), y, axis=0)
    ff_unit = ff_unit.reshape(ny * rl, 3 * fl)

    group_ids = place * groups + jnp.arange(groups, dtype=jnp.int32)
    end = jnp.zeros((micro, 1), jnp.int32)
    reset = group_ids[None, :] == end
    for i in range(lengths.shape[1]):
        end = end + lengths[:, i : i + 1]
        reset = reset | (group_ids[None, :] == end)
    is_open = 1.0 - reset.astype(f32)

    def mask_of(at):
        slot_ids = at * slots + jnp.arange(slots, dtype=jnp.int32)
        return (slot_ids[None, :] < end * GROUP).astype(bf16)[:, :, None]

    c_at, x_at = lax.axis_index("c"), lax.axis_index("x")
    quarter = slots // 4
    view = cotangent.reshape(micro, 2, slots // 2, depth)
    half_parts = others_y(lax.dynamic_index_in_dim(view, c_at, 1, keepdims=False))

    ff_full = lax.all_gather(ff_unit, "z", axis=0, tiled=True)
    qkv_parts = others_y(qkv_rows)
    go_parts = others_y(go_rows)

    inputs = to_relative(tokens.reshape(total, depth)).astype(f32)
    r_in = inv_rms(inputs)
    normed_in = (inputs * r_in * gain_in).astype(bf16)
    step = depth // ny
    low_rank = nt(normed_in, rank_t).astype(bf16)
    logits = nn(low_rank, decay_w) + bias
    decays = jax.nn.log_sigmoid(logits) / 16.0

    def columns(array, k):
        return array[:, k * step : (k + 1) * step]

    qkv = sum(nn(columns(normed_in, k), w) for k, w in enumerate(qkv_parts)).astype(bf16)

    runs = lengths[0, 0] >= 1

    def recurrence():
        local_out, far_query, state, keep = call_forward(qkv, decays, is_open, micro)
        keep = keep[:, 0, :]
        return local_out, far_query, collect_states(spread_states(state, keep, False), micro), keep

    local_out, far_query, enter, keep = as_one(runs, recurrence)

    out_low = cotangent * mask_of(place)
    low_parts = []
    for k, half in enumerate(half_parts):
        mask = mask_of(place - y + lax.rem(y + k, ny)).reshape(micro, 2, slots // 2, 1)
        mask = lax.dynamic_index_in_dim(mask, c_at, 1, keepdims=False)
        half = (half * mask).reshape(micro, 2, quarter, depth)
        low_parts.append(jnp.where(x_at == 0, half, half[:, ::-1]))
    if ny == 2:
        low_near = [
            jnp.stack([p[0] for p in low_parts], 1),
            jnp.stack([p[1] for p in low_parts], 0),
        ]
        low_near = jnp.stack(low_near).reshape(-1, depth)
    else:
        low_near = jnp.stack(low_parts, 2).reshape(-1, depth)
    low_far = swap(low_near, "c")

    outgate = sum(nn(columns(normed_in, k), w[:, :wide]) for k, w in enumerate(go_parts))
    outgate = outgate.astype(bf16).astype(f32)
    mixed = local_out + jnp.concatenate(
        [nt(far_query[m * slots : (m + 1) * slots], enter[m]) for m in range(micro)]
    )
    r_head = inv_rms(mixed)
    gated = (mixed * r_head * gain_head * silu(outgate)).astype(bf16)
    attention = jnp.concatenate([nt(gated, w[:, wide:]) for w in go_parts], axis=1)
    attention = scatter_head(attention.astype(bf16).reshape(micro, slots, depth))
    inputs_own = to_relative(own_quarter(tokens).reshape(-1, depth)).astype(f32)
    residual = inputs_own + attention.reshape(micro * quarter, depth)

    r_mid = inv_rms(residual)
    normed_mid = to_absolute((residual * r_mid * gain_mid).astype(bf16))
    mid_near, mid_far = gather_plane(normed_mid.reshape(micro, quarter, depth))
    out_grad = to_relative(own_quarter(out_low).reshape(-1, depth)).astype(f32)
    pair_far, hidden_far, part_far = call_feed(mid_far, low_far, ff_full, fl, out_grad)
    pair_near, hidden_near, part_near = call_feed(mid_near, low_near, ff_full, fl, part_far)
    mid_part = add_low(part_near, swap(part_far, "c"))
    def feed_back():
        ff_part = call_feed_grad(
            (mid_near, low_near, pair_near, hidden_near),
            (mid_far, low_far, pair_far, hidden_far),
        )
        return ff_part, *scatter_first(mid_part, micro, quarter)

    ff_part, mid_a, mid_b = as_one(runs, feed_back)
    ff_grad = reduce_z(ff_part)

    def feed_part(hidden):
        return nt(hidden, ff_full[:, 2 * fl :]).astype(bf16)

    def blocks_back():
        mid_grad = to_relative(scatter_second(mid_a, mid_b, quarter).reshape(-1, depth))

        resid_grad = out_grad + norm_back(residual, r_mid, gain_mid, mid_grad)
        grad_norm_mid = jnp.sum(mid_grad * residual * r_mid, axis=0)
        resid_low = gather_head(resid_grad.astype(bf16).reshape(micro, quarter, depth))
        resid_low = resid_low.reshape(total, depth)
        gated_grad = sum(nn(columns(resid_low, k), w[:, wide:]) for k, w in enumerate(go_parts))

        unit = mixed * r_head
        gate_act = silu(outgate)
        unit_grad = gated_grad * gate_act
        outgate_low = (gated_grad * unit * gain_head * silu_grad(outgate)).astype(bf16)
        mixed_grad = norm_back(mixed, r_head, gain_head, unit_grad).astype(bf16)
        grad_gain = jnp.sum(unit_grad * unit, axis=0)
        state_grad = jnp.stack(
            [
                tn(mixed_grad[m * slots : (m + 1) * slots], far_query[m * slots : (m + 1) * slots])
                for m in range(micro)
            ]
        ).astype(bf16)
        entering = spread_states(state_grad, keep, True)
        leave = collect_states(entering, micro)
        go_grads = [
            jnp.concatenate(
                [tn(columns(normed_in, k), outgate_low), tn(columns(resid_low, k), gated)], axis=1
            ).astype(bf16)
            for k in range(ny)
        ]
        go_rows_grad = sum_y(go_grads[:1] + [after(g, entering) for g in go_grads[1:]])
        feed_far = swap(feed_part(after(hidden_far, mixed_grad)), "c")
        feed_rows = add_low(feed_part(after(hidden_near, mixed_grad)), feed_far)
        feed = scatter_second(*scatter_first(feed_rows, micro, quarter), quarter)
        qkv_low, logit_grad = call_backward(
            qkv, decays, logits, mixed_grad, enter, leave, is_open, micro
        )
        logit_low = logit_grad.astype(bf16)
        qkv_grads = [tn(columns(normed_in, k), qkv_low).astype(bf16) for k in range(ny)]
        rank_part = nt(logit_low, decay_w).astype(bf16)
        rank_pad = jnp.pad(rank_part, ((0, 0), (0, 128 - rank)))
        qkv_later = after(qkv_low, *qkv_grads)
        in_part = [
            (nt(qkv_later, wq) + nt(outgate_low, wg[:, :wide])).astype(bf16)
            for wq, wg in zip(qkv_parts, go_parts)
        ]
        in_part = jnp.concatenate(in_part + [rank_pad], axis=1).reshape(micro, slots, depth + 128)
        return resid_grad, grad_norm_mid, grad_gain, go_rows_grad, qkv_grads, in_part, logit_low, feed

    resid_grad, grad_norm_mid, grad_gain, go_rows_grad, qkv_grads, in_part, logit_low, feed = as_one(
        runs, blocks_back
    )
    go_grad = reduce_z(go_rows_grad)

    def input_back():
        in_sum = scatter_head(in_part).reshape(-1, depth + 128)
        rank_low = in_sum[:, depth : depth + rank].astype(bf16)
        in_grad = in_sum[:, :depth] + nn(rank_low, rank_t)
        r_own = inv_rms(inputs_own)
        input_own = resid_grad + norm_back(inputs_own, r_own, gain_in, in_grad)
        grad_norm_in = jnp.sum(in_grad * inputs_own * r_own, axis=0)
        normed_own = own_quarter(normed_in.reshape(micro, slots, depth)).reshape(-1, depth)
        grad_rank_t = tn(rank_low, normed_own)
        grad_rows = jnp.concatenate([grad_norm_in[None], grad_norm_mid[None], grad_rank_t])
        input_own = to_absolute(input_own.astype(bf16))
        input_low = gather_head(input_own.reshape(micro, quarter, depth))
        return sum_y(qkv_grads), grad_rows, input_low

    qkv_rows_grad, grad_rows, input_low = input_back()
    qkv_rows_grad = after(qkv_rows_grad, ff_grad)
    qkv_grad = reduce_z(qkv_rows_grad)

    by_ctx = lambda v: v.reshape(nctx, -1)
    across = lambda v, n: v.reshape(v.shape[0], nctx, n).transpose(1, 0, 2).reshape(nctx, -1)

    def finish():
        ff_rows = after(ff_grad, qkv_rows_grad).reshape(ny, rl, 3 * fl)
        if ny == 2:
            joined = call_join_two(ff_rows, swap(call_pick(ff_rows, 1 - y), "y"), y)
        else:
            pieces = jnp.zeros((ny, rl, 3 * fl), bf16)
            pieces = lax.dynamic_update_slice_in_dim(
                pieces, lax.dynamic_index_in_dim(ff_rows, y, 0), y, 0
            )
            for k in range(1, ny):
                sent = lax.dynamic_index_in_dim(ff_rows, lax.rem(y + k, ny), 0)
                got = lax.ppermute(sent, "y", [(i, (i + k) % ny) for i in range(ny)])
                pieces = lax.dynamic_update_slice_in_dim(pieces, got, lax.rem(y - k + ny, ny), 0)
            joined = call_join(pieces)
        block_own = to_absolute((residual + to_relative(feed.reshape(-1, depth))).astype(bf16))
        block_out = gather_head(block_own.reshape(micro, quarter, depth))
        grad_decay = tn(low_rank, logit_low)
        grad_bias = jnp.sum(logit_low.astype(f32), axis=0)
        summed = jnp.concatenate(
            [vector_by_ctx(grad_rows).reshape(nctx, -1), by_ctx(grad_gain)], axis=1
        )
        headed = jnp.concatenate([across(grad_decay, dl), by_ctx(grad_bias)], axis=1)
        n_summed, n_headed = summed.shape[1], headed.shape[1]
        pad_s, pad_h = -n_summed % 1024, -n_headed % 1024
        tail = jnp.concatenate(
            [jnp.pad(summed, ((0, 0), (0, pad_s))), jnp.pad(headed, ((0, 0), (0, pad_h)))], axis=1
        ).reshape(nctx, -1, 128)
        tail = jnp.sum(lax.all_to_all(tail, ctx, 0, 0), axis=0)
        cut = (n_summed + pad_s) // 128
        summed, headed = tail[:cut], tail[cut:].reshape(-1)
        summed = summed + swap(summed, "c")
        summed = (summed + swap(summed, "x")).reshape(-1)
        return (
            block_out,
            input_low.astype(f32),
            *joined,
            summed[: 2 * rl],
            summed[2 * rl : (2 + rank) * rl].reshape(rank, rl).T,
            summed[(2 + rank) * rl : n_summed],
            headed[: rank * dl].reshape(1, rank, dl),
            headed[rank * dl : n_headed].reshape(1, dl),
        )

    block_out, input_grad, g_gate, g_up, g_down, g_norms, g_rank, g_gain, g_decay, g_bias = finish()
    g_norm_in, g_norm_mid = g_norms[:rl], g_norms[rl:]
    g_query, g_key, g_value = call_widen(widen_rows, qkv_grad, [(rl, width), (rl, width), (rl, wide)])
    g_outgate, g_out = call_widen(widen_turned, go_grad, [(rl, wide), (wide, rl)])
    return (
        block_out,
        input_grad,
        g_norm_in,
        g_query,
        g_key,
        g_value,
        g_outgate,
        g_rank,
        g_decay,
        g_bias,
        g_gain,
        g_out,
        g_norm_mid,
        g_gate,
        g_up,
        g_down,
    )


def solution(mesh):
    ctx = mesh.shape["ctx"]
    shape = (NZ, ctx // NZ, 2, mesh.shape["head"] // 2)
    fine = Mesh(mesh.devices.reshape(shape), ("z", "y", "x", "c"))
    c, h = ("z", "y"), ("x", "c")
    in_specs = (
        P(None, c, None), P(None, c, None), P(), P(c), P(c, h), P(c, h), P(c, h), P(c, h), P(c, None),
        P(h, None, c), P(h, c), P(c), P(h, c), P(c), P(c, h), P(c, h), P(h, c),
    )
    out_specs = (
        P(None, c, None), P(None, c, None), P(c), P(c, h), P(c, h), P(c, h), P(c, h), P(c, None),
        P(h, None, c), P(h, c), P(c), P(h, c), P(c), P(c, h), P(c, h), P(h, c),
    )
    return jax.shard_map(
        per_device, mesh=fine, in_specs=in_specs, out_specs=out_specs, check_vma=False
    )
```

```python
import functools

import numpy as np

import jax
import jax.numpy as jnp
from jax import lax
from jax.experimental import pallas as pl
from jax.experimental.pallas import tpu as pltpu
from jax.sharding import Mesh
from jax.sharding import PartitionSpec as P

GROUP = 64
EPS = 1e-06
LEVELS = (32, 16, 8, 4, 2, 1)
f32 = jnp.float32
bf16 = jnp.bfloat16
NZ = 4


def dot(a, b, dims):
    return lax.dot_general(a, b, (dims, ((), ())), preferred_element_type=f32)


def nn(a, b):
    return dot(a, b, ((1,), (0,)))


def nt(a, b):
    return dot(a, b, ((1,), (1,)))


def tn(a, b):
    return dot(a, b, ((0,), (0,)))


def swap(x, axis):
    return lax.ppermute(x, axis, [(0, 1), (1, 0)])


def after(value, *earlier):
    anywhere = pl.BlockSpec(memory_space=pl.ANY)
    return pl.pallas_call(
        lambda *refs: None,
        in_specs=[anywhere] * (1 + len(earlier)),
        out_specs=anywhere,
        out_shape=jax.ShapeDtypeStruct(value.shape, value.dtype),
        input_output_aliases={0: 0},
        cost_estimate=pl.CostEstimate(flops=0, bytes_accessed=0, transcendentals=0),
        name="after",
    )(value, *earlier)


def as_one(runs, work):
    shapes = jax.eval_shape(work)
    return lax.cond(
        runs, work, lambda: jax.tree.map(lambda s: jnp.zeros(s.shape, s.dtype), shapes)
    )


def add_low(a, b):
    return (a.astype(f32) + b.astype(f32)).astype(bf16)


def both_in_order(piece, axis, dim):
    other = swap(piece, axis)
    first = lax.axis_index(axis) == 0
    return jnp.where(
        first, jnp.stack([piece, other], dim), jnp.stack([other, piece], dim)
    )


def silu(v):
    return v * jax.nn.sigmoid(v)


def silu_grad(v):
    sig = jax.nn.sigmoid(v)
    return sig * (1.0 + v * (1.0 - sig))


def inv_rms(v):
    return lax.rsqrt(jnp.mean(v * v, axis=-1, keepdims=True) + EPS)


def norm_back(h, r, gain, grad):
    scaled = gain * grad
    inner = jnp.mean(h * scaled, axis=-1, keepdims=True)
    return r * scaled - h * (r * r * r) * inner


def level_map(rows):
    t = np.arange(rows)[:, None]
    u = np.arange(rows)[None, :]
    out = np.zeros((rows, rows), np.int32)
    for at, half in enumerate(LEVELS):
        hit = (t // (2 * half) == u // (2 * half)) & ((t // half) % 2 == 1) & ((u // half) % 2 == 0)
        out[hit] = at + 1
    out[t == u] = len(LEVELS) + 1
    return out


def lower_map(rows):
    t = np.arange(rows)[:, None]
    u = np.arange(rows)[None, :]
    return ((t // GROUP == u // GROUP) & (t >= u)).astype(np.float32)


def ones_times(ones, value):
    hi = value.astype(bf16)
    rest = value - hi.astype(f32)
    mid = rest.astype(bf16)
    low = (rest - mid.astype(f32)).astype(bf16)
    return nn(ones, hi) + (nn(ones, mid) + nn(ones, low))


def level_decay(cum, half):
    rows, width = cum.shape
    span = max(2 * half, 8)
    parts = cum.reshape(rows // span, span, width)
    if half >= 4:
        mid = parts[:, half - 1 : half, :]
    else:
        at = lax.broadcasted_iota(jnp.int32, parts.shape, 1)
        mid = parts[:, half - 1 : half, :]
        for start in range(2 * half, span, 2 * half):
            mid = jnp.where(at >= start, parts[:, start + half - 1 : start + half, :], mid)
    return jnp.exp(-jnp.abs(parts - mid)).reshape(rows, width)


def block_of(array, at):
    return array[at * GROUP : (at + 1) * GROUP, :]


def scan_forward(qkv_ref, decay_ref, lower_ref, level_ref, open_ref, out_ref, query_ref, state_ref, keep_ref):
    step = pl.program_id(0)
    rows, width = decay_ref.shape
    count = rows // GROUP
    scale = width**-0.5
    queries = qkv_ref[:, :width].astype(f32) * scale
    keys = qkv_ref[:, width : 2 * width].astype(f32)
    values = qkv_ref[:, 2 * width :]
    levels = level_ref[...]
    cum = ones_times(lower_ref[...], decay_ref[...])
    scores = jnp.where(
        levels == len(LEVELS) + 1, nt(queries.astype(bf16), keys.astype(bf16)), 0.0
    )
    for at, half in enumerate(LEVELS):
        decay = level_decay(cum, half)
        part = nt((queries * decay).astype(bf16), (keys * decay).astype(bf16))
        scores = jnp.where(levels == at + 1, part, scores)
    local = nn(scores.astype(bf16), values)
    faded = queries * jnp.exp(cum)
    state = jnp.zeros((values.shape[1], width), f32)
    keep = jnp.ones((1, width), f32)
    for c in range(count):
        is_open = open_ref[step, c]
        state = state * is_open
        keep = keep * is_open
        faded_c = block_of(faded, c)
        cum_c = block_of(cum, c)
        last = cum_c[GROUP - 1 :, :]
        here = block_of(local, c)
        if c:
            here = here + nt(faded_c.astype(bf16), state.astype(bf16))
        out_ref[c * GROUP : (c + 1) * GROUP, :] = here
        query_ref[c * GROUP : (c + 1) * GROUP, :] = (faded_c * keep).astype(bf16)
        carried = (block_of(keys, c) * jnp.exp(last - cum_c)).astype(bf16)
        update = tn(block_of(values, c), carried)
        shrink = jnp.exp(last)
        state = state * shrink + update
        keep = keep * shrink
    state_ref[0] = state.astype(bf16)
    keep_ref[0] = jnp.broadcast_to(keep, keep_ref.shape[1:])


def scan_backward(qkv_ref, decay_ref, logit_ref, grad_ref, enter_ref, leave_ref, lower_ref, upper_ref, level_ref, open_ref, *rest):
    out_ref, logit_out_ref, local_ref, past_ref = rest[-4:]
    step = pl.program_id(0)
    rows, width = decay_ref.shape
    count = rows // GROUP
    scale = width**-0.5
    queries = qkv_ref[:, :width].astype(f32) * scale
    keys = qkv_ref[:, width : 2 * width].astype(f32)
    values = qkv_ref[:, 2 * width :]
    grads = grad_ref[...]
    levels = level_ref[...]
    cum = ones_times(lower_ref[...], decay_ref[...])
    pair_grad = nt(grads, values)
    on_diagonal = levels == len(LEVELS) + 1
    own = jnp.sum(jnp.where(on_diagonal, pair_grad, 0.0), axis=1, keepdims=True)
    scores = jnp.where(on_diagonal, nt(queries.astype(bf16), keys.astype(bf16)), 0.0)
    query_grad = jnp.zeros((rows, width), f32)
    key_grad = jnp.zeros((rows, width), f32)
    for at, half in enumerate(LEVELS):
        decay = level_decay(cum, half)
        query_l = (queries * decay).astype(bf16)
        key_l = (keys * decay).astype(bf16)
        hit = levels == at + 1
        scores = jnp.where(hit, nt(query_l, key_l), scores)
        grad_l = jnp.where(hit, pair_grad, 0.0).astype(bf16)
        query_grad = query_grad + nn(grad_l, key_l) * decay
        key_grad = key_grad + tn(grad_l, query_l) * decay
    value_grad = tn(scores.astype(bf16), grads)
    rising = jnp.exp(cum)
    faded = queries * rising
    state = enter_ref[0].astype(f32)
    for c in range(count):
        state = state * open_ref[step, c]
        past_ref[c] = state
        cum_c = block_of(cum, c)
        last = cum_c[GROUP - 1 :, :]
        if c < count - 1:
            carried = (block_of(keys, c) * jnp.exp(last - cum_c)).astype(bf16)
            state = state * jnp.exp(last) + tn(block_of(values, c), carried)
    after = leave_ref[0].astype(f32)
    for c in range(count - 1, -1, -1):
        span = slice(c * GROUP, (c + 1) * GROUP)
        past = past_ref[c]
        cum_c = block_of(cum, c)
        last = cum_c[GROUP - 1 :, :]
        shrink = jnp.exp(last)
        fading = jnp.exp(last - cum_c)
        keys_c = block_of(keys, c)
        queries_c = block_of(queries, c)
        grads_c = block_of(grads, c)
        after_low = after.astype(bf16)
        query_c = block_of(query_grad, c) + nn(grads_c, past.astype(bf16)) * block_of(rising, c)
        key_far = nn(block_of(values, c), after_low) * fading
        key_c = block_of(key_grad, c) + key_far
        value_c = block_of(value_grad, c) + nt((keys_c * fading).astype(bf16), after_low)
        own_c = block_of(own, c)
        out_ref[span, :width] = ((query_c + own_c * keys_c) * scale).astype(bf16)
        out_ref[span, width : 2 * width] = (key_c + own_c * queries_c).astype(bf16)
        out_ref[span, 2 * width :] = value_c.astype(bf16)
        local_ref[span, :] = queries_c * query_c - keys_c * key_c
        at_last = jnp.sum(keys_c * key_far, axis=0, keepdims=True) + shrink * jnp.sum(
            past * after, axis=0, keepdims=True
        )
        logit_out_ref[span, :] = jnp.broadcast_to(at_last, (GROUP, width))
        if c:
            after = (after * shrink + tn(grads_c, block_of(faded, c).astype(bf16))) * open_ref[step, c]
    decay_grad = ones_times(upper_ref[...], local_ref[...]) + logit_out_ref[...]
    logit_out_ref[...] = decay_grad * jax.nn.sigmoid(-logit_ref[...]) * (1.0 / 16.0)


def call_forward(qkv, decays, is_open, micro_count):
    rows = qkv.shape[0] // micro_count
    width = decays.shape[1]
    wide = qkv.shape[1] - 2 * width
    lower = jnp.asarray(lower_map(rows), bf16)
    level = jnp.asarray(level_map(rows))
    whole = lambda m: (0, 0)
    mine = lambda m: (m, 0)
    mine3 = lambda m: (m, 0, 0)
    return pl.pallas_call(
        scan_forward,
        grid=(micro_count,),
        in_specs=[
            pl.BlockSpec((rows, qkv.shape[1]), mine),
            pl.BlockSpec((rows, width), mine),
            pl.BlockSpec((rows, rows), whole),
            pl.BlockSpec((rows, rows), whole),
            pl.BlockSpec(memory_space=pltpu.SMEM),
        ],
        out_specs=[
            pl.BlockSpec((rows, wide), mine),
            pl.BlockSpec((rows, width), mine),
            pl.BlockSpec((1, wide, width), mine3),
            pl.BlockSpec((1, 8, width), mine3),
        ],
        out_shape=[
            jax.ShapeDtypeStruct((micro_count * rows, wide), f32),
            jax.ShapeDtypeStruct((micro_count * rows, width), bf16),
            jax.ShapeDtypeStruct((micro_count, wide, width), bf16),
            jax.ShapeDtypeStruct((micro_count, 8, width), f32),
        ],
        compiler_params=pltpu.CompilerParams(vmem_limit_bytes=40 * 2**20),
        cost_estimate=pl.CostEstimate(flops=2_000_000_000, bytes_accessed=8_000_000, transcendentals=1_500_000),
        name="scan_forward",
    )(qkv, decays, lower, level, is_open)


def call_backward(qkv, decays, logits, grads, enter, leave, is_open, micro_count, *earlier):
    rows = qkv.shape[0] // micro_count
    width = decays.shape[1]
    wide = qkv.shape[1] - 2 * width
    lower = jnp.asarray(lower_map(rows), bf16)
    upper = jnp.asarray(lower_map(rows).T, bf16)
    level = jnp.asarray(level_map(rows))
    whole = lambda m: (0, 0)
    mine = lambda m: (m, 0)
    mine3 = lambda m: (m, 0, 0)
    return pl.pallas_call(
        scan_backward,
        grid=(micro_count,),
        in_specs=[
            pl.BlockSpec((rows, qkv.shape[1]), mine),
            pl.BlockSpec((rows, width), mine),
            pl.BlockSpec((rows, width), mine),
            pl.BlockSpec((rows, wide), mine),
            pl.BlockSpec((1, wide, width), mine3),
            pl.BlockSpec((1, wide, width), mine3),
            pl.BlockSpec((rows, rows), whole),
            pl.BlockSpec((rows, rows), whole),
            pl.BlockSpec((rows, rows), whole),
            pl.BlockSpec(memory_space=pltpu.SMEM),
        ]
        + [pl.BlockSpec(memory_space=pl.ANY)] * len(earlier),
        out_specs=[
            pl.BlockSpec((rows, qkv.shape[1]), mine),
            pl.BlockSpec((rows, width), mine),
        ],
        out_shape=[
            jax.ShapeDtypeStruct((micro_count * rows, qkv.shape[1]), bf16),
            jax.ShapeDtypeStruct((micro_count * rows, width), f32),
        ],
        scratch_shapes=[
            pltpu.VMEM((rows, width), f32),
            pltpu.VMEM((rows // GROUP, wide, width), f32),
        ],
        compiler_params=pltpu.CompilerParams(vmem_limit_bytes=40 * 2**20),
        cost_estimate=pl.CostEstimate(flops=5_000_000_000, bytes_accessed=12_000_000, transcendentals=1_500_000),
        name="scan_backward",
    )(qkv, decays, logits, grads, enter, leave, lower, upper, level, is_open, *earlier)


def scan_states(got_ref, out_ref, *, micro, strip, reverse):
    count = got_ref.shape[0]
    width = got_ref.shape[2]
    running = [jnp.zeros((strip, width), f32) for _ in range(micro)]
    order = range(count - 1, -1, -1) if reverse else range(count)
    for at in order:
        tail = got_ref[at, micro * strip :, :].astype(f32)
        for m in range(micro):
            span = slice(m * strip, (m + 1) * strip)
            out_ref[at, span, :] = running[m].astype(bf16)
            keep = tail[m : m + 1, :] + tail[micro + m : micro + m + 1, :]
            running[m] = running[m] * keep + got_ref[at, span, :].astype(f32)


def spread_states(state, keep, reverse):
    ctx = ("z", "y")
    count = lax.axis_size(ctx)
    micro, wide, width = state.shape
    strip = wide // count
    parts = state.reshape(micro, count, strip, width).transpose(1, 0, 2, 3)
    parts = parts.reshape(count, micro * strip, width)
    keep_hi = keep.astype(bf16)
    keep_lo = (keep - keep_hi.astype(f32)).astype(bf16)
    extra = jnp.concatenate([keep_hi, keep_lo, jnp.zeros((16 - 2 * micro, width), bf16)])
    sent = jnp.concatenate(
        [parts, jnp.broadcast_to(extra[None], (count, 16, width))], axis=1
    )
    got = lax.all_to_all(sent, ctx, 0, 0)
    return pl.pallas_call(
        functools.partial(scan_states, micro=micro, strip=strip, reverse=reverse),
        out_shape=jax.ShapeDtypeStruct((count, micro * strip, width), bf16),
        compiler_params=pltpu.CompilerParams(vmem_limit_bytes=16 * 2**20),
        cost_estimate=pl.CostEstimate(flops=2_000_000, bytes_accessed=1_100_000, transcendentals=0),
        name="scan_states",
    )(got)


def collect_states(entering, micro):
    count, _, width = entering.shape
    strip = entering.shape[1] // micro
    back = lax.all_to_all(entering, ("z", "y"), 0, 0)
    return back.reshape(count, micro, strip, width).transpose(1, 0, 2, 3).reshape(micro, -1, width)


def feed_kernel(mid_ref, low_ref, weight_ref, *rest, units):
    pair_ref, hidden_ref, grad_ref = rest[-3:]
    both = nn(mid_ref[...], weight_ref[:, : 2 * units])
    gate, up = both[:, :units], both[:, units:]
    back = nn(low_ref[...], weight_ref[:, 2 * units :])
    sig = jax.nn.sigmoid(gate)
    act = gate * sig
    hidden_ref[...] = (act * up).astype(bf16)
    pair_ref[:, :units] = (back * up * (sig * (1.0 + gate * (1.0 - sig)))).astype(bf16)
    pair_ref[:, units:] = (back * act).astype(bf16)
    grad_ref[...] = nt(pair_ref[...], weight_ref[:, : 2 * units]).astype(bf16)


def call_feed(plane_mid, plane_low, weight, units, *earlier):
    rows, depth = plane_mid.shape
    tile = 256
    return pl.pallas_call(
        functools.partial(feed_kernel, units=units),
        grid=(rows // tile,),
        in_specs=[
            pl.BlockSpec((tile, depth), lambda i: (i, 0)),
            pl.BlockSpec((tile, depth), lambda i: (i, 0)),
            pl.BlockSpec(weight.shape, lambda i: (0, 0), pipeline_mode=pl.Buffered(1)),
        ]
        + [pl.BlockSpec(memory_space=pl.ANY)] * len(earlier),
        out_specs=[
            pl.BlockSpec((tile, 2 * units), lambda i: (i, 0)),
            pl.BlockSpec((tile, units), lambda i: (i, 0)),
            pl.BlockSpec((tile, depth), lambda i: (i, 0)),
        ],
        out_shape=[
            jax.ShapeDtypeStruct((rows, 2 * units), bf16),
            jax.ShapeDtypeStruct((rows, units), bf16),
            jax.ShapeDtypeStruct((rows, depth), bf16),
        ],
        compiler_params=pltpu.CompilerParams(vmem_limit_bytes=48 * 2**20),
        cost_estimate=pl.CostEstimate(
            flops=10 * rows * depth * units, bytes_accessed=28_000_000, transcendentals=rows * units
        ),
        name="feed_forward",
    )(plane_mid, plane_low, weight, *earlier)


def split_units(gate_ref, up_ref, down_ref, out_ref):
    parts, rows, width = out_ref.shape
    units = width // 3
    for k in range(parts):
        span = slice(k * units, (k + 1) * units)
        out_ref[k, :, :units] = gate_ref[:, span]
        out_ref[k, :, units : 2 * units] = up_ref[:, span]
        out_ref[k, :, 2 * units :] = down_ref[span, :].astype(f32).T.astype(bf16)


def call_split(w_gate, w_up, w_down, parts):
    rows, ff = w_gate.shape
    return pl.pallas_call(
        split_units,
        out_shape=jax.ShapeDtypeStruct((parts, rows, 3 * ff // parts), bf16),
        compiler_params=pltpu.CompilerParams(vmem_limit_bytes=32 * 2**20),
        cost_estimate=pl.CostEstimate(flops=0, bytes_accessed=12 * rows * ff, transcendentals=0),
        name="split_units",
    )(w_gate, w_up, w_down)


def join_units(in_ref, gate_ref, up_ref, down_ref):
    parts, rows, width = in_ref.shape
    units = width // 3
    for k in range(parts):
        span = slice(k * units, (k + 1) * units)
        gate_ref[:, span] = in_ref[k, :, :units].astype(f32)
        up_ref[:, span] = in_ref[k, :, units : 2 * units].astype(f32)
        down_ref[span, :] = in_ref[k, :, 2 * units :].astype(f32).T


def call_join(pieces):
    parts, rows, width = pieces.shape
    ff = width // 3 * parts
    return pl.pallas_call(
        join_units,
        out_shape=[
            jax.ShapeDtypeStruct((rows, ff), f32),
            jax.ShapeDtypeStruct((rows, ff), f32),
            jax.ShapeDtypeStruct((ff, rows), f32),
        ],
        compiler_params=pltpu.CompilerParams(vmem_limit_bytes=32 * 2**20),
        cost_estimate=pl.CostEstimate(flops=0, bytes_accessed=18 * rows * ff, transcendentals=0),
        name="join_units",
    )(pieces)


def pick_rows(at_ref, in_ref, out_ref):
    out_ref[:, : in_ref.shape[2]] = in_ref[0]


def call_pick(pieces, at):
    _, rows, width = pieces.shape
    full = width + -width % 128
    return pl.pallas_call(
        pick_rows,
        grid_spec=pltpu.PrefetchScalarGridSpec(
            num_scalar_prefetch=1,
            grid=(1,),
            in_specs=[pl.BlockSpec((1, rows, width), lambda i, at: (at[0], 0, 0))],
            out_specs=pl.BlockSpec((rows, full), lambda i, at: (0, 0)),
        ),
        out_shape=jax.ShapeDtypeStruct((rows, full), pieces.dtype),
        compiler_params=pltpu.CompilerParams(vmem_limit_bytes=16 * 2**20),
        cost_estimate=pl.CostEstimate(flops=0, bytes_accessed=4 * rows * width, transcendentals=0),
        name="pick_rows",
    )(at.reshape(1), pieces)


def join_two(at_ref, own_ref, got_ref, gate_ref, up_ref, down_ref):
    units = own_ref.shape[2] // 3
    first = at_ref[0] == 0
    for k in range(2):
        mine = jnp.logical_xor(first, k == 1)
        span = slice(k * units, (k + 1) * units)

        @pl.when(mine)
        def _():
            value = own_ref[0].astype(f32)
            gate_ref[:, span] = value[:, :units]
            up_ref[:, span] = value[:, units : 2 * units]
            down_ref[span, :] = value[:, 2 * units : 3 * units].T

        @pl.when(jnp.logical_not(mine))
        def _():
            value = got_ref[...].astype(f32)
            gate_ref[:, span] = value[:, :units]
            up_ref[:, span] = value[:, units : 2 * units]
            down_ref[span, :] = value[:, 2 * units : 3 * units].T


def call_join_two(pieces, got, at):
    _, rows, width = pieces.shape
    ff = width // 3 * 2
    return pl.pallas_call(
        join_two,
        grid_spec=pltpu.PrefetchScalarGridSpec(
            num_scalar_prefetch=1,
            grid=(1,),
            in_specs=[
                pl.BlockSpec((1, rows, width), lambda i, at: (at[0], 0, 0)),
                pl.BlockSpec(got.shape, lambda i, at: (0, 0)),
            ],
            out_specs=[
                pl.BlockSpec((rows, ff), lambda i, at: (0, 0)),
                pl.BlockSpec((rows, ff), lambda i, at: (0, 0)),
                pl.BlockSpec((ff, rows), lambda i, at: (0, 0)),
            ],
        ),
        out_shape=[
            jax.ShapeDtypeStruct((rows, ff), f32),
            jax.ShapeDtypeStruct((rows, ff), f32),
            jax.ShapeDtypeStruct((ff, rows), f32),
        ],
        compiler_params=pltpu.CompilerParams(vmem_limit_bytes=32 * 2**20),
        cost_estimate=pl.CostEstimate(flops=0, bytes_accessed=18 * rows * ff, transcendentals=0),
        name="join_two",
    )(at.reshape(1), pieces, got)


def widen_rows(in_ref, query_ref, key_ref, value_ref):
    width = query_ref.shape[1]
    query_ref[...] = in_ref[:, :width].astype(f32)
    key_ref[...] = in_ref[:, width : 2 * width].astype(f32)
    value_ref[...] = in_ref[:, 2 * width :].astype(f32)


def widen_turned(in_ref, gate_ref, out_ref):
    wide = gate_ref.shape[1]
    gate_ref[...] = in_ref[:, :wide].astype(f32)
    out_ref[...] = in_ref[:, wide:].astype(f32).T


def call_widen(kernel, value, shapes):
    return pl.pallas_call(
        kernel,
        out_shape=[jax.ShapeDtypeStruct(shape, f32) for shape in shapes],
        compiler_params=pltpu.CompilerParams(vmem_limit_bytes=16 * 2**20),
        cost_estimate=pl.CostEstimate(flops=0, bytes_accessed=6 * value.size, transcendentals=0),
        name="widen",
    )(value)


def feed_grad_kernel(*refs):
    out_ref = refs[-1]
    two = refs[2].shape[1]
    mid_a, low_a, pair_a, hidden_a, mid_b, low_b, pair_b, hidden_b = (r[...] for r in refs[:8])
    out_ref[:, :two] = (tn(mid_a, pair_a) + tn(mid_b, pair_b)).astype(bf16)
    out_ref[:, two:] = (tn(low_a, hidden_a) + tn(low_b, hidden_b)).astype(bf16)


def call_feed_grad(near, far, *earlier):
    rows, depth = near[0].shape
    two, units = near[2].shape[1], near[3].shape[1]
    tile = 256
    one = [
        pl.BlockSpec((rows, tile), lambda i: (0, i)),
        pl.BlockSpec((rows, tile), lambda i: (0, i)),
        pl.BlockSpec((rows, two), lambda i: (0, 0), pipeline_mode=pl.Buffered(1)),
        pl.BlockSpec((rows, units), lambda i: (0, 0), pipeline_mode=pl.Buffered(1)),
    ]
    return pl.pallas_call(
        feed_grad_kernel,
        grid=(depth // tile,),
        in_specs=one + one + [pl.BlockSpec(memory_space=pl.ANY)] * len(earlier),
        out_specs=pl.BlockSpec((tile, two + units), lambda i: (i, 0)),
        out_shape=jax.ShapeDtypeStruct((depth, two + units), bf16),
        compiler_params=pltpu.CompilerParams(vmem_limit_bytes=48 * 2**20),
        cost_estimate=pl.CostEstimate(
            flops=4 * rows * depth * (two + units), bytes_accessed=21_000_000, transcendentals=0
        ),
        name="feed_grad",
    )(*near, *far, *earlier)


def gather_plane(piece):
    count = lax.axis_size("y")
    if count == 2:
        a, b = piece[0], piece[1]
        a_y, b_x = swap(a, "y"), swap(b, "x")
        a, b = jnp.stack([a, a_y]), jnp.stack([b, b_x])
        a_x, b_y = swap(a, "x"), swap(b, "y")
        here = jnp.concatenate([a, a_x, b, b_y])
    else:
        rows = [piece]
        for k in range(1, count):
            rows.append(lax.ppermute(piece, "y", [((i + k) % count, i) for i in range(count)]))
        here = jnp.stack(rows, axis=1)
        here = jnp.stack([here, swap(here, "x")], axis=1)
        here = here.reshape((-1,) + piece.shape[1:])
    here = here.reshape(-1, piece.shape[-1])
    return here, swap(here, "c")


def scatter_first(here, micro, quarter):
    count = lax.axis_size("y")
    depth = here.shape[-1]
    if count == 2:
        here = here.reshape(2, 2, 2 * quarter, depth)
        a, b = here[0], here[1]
        a_got, b_got = swap(a[1], "x"), swap(b[1], "y")
        return add_low(a[0], a_got), add_low(b[0], b_got)
    here = here.reshape(micro, 2, count, quarter, depth)
    here = add_low(here[:, 0], swap(here[:, 1], "x"))
    return here[:, :1], here[:, 1:]


def scatter_second(a, b, quarter):
    count = lax.axis_size("y")
    if count == 2:
        a, b = (v.reshape(2, quarter, -1) for v in (a, b))
        a_got, b_got = swap(a[1], "y"), swap(b[1], "x")
        a = a[0].astype(f32) + a_got.astype(f32)
        b = b[0].astype(f32) + b_got.astype(f32)
        return jnp.stack([a, b])
    total = a[:, 0].astype(f32)
    for k in range(1, count):
        got = lax.ppermute(b[:, k - 1], "y", [(i, (i + k) % count) for i in range(count)])
        total = total + got.astype(f32)
    return total


def scatter_head(part):
    micro, slots, width = part.shape
    c, x = lax.axis_index("c"), lax.axis_index("x")
    view = part.reshape(micro, 2, slots // 2, width)
    mine = lax.dynamic_index_in_dim(view, c, 1, keepdims=False)
    other = lax.dynamic_index_in_dim(view, 1 - c, 1, keepdims=False)
    mine = add_low(mine, swap(other, "c"))
    view = mine.reshape(micro, 2, slots // 4, width)
    mine = lax.dynamic_index_in_dim(view, x, 1, keepdims=False)
    other = lax.dynamic_index_in_dim(view, 1 - x, 1, keepdims=False)
    return mine.astype(f32) + swap(other, "x").astype(f32)


def gather_head(piece):
    micro, quarter, width = piece.shape
    both = both_in_order(piece, "x", 1)
    both = both_in_order(both, "c", 1)
    return both.reshape(micro, 4 * quarter, width)


def own_quarter(array):
    micro, slots, width = array.shape
    c, x = lax.axis_index("c"), lax.axis_index("x")
    view = array.reshape(micro, 4, slots // 4, width)
    return lax.dynamic_index_in_dim(view, 2 * c + x, 1, keepdims=False)


def others_y(piece):
    count = lax.axis_size("y")
    out = [piece]
    for k in range(1, count):
        out.append(lax.ppermute(piece, "y", [((i + k) % count, i) for i in range(count)]))
    return out


def to_relative(array):
    count, y = lax.axis_size("y"), lax.axis_index("y")
    t, depth = array.shape
    rl = depth // (NZ * count)
    if count == 2:
        even = jnp.concatenate([array[:, 2 * z * rl : (2 * z + 1) * rl] for z in range(NZ)], axis=1)
        odd = jnp.concatenate([array[:, (2 * z + 1) * rl : (2 * z + 2) * rl] for z in range(NZ)], axis=1)
        first = y == 0
        return jnp.concatenate([jnp.where(first, even, odd), jnp.where(first, odd, even)], axis=1)
    view = jnp.roll(array.reshape(t, NZ, count, rl), -y, axis=2)
    return view.transpose(0, 2, 1, 3).reshape(t, depth)


def to_absolute(array):
    count, y = lax.axis_size("y"), lax.axis_index("y")
    t, depth = array.shape
    rl = depth // (NZ * count)
    if count == 2:
        first = y == 0
        out = []
        for z in range(NZ):
            own = array[:, z * rl : (z + 1) * rl]
            other = array[:, (NZ + z) * rl : (NZ + z + 1) * rl]
            out += [jnp.where(first, own, other), jnp.where(first, other, own)]
        return jnp.concatenate(out, axis=1)
    view = array.reshape(t, count, NZ, rl).transpose(0, 2, 1, 3)
    return jnp.roll(view, y, axis=2).reshape(t, depth)


def vector_by_ctx(value):
    count, y = lax.axis_size("y"), lax.axis_index("y")
    view = value.reshape(value.shape[0], count, NZ, -1)
    if count == 2:
        view = jnp.where(y == 0, view, view[:, ::-1])
    else:
        view = jnp.roll(view, y, axis=1)
    return view.transpose(2, 1, 0, 3).reshape(NZ * count, value.shape[0], -1)


def vector_from_ctx(value):
    count, y = lax.axis_size("y"), lax.axis_index("y")
    view = value.reshape((NZ, count) + value.shape[1:]).transpose(2, 1, 0, 3)
    if count == 2:
        view = jnp.where(y == 0, view, view[:, ::-1])
    else:
        view = jnp.roll(view, -y, axis=1)
    return view.reshape(value.shape[1], -1)


def sum_y(parts, *between):
    count = lax.axis_size("y")
    total = (after(parts[0], *between) if between else parts[0]).astype(f32)
    for k in range(1, count):
        got = lax.ppermute(parts[k], "y", [(i, (i + k) % count) for i in range(count)])
        total = total + got.astype(f32)
    return total.astype(bf16)


def reduce_z(part):
    return lax.psum_scatter(part, "z", scatter_dimension=0, tiled=True)


def per_device(
    tokens, cotangent, lengths, norm_in, w_query, w_key, w_value, w_outgate, w_rank,
    w_decay, decay_bias, head_gain, w_out, norm_mid, w_gate, w_up, w_down,
):
    ctx = ("z", "y")
    ny = lax.axis_size("y")
    nctx = NZ * ny
    y = lax.axis_index("y")
    place = lax.axis_index(ctx)
    micro, slots, depth = tokens.shape
    groups = slots // GROUP
    rl = w_query.shape[0]
    width = w_query.shape[1]
    wide = w_value.shape[1]
    rank = w_rank.shape[1]
    ff = w_gate.shape[1]
    fl = ff // ny
    total = micro * slots

    w_qkv = jnp.concatenate([w_query, w_key, w_value], axis=1)
    qkv_rows = lax.all_gather(w_qkv, "z", axis=0, tiled=True)
    w_go = jnp.concatenate([w_outgate, w_out.T], axis=1)
    go_rows = lax.all_gather(w_go, "z", axis=0, tiled=True)

    small = jnp.concatenate(
        [norm_in, norm_mid, w_rank.T.reshape(-1), w_decay[0].reshape(-1), decay_bias[0], head_gain]
    )
    n_small = small.shape[0]
    pad = -n_small % 1024
    small = jnp.pad(small, (0, pad)).reshape(1, -1, 128)
    small = jnp.broadcast_to(small, (nctx,) + small.shape[1:])
    small = lax.all_to_all(small, ctx, 0, 0).reshape(nctx, -1)
    at = 0

    def take(size):
        nonlocal at
        at += size
        return small[:, at - size : at]

    by_row = vector_from_ctx(take((2 + rank) * rl).reshape(nctx, 2 + rank, rl))
    gain_in = by_row[:1].astype(f32)
    gain_mid = by_row[1:2].astype(f32)
    rank_t = by_row[2:]
    dl = width // nctx
    decay_w = take(rank * dl).reshape(nctx, rank, dl).transpose(1, 0, 2).reshape(rank, width)
    bias = take(dl).reshape(1, width).astype(f32)
    gain_head = take(wide // nctx).reshape(1, wide).astype(f32)

    ff_local = call_split(w_gate, w_up, w_down, ny)
    own = lax.dynamic_index_in_dim(ff_local, y, 0, keepdims=False)
    if ny == 2:
        got = swap(lax.dynamic_index_in_dim(ff_local, 1 - y, 0, keepdims=False), "y")
        ff_unit = jnp.where(y == 0, jnp.stack([own, got]), jnp.stack([got, own]))
    else:
        pieces = [own]
        for k in range(1, ny):
            sent = lax.dynamic_index_in_dim(ff_local, lax.rem(y + ny - k, ny), 0, keepdims=False)
            pieces.append(lax.ppermute(sent, "y", [((i + k) % ny, i) for i in range(ny)]))
        ff_unit = jnp.roll(jnp.stack(pieces), y, axis=0)
    ff_unit = ff_unit.reshape(ny * rl, 3 * fl)

    group_ids = place * groups + jnp.arange(groups, dtype=jnp.int32)
    end = jnp.zeros((micro, 1), jnp.int32)
    reset = group_ids[None, :] == end
    for i in range(lengths.shape[1]):
        end = end + lengths[:, i : i + 1]
        reset = reset | (group_ids[None, :] == end)
    is_open = 1.0 - reset.astype(f32)

    def mask_of(at):
        slot_ids = at * slots + jnp.arange(slots, dtype=jnp.int32)
        return (slot_ids[None, :] < end * GROUP).astype(bf16)[:, :, None]

    c_at, x_at = lax.axis_index("c"), lax.axis_index("x")
    quarter = slots // 4
    view = cotangent.reshape(micro, 2, slots // 2, depth)
    half_parts = others_y(lax.dynamic_index_in_dim(view, c_at, 1, keepdims=False))

    ff_full = lax.all_gather(ff_unit, "z", axis=0, tiled=True)
    qkv_parts = others_y(qkv_rows)
    go_parts = others_y(go_rows)

    inputs = to_relative(tokens.reshape(total, depth)).astype(f32)
    r_in = inv_rms(inputs)
    normed_in = (inputs * r_in * gain_in).astype(bf16)
    step = depth // ny
    low_rank = nt(normed_in, rank_t).astype(bf16)
    logits = nn(low_rank, decay_w) + bias
    decays = jax.nn.log_sigmoid(logits) / 16.0

    def columns(array, k):
        return array[:, k * step : (k + 1) * step]

    qkv = sum(nn(columns(normed_in, k), w) for k, w in enumerate(qkv_parts)).astype(bf16)

    runs = lengths[0, 0] >= 1

    def recurrence():
        local_out, far_query, state, keep = call_forward(qkv, decays, is_open, micro)
        keep = keep[:, 0, :]
        return local_out, far_query, collect_states(spread_states(state, keep, False), micro), keep

    local_out, far_query, enter, keep = as_one(runs, recurrence)

    out_low = cotangent * mask_of(place)
    low_parts = []
    for k, half in enumerate(half_parts):
        mask = mask_of(place - y + lax.rem(y + k, ny)).reshape(micro, 2, slots // 2, 1)
        mask = lax.dynamic_index_in_dim(mask, c_at, 1, keepdims=False)
        half = (half * mask).reshape(micro, 2, quarter, depth)
        low_parts.append(jnp.where(x_at == 0, half, half[:, ::-1]))
    if ny == 2:
        low_near = [
            jnp.stack([p[0] for p in low_parts], 1),
            jnp.stack([p[1] for p in low_parts], 0),
        ]
        low_near = jnp.stack(low_near).reshape(-1, depth)
    else:
        low_near = jnp.stack(low_parts, 2).reshape(-1, depth)
    low_far = swap(low_near, "c")

    outgate = sum(nn(columns(normed_in, k), w[:, :wide]) for k, w in enumerate(go_parts))
    outgate = outgate.astype(bf16).astype(f32)
    mixed = local_out + jnp.concatenate(
        [nt(far_query[m * slots : (m + 1) * slots], enter[m]) for m in range(micro)]
    )
    r_head = inv_rms(mixed)
    gated = (mixed * r_head * gain_head * silu(outgate)).astype(bf16)
    attention = jnp.concatenate([nt(gated, w[:, wide:]) for w in go_parts], axis=1)
    attention = scatter_head(attention.astype(bf16).reshape(micro, slots, depth))
    inputs_own = to_relative(own_quarter(tokens).reshape(-1, depth)).astype(f32)
    residual = inputs_own + attention.reshape(micro * quarter, depth)

    r_mid = inv_rms(residual)
    normed_mid = to_absolute((residual * r_mid * gain_mid).astype(bf16))
    mid_near, mid_far = gather_plane(normed_mid.reshape(micro, quarter, depth))
    out_grad = to_relative(own_quarter(out_low).reshape(-1, depth)).astype(f32)
    pair_far, hidden_far, part_far = call_feed(mid_far, low_far, ff_full, fl, out_grad)
    pair_near, hidden_near, part_near = call_feed(mid_near, low_near, ff_full, fl, part_far)
    mid_part = add_low(part_near, swap(part_far, "c"))
    def feed_back():
        ff_part = call_feed_grad(
            (mid_near, low_near, pair_near, hidden_near),
            (mid_far, low_far, pair_far, hidden_far),
        )
        return ff_part, *scatter_first(mid_part, micro, quarter)

    ff_part, mid_a, mid_b = as_one(runs, feed_back)
    ff_grad = reduce_z(ff_part)

    def feed_part(hidden):
        return nt(hidden, ff_full[:, 2 * fl :]).astype(bf16)

    def blocks_back():
        mid_grad = to_relative(scatter_second(mid_a, mid_b, quarter).reshape(-1, depth))

        resid_grad = out_grad + norm_back(residual, r_mid, gain_mid, mid_grad)
        grad_norm_mid = jnp.sum(mid_grad * residual * r_mid, axis=0)
        resid_low = gather_head(resid_grad.astype(bf16).reshape(micro, quarter, depth))
        resid_low = resid_low.reshape(total, depth)
        gated_grad = sum(nn(columns(resid_low, k), w[:, wide:]) for k, w in enumerate(go_parts))

        unit = mixed * r_head
        gate_act = silu(outgate)
        unit_grad = gated_grad * gate_act
        outgate_low = (gated_grad * unit * gain_head * silu_grad(outgate)).astype(bf16)
        mixed_grad = norm_back(mixed, r_head, gain_head, unit_grad).astype(bf16)
        grad_gain = jnp.sum(unit_grad * unit, axis=0)
        state_grad = jnp.stack(
            [
                tn(mixed_grad[m * slots : (m + 1) * slots], far_query[m * slots : (m + 1) * slots])
                for m in range(micro)
            ]
        ).astype(bf16)
        entering = spread_states(state_grad, keep, True)
        leave = collect_states(entering, micro)
        go_grads = [
            jnp.concatenate(
                [tn(columns(normed_in, k), outgate_low), tn(columns(resid_low, k), gated)], axis=1
            ).astype(bf16)
            for k in range(ny)
        ]
        go_rows_grad = sum_y(go_grads[:1] + [after(g, entering) for g in go_grads[1:]])
        feed_far = swap(feed_part(after(hidden_far, mixed_grad)), "c")
        feed_rows = add_low(feed_part(after(hidden_near, mixed_grad)), feed_far)
        feed = scatter_second(*scatter_first(feed_rows, micro, quarter), quarter)
        qkv_low, logit_grad = call_backward(
            qkv, decays, logits, mixed_grad, enter, leave, is_open, micro
        )
        logit_low = logit_grad.astype(bf16)
        qkv_grads = [tn(columns(normed_in, k), qkv_low).astype(bf16) for k in range(ny)]
        rank_part = nt(logit_low, decay_w).astype(bf16)
        rank_pad = jnp.pad(rank_part, ((0, 0), (0, 128 - rank)))
        qkv_later = after(qkv_low, *qkv_grads)
        in_part = [
            (nt(qkv_later, wq) + nt(outgate_low, wg[:, :wide])).astype(bf16)
            for wq, wg in zip(qkv_parts, go_parts)
        ]
        in_part = jnp.concatenate(in_part + [rank_pad], axis=1).reshape(micro, slots, depth + 128)
        return resid_grad, grad_norm_mid, grad_gain, go_rows_grad, qkv_grads, in_part, logit_low, feed

    resid_grad, grad_norm_mid, grad_gain, go_rows_grad, qkv_grads, in_part, logit_low, feed = as_one(
        runs, blocks_back
    )
    go_grad = reduce_z(go_rows_grad)

    def input_back():
        in_sum = scatter_head(in_part).reshape(-1, depth + 128)
        rank_low = in_sum[:, depth : depth + rank].astype(bf16)
        in_grad = in_sum[:, :depth] + nn(rank_low, rank_t)
        r_own = inv_rms(inputs_own)
        input_own = resid_grad + norm_back(inputs_own, r_own, gain_in, in_grad)
        grad_norm_in = jnp.sum(in_grad * inputs_own * r_own, axis=0)
        normed_own = own_quarter(normed_in.reshape(micro, slots, depth)).reshape(-1, depth)
        grad_rank_t = tn(rank_low, normed_own)
        grad_rows = jnp.concatenate([grad_norm_in[None], grad_norm_mid[None], grad_rank_t])
        input_own = to_absolute(input_own.astype(bf16))
        input_low = gather_head(input_own.reshape(micro, quarter, depth))
        return sum_y(qkv_grads), grad_rows, input_low

    qkv_rows_grad, grad_rows, input_low = input_back()
    qkv_rows_grad = after(qkv_rows_grad, ff_grad)
    qkv_grad = reduce_z(qkv_rows_grad)

    by_ctx = lambda v: v.reshape(nctx, -1)
    across = lambda v, n: v.reshape(v.shape[0], nctx, n).transpose(1, 0, 2).reshape(nctx, -1)

    def finish():
        ff_rows = after(ff_grad, qkv_rows_grad).reshape(ny, rl, 3 * fl)
        if ny == 2:
            joined = call_join_two(ff_rows, swap(call_pick(ff_rows, 1 - y), "y"), y)
        else:
            pieces = jnp.zeros((ny, rl, 3 * fl), bf16)
            pieces = lax.dynamic_update_slice_in_dim(
                pieces, lax.dynamic_index_in_dim(ff_rows, y, 0), y, 0
            )
            for k in range(1, ny):
                sent = lax.dynamic_index_in_dim(ff_rows, lax.rem(y + k, ny), 0)
                got = lax.ppermute(sent, "y", [(i, (i + k) % ny) for i in range(ny)])
                pieces = lax.dynamic_update_slice_in_dim(pieces, got, lax.rem(y - k + ny, ny), 0)
            joined = call_join(pieces)
        feed_own = after(feed, qkv_rows_grad).reshape(-1, depth)
        block_own = to_absolute((residual + to_relative(feed_own)).astype(bf16))
        block_out = gather_head(block_own.reshape(micro, quarter, depth))
        grad_decay = tn(low_rank, logit_low)
        grad_bias = jnp.sum(logit_low.astype(f32), axis=0)
        summed = jnp.concatenate(
            [vector_by_ctx(grad_rows).reshape(nctx, -1), by_ctx(grad_gain)], axis=1
        )
        headed = jnp.concatenate([across(grad_decay, dl), by_ctx(grad_bias)], axis=1)
        n_summed, n_headed = summed.shape[1], headed.shape[1]
        pad_s, pad_h = -n_summed % 1024, -n_headed % 1024
        tail = jnp.concatenate(
            [jnp.pad(summed, ((0, 0), (0, pad_s))), jnp.pad(headed, ((0, 0), (0, pad_h)))], axis=1
        ).reshape(nctx, -1, 128)
        tail = jnp.sum(lax.all_to_all(tail, ctx, 0, 0), axis=0)
        cut = (n_summed + pad_s) // 128
        summed, headed = tail[:cut], tail[cut:].reshape(-1)
        summed = summed + swap(summed, "c")
        summed = (summed + swap(summed, "x")).reshape(-1)
        return (
            block_out,
            input_low.astype(f32),
            *joined,
            summed[: 2 * rl],
            summed[2 * rl : (2 + rank) * rl].reshape(rank, rl).T,
            summed[(2 + rank) * rl : n_summed],
            headed[: rank * dl].reshape(1, rank, dl),
            headed[rank * dl : n_headed].reshape(1, dl),
        )

    block_out, input_grad, g_gate, g_up, g_down, g_norms, g_rank, g_gain, g_decay, g_bias = finish()
    g_norm_in, g_norm_mid = g_norms[:rl], g_norms[rl:]
    g_query, g_key, g_value = call_widen(widen_rows, qkv_grad, [(rl, width), (rl, width), (rl, wide)])
    g_outgate, g_out = call_widen(widen_turned, go_grad, [(rl, wide), (wide, rl)])
    return (
        block_out,
        input_grad,
        g_norm_in,
        g_query,
        g_key,
        g_value,
        g_outgate,
        g_rank,
        g_decay,
        g_bias,
        g_gain,
        g_out,
        g_norm_mid,
        g_gate,
        g_up,
        g_down,
    )


def solution(mesh):
    ctx = mesh.shape["ctx"]
    shape = (NZ, ctx // NZ, 2, mesh.shape["head"] // 2)
    fine = Mesh(mesh.devices.reshape(shape), ("z", "y", "x", "c"))
    c, h = ("z", "y"), ("x", "c")
    in_specs = (
        P(None, c, None), P(None, c, None), P(), P(c), P(c, h), P(c, h), P(c, h), P(c, h), P(c, None),
        P(h, None, c), P(h, c), P(c), P(h, c), P(c), P(c, h), P(c, h), P(h, c),
    )
    out_specs = (
        P(None, c, None), P(None, c, None), P(c), P(c, h), P(c, h), P(c, h), P(c, h), P(c, None),
        P(h, None, c), P(h, c), P(c), P(h, c), P(c), P(c, h), P(c, h), P(h, c),
    )
    return jax.shard_map(
        per_device, mesh=fine, in_specs=in_specs, out_specs=out_specs, check_vma=False
    )
```
